32 devices in a mesh: expert: 8 (over z, x), tensor: 4 (over y, core).
Axes of the slice: x: 2, y: 2, z: 4, core: 2. Of those that a mesh axis runs over, the one named last changes fastest.
Arguments:
- hidden_in: bfloat16 [8192, 768], P('expert'), may hold values from -6 to 6
- norm_attn: float32 [768], replicated, may hold values from 0.5 to 1.5
- w_query: bfloat16 [768, 768], P(None, 'tensor'), may hold values from -0.21875 to 0.21875
- w_key: bfloat16 [768, 768], P(None, 'tensor'), may hold values from -0.21875 to 0.21875
- w_value: bfloat16 [768, 768], P(None, 'tensor'), may hold values from -0.21875 to 0.21875
- w_out: bfloat16 [768, 768], P('tensor'), may hold values from -0.625 to 0.625
- norm_ffn: float32 [768], replicated, may hold values from 0.5 to 1.5
- w_router: bfloat16 [768, 8], replicated, may hold values from -0.15625 to 0.15625
- shared_gate: bfloat16 [768, 2048], P(None, 'tensor'), may hold values from -0.21875 to 0.21875
- shared_up: bfloat16 [768, 2048], P(None, 'tensor'), may hold values from -0.21875 to 0.21875
- shared_down: bfloat16 [2048, 768], P('tensor'), may hold values from -0.125 to 0.125
- expert_gate: bfloat16 [8, 768, 2048], P('expert', None, 'tensor'), may hold values from -0.21875 to 0.21875
- expert_up: bfloat16 [8, 768, 2048], P('expert', None, 'tensor'), may hold values from -0.21875 to 0.21875
- expert_down: bfloat16 [8, 2048, 768], P('expert', 'tensor'), may hold values from -0.125 to 0.125
- segment: int32 [8192], P('expert'), may hold values from 0 to 8, as said below
- routes: int32 [8192, 2], P('expert'), may hold values from 0 to 7, as said below
- slots: int32 [8192, 2], P('expert'), may hold values from 0 to 384, as said below
- teacher: bfloat16 [8192, 768], P('expert', 'tensor'), may hold values from -6 to 6
Outputs:
- loss: float32 [], replicated
- activations: bfloat16 [8192, 768], P('expert', 'tensor')
- grad_input: float32 [8192, 768], P('expert', 'tensor')
- grad_norm_attn: float32 [768], replicated
- grad_query: float32 [768, 768], P(None, 'tensor')
- grad_key: float32 [768, 768], P(None, 'tensor')
- grad_value: float32 [768, 768], P(None, 'tensor')
- grad_out: float32 [768, 768], P('tensor')
- grad_norm_ffn: float32 [768], replicated
- grad_router: float32 [768, 8], replicated
- grad_shared_gate: float32 [768, 2048], P(None, 'tensor')
- grad_shared_up: float32 [768, 2048], P(None, 'tensor')
- grad_shared_down: float32 [2048, 768], P('tensor')
- grad_expert_gate: float32 [8, 768, 2048], P('expert', None, 'tensor')
- grad_expert_up: float32 [8, 768, 2048], P('expert', None, 'tensor')
- grad_expert_down: float32 [8, 2048, 768], P('expert', 'tensor')
The draws below stay inside these ranges and needn't reach their ends.
Inputs may be any that keep to these rules, and one draw needn't show every extreme that they name: `segment`: each run of 1024 consecutive tokens is one sequence: document ids 1, 2, ... never falling along it (some documents may be empty), then padding with id 0 at its end, at most 128 tokens. `routes`: A token's two experts differ. `slots`: within one sequence, the pairs that name an expert carry the rows 0, 1, 2, ... in some order, and those beyond 384 carry 384 (dropped); in every draw some expert is named by more than 384 pairs of every sequence.
All inputs are finite; a program needn't handle non-finite values.
Results may differ from the reference program's by a relative error of at most 0.02.
Values may be sent and summed in bfloat16 or wider, within the bound.
A program may use at most 256 MiB of HBM per device.

```python
import jax
import jax.numpy as jnp
from jax import lax

D = 768
HEADS = 12
HD = 64
FF = 2048
TOK_DEV = 1024
DOCS = 8
EXPERTS = 8
CAP = 384
TOKENS = 8192
N_EXPERT = 8


def route_pairs(key):
    base = jax.random.fold_in(key, 17)
    streams = jax.random.split(base, 5)
    labels = jax.random.permutation(streams[0], EXPERTS)
    first = jax.random.randint(streams[1], (TOKENS,), 0, EXPERTS)
    other = jax.random.randint(streams[2], (TOKENS,), 0, EXPERTS)
    ranked = jnp.minimum(first, other)
    within = jnp.arange(TOKENS) % TOK_DEV
    ranked = jnp.where(within <= CAP, 0, ranked)
    offset = jax.random.randint(streams[3], (TOKENS,), 1, EXPERTS)
    second = (ranked + offset) % EXPERTS
    chosen = jnp.stack([labels[ranked], labels[second]], axis=1).astype(jnp.int32)
    blocks = TOKENS // TOK_DEV
    pairs = 2 * TOK_DEV
    priority = jax.random.randint(streams[4], (blocks, pairs), 0, 65536) * pairs + jnp.arange(pairs)[None, :]
    order = jnp.argsort(priority, axis=1)
    flat = chosen.reshape(blocks, pairs)
    sorted_ids = jnp.take_along_axis(flat, order, axis=1)
    matches = (sorted_ids[:, :, None] == jnp.arange(EXPERTS)[None, None, :]).astype(jnp.int32)
    running = jnp.cumsum(matches, axis=1)
    rank_sorted = jnp.sum(running * matches, axis=2) - 1
    inverse = jnp.argsort(order, axis=1)
    ranks = jnp.take_along_axis(rank_sorted, inverse, axis=1)
    placed = jnp.minimum(ranks, CAP).reshape(TOKENS, 2).astype(jnp.int32)
    return (chosen, placed)


def draw_routes(key, part):
    return route_pairs(key)[0]


def draw_slots(key, part):
    return route_pairs(key)[1]


def draw_segment(key, part):
    base = jax.random.fold_in(key, 29)
    streams = jax.random.split(base, 2)
    seqs = TOKENS // TOK_DEV
    padding = jax.random.randint(streams[0], (seqs, 1), 0, TOK_DEV // 8 + 1)
    raw = jax.random.randint(streams[1], (seqs, DOCS - 1), 1, TOK_DEV)
    cuts = raw * raw // TOK_DEV * raw // TOK_DEV
    places = jnp.arange(TOK_DEV)
    ids = 1 + jnp.sum((cuts[:, None, :] <= places[None, :, None]).astype(jnp.int32), axis=2)
    live = places[None, :] < TOK_DEV - padding
    return jnp.where(live, ids, 0).reshape(TOKENS).astype(jnp.int32)


def block_scale(key, dims, shards, smallest, largest):
    level = 1.0
    for dim, parts in shards:
        draws = jax.random.uniform(jax.random.fold_in(jax.random.fold_in(key, 6), dim), (parts,), jnp.float32, smallest / len(shards), largest / len(shards))
        level = level * jnp.repeat(jnp.exp(draws), dims[dim] // parts).reshape((-1,) + (1,) * (len(dims) - 1 - dim))
    return level


def centred(key, extent, spread, most, shards=(), kind=jnp.bfloat16):
    values = spread * jax.random.normal(key, extent, jnp.float32)
    if shards:
        values = values * block_scale(key, extent, shards, -0.22, 0.18)
    return jnp.clip(values, -most, most).astype(kind)


def setup_inputs(seed: int = 0) -> dict:
    streams_of = jax.random.split(jax.random.key(seed), 19)
    return {
        "hidden_in": centred(streams_of[0], (TOKENS, D), 1.0, 6.0, ((0, 8),)),
        "norm_attn": jnp.clip(1.0 + 0.1 * jax.random.normal(streams_of[1], (D,), jnp.float32), 0.5, 1.5),
        "w_query": centred(streams_of[2], (D, HEADS * HD), D ** -0.5, 0.21875, ((1, 4),)),
        "w_key": centred(streams_of[3], (D, HEADS * HD), D ** -0.5, 0.21875, ((1, 4),)),
        "w_value": centred(streams_of[4], (D, HEADS * HD), D ** -0.5, 0.21875, ((1, 4),)),
        "w_out": centred(streams_of[5], (HEADS * HD, D), (HEADS * HD // 8) ** -0.5, 0.625, ((0, 4),)),
        "norm_ffn": jnp.clip(1.0 + 0.1 * jax.random.normal(streams_of[6], (D,), jnp.float32), 0.5, 1.5),
        "w_router": centred(streams_of[7], (D, EXPERTS), (2 * D) ** -0.5, 0.15625),
        "shared_gate": centred(streams_of[8], (D, FF), D ** -0.5, 0.21875, ((1, 4),)),
        "shared_up": centred(streams_of[9], (D, FF), D ** -0.5, 0.21875, ((1, 4),)),
        "shared_down": centred(streams_of[10], (FF, D), FF ** -0.5, 0.125, ((0, 4),)),
        "expert_gate": centred(streams_of[11], (EXPERTS, D, FF), D ** -0.5, 0.21875, ((0, 8), (2, 4))),
        "expert_up": centred(streams_of[12], (EXPERTS, D, FF), D ** -0.5, 0.21875, ((0, 8), (2, 4))),
        "expert_down": centred(streams_of[13], (EXPERTS, FF, D), FF ** -0.5, 0.125, ((0, 8), (1, 4))),
        "segment": draw_segment(jax.random.fold_in(streams_of[18], 71), 0),
        "routes": draw_routes(jax.random.fold_in(streams_of[18], 71), 0),
        "slots": draw_slots(jax.random.fold_in(streams_of[18], 71), 0),
        "teacher": centred(streams_of[17], (TOKENS, D), 1.0, 6.0, ((0, 8), (1, 4))),
    }


@jax.custom_vjp
def low(v):
    return lax.optimization_barrier(v.astype(jnp.bfloat16)).astype(jnp.float32)

@jax.custom_vjp
def low_back(v):
    return v

def low_keep(v):
    return (low(v), None)

def low_pass(kept, grad):
    return (grad,)

def back_keep(v):
    return (v, None)

def back_low(kept, grad):
    return (low(grad),)
low.defvjp(low_keep, low_pass)
low_back.defvjp(back_keep, back_low)
eps_norm = 1e-06
highest = lax.Precision.HIGHEST

def matmul(left, right):
    return jnp.dot(left, right, precision=highest, preferred_element_type=jnp.float32)

def rms_scale(value):
    return lax.rsqrt(lax.optimization_barrier(jnp.mean(value * value, axis=-1, keepdims=True)) + eps_norm)

def rope_tables(length, head_dim):
    half = head_dim // 2
    freqs = 10000.0 ** (-2.0 * jnp.arange(half, dtype=jnp.float32) / head_dim)
    angles = jnp.arange(length, dtype=jnp.float32)[:, None] * freqs[None, :]
    return (jnp.cos(angles), jnp.sin(angles))

def rotate(vec, cosine, sine):
    half = vec.shape[-1] // 2
    first = vec[..., :half]
    second = vec[..., half:]
    return jnp.concatenate([first * cosine - second * sine, second * cosine + first * sine], axis=-1)

def attend(normed_seq, seg_seq, w_query, w_key, w_value, w_out):
    length = normed_seq.shape[0]

    def heads_of(weight):
        return matmul(normed_seq, weight).reshape(length, HEADS, HD).transpose(1, 0, 2)
    cosine, sine = rope_tables(length, HD)
    query = low(rotate(low_back(heads_of(w_query)), cosine, sine))
    keys = low(rotate(low_back(heads_of(w_key)), cosine, sine))
    values = low(low_back(heads_of(w_value)))
    places = jnp.arange(length)
    allowed = (seg_seq[:, None] == seg_seq[None, :]) & (places[None, :] <= places[:, None])
    scores = jnp.einsum('hqd,hkd->hqk', query, keys, precision=highest) * HD ** (-0.5)
    scores = low_back(scores)
    scores = jnp.where(allowed[None], scores, -1e+30)
    top = lax.optimization_barrier(jnp.max(scores, axis=-1, keepdims=True))
    expo = jnp.exp(scores - top)
    prob = expo / lax.optimization_barrier(jnp.sum(expo, axis=-1, keepdims=True))
    mixed = jnp.einsum('hqk,hkd->hqd', low(prob), values, precision=highest)
    mixed = low(low_back(mixed)).transpose(1, 0, 2).reshape(length, HEADS * HD)
    return matmul(mixed, w_out)

def expert_rows(normed_two, index, gate_w, up_w, down_w):
    present = index >= 0
    rows = jnp.where(present[:, None], normed_two[jnp.maximum(index, 0)], 0.0)
    rows = low_back(rows)
    pre = low_back(matmul(rows, gate_w))
    lin = low_back(matmul(rows, up_w))
    hidden = low(jax.nn.silu(pre) * lin)
    return low_back(low(matmul(hidden, down_w)))

def layer(inputs, norm_attn, w_query, w_key, w_value, w_out, norm_ffn, w_router, shared_gate, shared_up, shared_down, expert_gate, expert_up, expert_down, segment, routes, slots, teacher):
    normed_one = low(inputs * rms_scale(inputs) * norm_attn)
    attend_ck = jax.checkpoint(attend)

    def one_sequence(carry, pieces):
        normed_seq, seg_seq = pieces
        return (carry, attend_ck(normed_seq, seg_seq, w_query, w_key, w_value, w_out))
    seqs = TOKENS // TOK_DEV
    empty, attention = lax.scan(one_sequence, jnp.zeros((), inputs.dtype), (normed_one.reshape(seqs, TOK_DEV, D), segment.reshape(seqs, TOK_DEV)))
    residual = inputs + attention.reshape(TOKENS, D)
    normed_two = low(residual * rms_scale(residual) * norm_ffn)
    logits = low_back(matmul(normed_two, w_router))
    onehot = (routes[:, :, None] == jnp.arange(EXPERTS, dtype=jnp.int32)[None, None, :]).astype(inputs.dtype)
    chosen = jnp.einsum('te,tke->tk', logits, onehot, precision=highest)
    gates = jax.nn.softmax(chosen, axis=1)
    side_pre = low_back(matmul(normed_two, shared_gate))
    side_lin = low_back(matmul(normed_two, shared_up))
    side_hidden = low(jax.nn.silu(side_pre) * side_lin)
    side_out = low_back(matmul(side_hidden, shared_down))
    token_ids = jnp.arange(TOKENS, dtype=jnp.int32)
    source = (token_ids // TOK_DEV).astype(jnp.int32)
    source_pair = jnp.broadcast_to(source[:, None], (TOKENS, 2))
    token_pair = jnp.broadcast_to(token_ids[:, None], (TOKENS, 2))
    table = jnp.full((EXPERTS, N_EXPERT, CAP), -1, jnp.int32)
    table = table.at[routes, source_pair, slots].set(token_pair, mode='drop')
    expert_ck = jax.checkpoint(expert_rows)
    outputs = lax.map(lambda pieces: expert_ck(normed_two, pieces[0], pieces[1], pieces[2], pieces[3]), (table.reshape(EXPERTS, N_EXPERT * CAP), expert_gate, expert_up, expert_down))
    outputs = outputs.reshape(EXPERTS, N_EXPERT, CAP, D)
    kept = slots < CAP
    fetched = outputs[routes, source_pair, jnp.minimum(slots, CAP - 1)]
    fetched = jnp.where(kept[:, :, None], fetched, 0.0)
    mixture = lax.optimization_barrier(jnp.sum(gates[:, :, None] * fetched, axis=1))
    final = residual + side_out + mixture
    valid = (segment != 0).astype(inputs.dtype)
    count = jnp.sum(valid)
    error = final - teacher
    loss = jnp.sum(valid[:, None] * error * error) / (count * D)
    objective = loss * (TOKENS * D)
    return (objective, (final, loss))

def reference(hidden_in, norm_attn, w_query, w_key, w_value, w_out, norm_ffn, w_router, shared_gate, shared_up, shared_down, expert_gate, expert_up, expert_down, segment, routes, slots, teacher):
    weights = [hidden_in, norm_attn, w_query, w_key, w_value, w_out, norm_ffn, w_router, shared_gate, shared_up, shared_down, expert_gate, expert_up, expert_down]
    weights = [item.astype(jnp.float32) for item in weights]
    target = teacher.astype(jnp.float32)

    def forward(*params):
        return layer(*params, segment, routes, slots, target)
    objective, pullback, extras = jax.vjp(forward, *weights, has_aux=True)
    grads = pullback(jnp.ones_like(objective))
    final, loss = extras
    return (loss, final.astype(jnp.bfloat16), grads[0], grads[1], grads[2], grads[3], grads[4], grads[5], grads[6], grads[7], grads[8], grads[9], grads[10], grads[11], grads[12], grads[13])
```

```python
import jax
import jax.numpy as jnp
from jax import lax
from jax.sharding import PartitionSpec as P

HD = 64


eps_norm = 1e-06


def rope_tables(length, head_dim):
    half = head_dim // 2
    freqs = 10000.0 ** (-2.0 * jnp.arange(half, dtype=jnp.float32) / head_dim)
    angles = jnp.arange(length, dtype=jnp.float32)[:, None] * freqs[None, :]
    return (jnp.cos(angles), jnp.sin(angles))


def rotate(vec, cosine, sine):
    half = vec.shape[-1] // 2
    first = vec[..., :half]
    second = vec[..., half:]
    return jnp.concatenate(
        [first * cosine - second * sine, second * cosine + first * sine], axis=-1
    )


def rotate_back(grad, cosine, sine):
    half = grad.shape[-1] // 2
    first = grad[..., :half]
    second = grad[..., half:]
    return jnp.concatenate(
        [first * cosine + second * sine, second * cosine - first * sine], axis=-1
    )


def silu_slope(value):
    sigma = jax.nn.sigmoid(value)
    return sigma * (1.0 + value * (1.0 - sigma))


def norm_back(grad, value, scale, gain):
    scaled = grad * gain
    inner = jnp.mean(scaled * value, axis=-1, keepdims=True)
    return (
        scale * scaled - value * scale * scale * scale * inner,
        jnp.sum(grad * value * scale, axis=0),
    )


def split_heads(flat, heads):
    return flat.reshape(flat.shape[0], heads, -1).transpose(1, 0, 2)


def merge_heads(stacked):
    return stacked.transpose(1, 0, 2).reshape(stacked.shape[1], -1)


def block_scores(q_block, keys, segment, start, block):
    length = keys.shape[1]
    scale = keys.shape[2] ** (-0.5)
    seg_block = lax.dynamic_slice_in_dim(segment, start, block, 0)
    places = jnp.arange(length)
    rows_at = start + jnp.arange(block)
    allowed = (seg_block[:, None] == segment[None, :]) & (places[None, :] <= rows_at[:, None])
    scores = jnp.einsum("hqd,hkd->hqk", q_block, keys, preferred_element_type=jnp.float32) * scale
    return (jnp.where(allowed[None], scores, -1e30), allowed)


def attend_forward(query, keys, values, segment, block):
    heads, length, width = query.shape

    def one_block(start):
        q_block = lax.dynamic_slice_in_dim(query, start, block, 1)
        scores, allowed = block_scores(q_block, keys, segment, start, block)
        top = jnp.max(scores, axis=-1, keepdims=True)
        expo = jnp.exp(scores - top)
        total = jnp.sum(expo, axis=-1, keepdims=True)
        prob = (expo / total).astype(jnp.bfloat16)
        mixed = jnp.einsum("hqk,hkd->hqd", prob, values, preferred_element_type=jnp.float32)
        return (mixed, (top + jnp.log(total))[..., 0])

    starts = jnp.arange(length // block) * block
    mixed, summary = lax.map(one_block, starts)
    mixed = mixed.transpose(1, 0, 2, 3).reshape(heads, length, width)
    summary = summary.transpose(1, 0, 2).reshape(heads, length)
    return (mixed, summary)


def attend_backward(query, keys, values, segment, summary, grad_mixed, block):
    heads, length, width = query.shape
    scale = width ** (-0.5)

    def one_block(carry, start):
        grad_keys, grad_values = carry
        q_block = lax.dynamic_slice_in_dim(query, start, block, 1)
        scores, allowed = block_scores(q_block, keys, segment, start, block)
        sum_block = lax.dynamic_slice_in_dim(summary, start, block, 1)
        prob = jnp.where(allowed[None], jnp.exp(scores - sum_block[..., None]), 0.0)
        grad_block = lax.dynamic_slice_in_dim(grad_mixed, start, block, 1)
        grad_prob = jnp.einsum(
            "hqd,hkd->hqk", grad_block, values, preferred_element_type=jnp.float32
        )
        inner = jnp.sum(prob * grad_prob, axis=-1, keepdims=True)
        grad_scores = (prob * (grad_prob - inner)).astype(jnp.bfloat16)
        grad_q = (
            jnp.einsum("hqk,hkd->hqd", grad_scores, keys, preferred_element_type=jnp.float32)
            * scale
        )
        grad_keys = (
            grad_keys
            + jnp.einsum("hqk,hqd->hkd", grad_scores, q_block, preferred_element_type=jnp.float32)
            * scale
        )
        grad_values = grad_values + jnp.einsum(
            "hqk,hqd->hkd",
            prob.astype(jnp.bfloat16),
            grad_block,
            preferred_element_type=jnp.float32,
        )
        return ((grad_keys, grad_values), grad_q)

    starts = jnp.arange(length // block) * block
    zeros = jnp.zeros((heads, length, width), jnp.float32)
    (grad_keys, grad_values), grad_q = lax.scan(one_block, (zeros, zeros), starts)
    grad_q = grad_q.transpose(1, 0, 2, 3).reshape(heads, length, width)
    return (grad_q, grad_keys, grad_values)


def body(
    hidden_in,
    norm_attn,
    w_query,
    w_key,
    w_value,
    w_out,
    norm_ffn,
    w_router,
    shared_gate,
    shared_up,
    shared_down,
    expert_gate,
    expert_up,
    expert_down,
    segment,
    routes,
    slots,
    teacher,
):
    length, width = hidden_in.shape
    groups = lax.axis_size("expert")
    members = lax.axis_size("tensor")
    me = lax.axis_index("tensor")
    quarter = width // members
    experts = w_router.shape[1]
    capacity = 3 * length // groups
    share = capacity // members
    rows = groups * share
    tokens = length * groups
    local_heads = w_query.shape[1] // HD
    block = min(512, length)
    f32, bf16 = jnp.float32, jnp.bfloat16

    def mm(a, b):
        return jnp.dot(a, b, preferred_element_type=f32)

    gate_all = lax.all_gather(expert_gate[0], "tensor", axis=0)
    up_all = lax.all_gather(expert_up[0], "tensor", axis=0)
    down_all = lax.all_gather(expert_down[0], "tensor", axis=0)
    out_all = lax.all_gather(w_out, "tensor", axis=0)

    inputs = hidden_in.astype(f32)
    scale_one = lax.rsqrt(jnp.mean(inputs * inputs, axis=-1, keepdims=True) + eps_norm)
    normed_one = (inputs * scale_one * norm_attn).astype(bf16)
    cosine, sine = rope_tables(length, HD)
    query = rotate(split_heads(mm(normed_one, w_query), local_heads), cosine, sine).astype(bf16)
    keys = rotate(split_heads(mm(normed_one, w_key), local_heads), cosine, sine).astype(bf16)
    values = split_heads(mm(normed_one, w_value), local_heads).astype(bf16)
    mixed, summary = attend_forward(query, keys, values, segment, block)
    mixed_low = merge_heads(mixed).astype(bf16)
    mixed_all = lax.all_gather(mixed_low, "tensor", axis=0)
    attention = jnp.einsum("mth,mhd->td", mixed_all, out_all, preferred_element_type=f32)
    residual = inputs + attention
    scale_two = lax.rsqrt(jnp.mean(residual * residual, axis=-1, keepdims=True) + eps_norm)
    normed_two = (residual * scale_two * norm_ffn).astype(bf16)
    logits = mm(normed_two, w_router)
    onehot = (routes[:, :, None] == jnp.arange(experts, dtype=jnp.int32)[None, None, :]).astype(f32)
    chosen = jnp.sum(logits[:, None, :] * onehot, axis=2)
    gates = jax.nn.softmax(chosen, axis=1)
    mine = (slots < capacity) & (slots // share == me)
    place = jnp.where(mine, routes * share + slots - me * share, -1)
    columns = jnp.arange(rows, dtype=jnp.int32)[None, :]
    pick = [(place[:, k][:, None] == columns).astype(bf16) for k in range(2)]
    outgoing = mm((pick[0] + pick[1]).T, normed_two).astype(bf16).reshape(groups, share, width)
    arrived = lax.all_to_all(outgoing, "expert", split_axis=0, concat_axis=0, tiled=True)
    side_pre = mm(normed_two, shared_gate)
    side_lin = mm(normed_two, shared_up)
    side_hidden = (jax.nn.silu(side_pre) * side_lin).astype(bf16)
    side_part = mm(side_hidden, shared_down)
    rows_in = arrived.reshape(rows, width)
    pre = [mm(rows_in, gate_all[m]) for m in range(members)]
    lin = [mm(rows_in, up_all[m]) for m in range(members)]
    hid = [(jax.nn.silu(p) * u).astype(bf16) for p, u in zip(pre, lin)]
    made = sum(mm(hid[m], down_all[m]) for m in range(members))
    returned = lax.all_to_all(
        made.astype(bf16).reshape(groups, share, width),
        "expert",
        split_axis=0,
        concat_axis=0,
        tiled=True,
    ).reshape(rows, width)
    fetched = [mm(p, returned) for p in pick]
    mixture = gates[:, 0:1] * fetched[0] + gates[:, 1:2] * fetched[1]
    own = lax.dynamic_slice_in_dim
    part_sum = lax.psum_scatter(
        (side_part + mixture).astype(bf16), "tensor", scatter_dimension=1, tiled=True
    ).astype(f32)
    final = own(residual, me * quarter, quarter, 1) + part_sum
    valid = (segment != 0).astype(f32)
    error = (final - teacher.astype(f32)) * valid[:, None]
    grad_full = lax.all_gather(error.astype(bf16), "tensor", axis=1, tiled=True)
    grad_wide = grad_full.astype(f32)
    gate_part = jnp.concatenate(
        [jnp.sum(grad_wide * f, axis=1, keepdims=True) for f in fetched], axis=1
    )
    pair_grad = [(gates[:, k : k + 1] * grad_wide).astype(bf16) for k in range(2)]
    grad_out_rows = (mm(pick[0].T, pair_grad[0]) + mm(pick[1].T, pair_grad[1])).astype(bf16)
    grad_arrived = lax.all_to_all(
        grad_out_rows.reshape(groups, share, width), "expert", split_axis=0, concat_axis=0, tiled=True
    ).reshape(rows, width)
    grad_side_hidden = mm(grad_full, shared_down.T)
    grad_shared_down = mm(side_hidden.T, grad_full)
    side_pre_grad = (grad_side_hidden * side_lin * silu_slope(side_pre)).astype(bf16)
    side_lin_grad = (grad_side_hidden * jax.nn.silu(side_pre)).astype(bf16)
    grad_shared_gate = mm(normed_two.T, side_pre_grad)
    grad_shared_up = mm(normed_two.T, side_lin_grad)
    grad_normed = mm(side_pre_grad, shared_gate.T) + mm(side_lin_grad, shared_up.T)

    grad_hid = [mm(grad_arrived, down_all[m].T) for m in range(members)]
    pre_grad = [
        (g * u * silu_slope(p)).astype(bf16) for g, u, p in zip(grad_hid, lin, pre)
    ]
    lin_grad = [(g * jax.nn.silu(p)).astype(bf16) for g, p in zip(grad_hid, pre)]
    grad_rows = sum(
        mm(pre_grad[m], gate_all[m].T) + mm(lin_grad[m], up_all[m].T) for m in range(members)
    )
    grad_back = lax.all_to_all(
        grad_rows.astype(bf16).reshape(groups, share, width),
        "expert",
        split_axis=0,
        concat_axis=0,
        tiled=True,
    ).reshape(rows, width)

    def reduced(parts):
        return lax.psum_scatter(jnp.stack(parts), "tensor", scatter_dimension=0)

    grad_expert_down = reduced([mm(h.T, grad_arrived).astype(bf16) for h in hid])
    grad_expert_gate = reduced([mm(rows_in.T, g).astype(bf16) for g in pre_grad])
    grad_expert_up = reduced([mm(rows_in.T, g).astype(bf16) for g in lin_grad])

    grad_normed = grad_normed + mm(pick[0] + pick[1], grad_back)
    grad_chosen = gates * (gate_part - jnp.sum(gates * gate_part, axis=1, keepdims=True))
    grad_logits = jnp.sum(grad_chosen[:, :, None] * onehot, axis=1).astype(bf16)
    grad_router = mm(normed_two.T, grad_logits)
    grad_normed = grad_normed + mm(grad_logits, w_router.T)
    grad_normed = lax.psum(grad_normed.astype(bf16), "tensor").astype(f32)
    grad_through, grad_norm_ffn = norm_back(grad_normed, residual, scale_two, norm_ffn)
    grad_residual = grad_wide + grad_through
    grad_attention = grad_residual.astype(bf16)
    grad_w_out = mm(mixed_low.T, grad_attention)
    grad_mixed = split_heads(mm(grad_attention, w_out.T), local_heads).astype(bf16)
    grad_q, grad_k, grad_v = attend_backward(
        query, keys, values, segment, summary, grad_mixed, block
    )
    grad_q = merge_heads(rotate_back(grad_q, cosine, sine)).astype(bf16)
    grad_k = merge_heads(rotate_back(grad_k, cosine, sine)).astype(bf16)
    grad_v = merge_heads(grad_v).astype(bf16)
    grad_w_query = mm(normed_one.T, grad_q)
    grad_w_key = mm(normed_one.T, grad_k)
    grad_w_value = mm(normed_one.T, grad_v)
    grad_normed_one = mm(grad_q, w_query.T) + mm(grad_k, w_key.T) + mm(grad_v, w_value.T)
    grad_normed_one = lax.psum(grad_normed_one.astype(bf16), "tensor").astype(f32)
    grad_inner, grad_norm_attn = norm_back(grad_normed_one, inputs, scale_one, norm_attn)
    grad_input = grad_residual + grad_inner
    early = lax.psum(
        tuple(g.astype(bf16) for g in (grad_shared_gate, grad_shared_up, grad_shared_down)), "expert"
    )
    late = lax.psum(
        tuple(g.astype(bf16) for g in (grad_w_query, grad_w_key, grad_w_value, grad_w_out)), "expert"
    )
    square_sum, count, grad_router, grad_norm_ffn, grad_norm_attn = lax.psum(
        (
            jnp.sum(error * error),
            jnp.sum(valid) / members,
            grad_router,
            grad_norm_ffn / members,
            grad_norm_attn / members,
        ),
        ("expert", "tensor"),
    )
    factor = 2.0 * tokens / count

    def scaled(value):
        return value.astype(f32) * factor

    return (
        square_sum / (count * width),
        final.astype(bf16),
        scaled(own(grad_input, me * quarter, quarter, 1)),
        scaled(grad_norm_attn),
        *(scaled(g) for g in late),
        scaled(grad_norm_ffn),
        scaled(grad_router),
        *(scaled(g) for g in early),
        scaled(grad_expert_gate)[None],
        scaled(grad_expert_up)[None],
        scaled(grad_expert_down)[None],
    )


def solution(mesh):
    placed = (
        P("expert", None),
        P(),
        P(None, "tensor"),
        P(None, "tensor"),
        P(None, "tensor"),
        P("tensor", None),
        P(),
        P(),
        P(None, "tensor"),
        P(None, "tensor"),
        P("tensor", None),
        P("expert", None, "tensor"),
        P("expert", None, "tensor"),
        P("expert", "tensor", None),
        P("expert"),
        P("expert", None),
        P("expert", None),
        P("expert", "tensor"),
    )
    return jax.shard_map(
        body,
        mesh=mesh,
        in_specs=placed,
        out_specs=(
            P(),
            P("expert", "tensor"),
            P("expert", "tensor"),
            P(),
            P(None, "tensor"),
            P(None, "tensor"),
            P(None, "tensor"),
            P("tensor", None),
            P(),
            P(),
            P(None, "tensor"),
            P(None, "tensor"),
            P("tensor", None),
            P("expert", None, "tensor"),
            P("expert", None, "tensor"),
            P("expert", "tensor", None),
        ),
        check_vma=False,
    )
```

```python
import functools

import jax
import jax.numpy as jnp
import numpy as np
from jax import lax
from jax.experimental import pallas as pl
from jax.experimental.pallas import tpu as pltpu
from jax.sharding import PartitionSpec as P

HD = 64
F32, BF16 = jnp.float32, jnp.bfloat16
MESH = pl.DeviceIdType.MESH


eps_norm = 1e-06


def rope_rows(length, heads):
    half = HD // 2
    freqs = (10000.0 ** (-2.0 * np.arange(half) / HD)).astype(np.float32)
    angles = np.arange(length, dtype=np.float32)[:, None] * freqs[None, :]
    cosine, sine = np.cos(angles), np.sin(angles)
    return (
        np.tile(np.concatenate([cosine, cosine], axis=1), (1, heads)).astype(np.float32),
        np.tile(np.concatenate([-sine, sine], axis=1), (1, heads)).astype(np.float32),
    )


def peer_of(t, step):
    if step == 1:
        return t + 1 - 2 * lax.rem(t, 2)
    return lax.rem(t + 2, 4)


def greet(peers):
    barrier = pltpu.get_barrier_semaphore()
    for peer in peers:
        pl.semaphore_signal(barrier, inc=1, device_id=peer, device_id_type=MESH)
    pl.semaphore_wait(barrier, len(peers))


def mm(a, b):
    return lax.dot_general(a, b, (((1,), (0,)), ((), ())), preferred_element_type=F32)


def mm_nt(a, b):
    return lax.dot_general(a, b, (((1,), (1,)), ((), ())), preferred_element_type=F32)


def mm_tn(a, b):
    return lax.dot_general(a, b, (((0,), (0,)), ((), ())), preferred_element_type=F32)


def swap_halves(width):
    row = lax.broadcasted_iota(jnp.int32, (width, width), 0)
    col = lax.broadcasted_iota(jnp.int32, (width, width), 1)
    half = HD // 2
    other = jnp.where(lax.rem(col, HD) < half, col + half, col - half)
    return (row == other).astype(F32).astype(BF16)


def head_mask(rows, width, head):
    col = lax.broadcasted_iota(jnp.int32, (rows, width), 1)
    return (col >= head * HD) & (col < (head + 1) * HD)


def only(value, head):
    keep = head_mask(value.shape[0], value.shape[1], head)
    return jnp.where(keep, value, jnp.zeros_like(value))


def attend_kernel(
    block,
    hidden,
    gain_one,
    w_query,
    w_key,
    w_value,
    w_out,
    gain_two,
    cosine,
    sine,
    seg_col,
    seg_row,
    query,
    keys,
    values,
    summary,
    residual,
    normed_two,
    mixed_all,
    out_all,
    send_sem,
    recv_sem,
    wsend_sem,
    wrecv_sem,
    copy_sem,
):
    length = hidden.shape[0]
    lanes = w_query.shape[1]
    heads = lanes // HD
    blocks = length // block
    e, t = lax.axis_index("expert"), lax.axis_index("tensor")
    beside, across = peer_of(t, 1), peer_of(t, 2)
    greet([(e, beside), (e, across)])

    def share(src, dst, device, sem):
        return pltpu.make_async_remote_copy(
            src_ref=src,
            dst_ref=dst,
            send_sem=sem[0],
            recv_sem=sem[1],
            device_id=(e, device),
            device_id_type=MESH,
        )

    def weight(k):
        src = w_out if k < 2 else out_all.at[across]
        dst = out_all.at[t] if k < 2 else out_all.at[across]
        return share(src, dst, across if k == 0 else beside, (wsend_sem.at[k], wrecv_sem.at[k]))

    own = pltpu.make_async_copy(w_out, out_all.at[t], copy_sem)
    own.start()
    weight(0).start()
    weight(1).start()

    def piece(i, k):
        rows = pl.ds(i * block, block)
        slot = t if k < 2 else across
        ref = mixed_all.at[slot, rows]
        return share(
            ref, ref, across if k == 0 else beside, (send_sem.at[i, k], recv_sem.at[i, k])
        )

    for i in range(blocks):
        rows = pl.ds(i * block, block)
        inputs = hidden[rows, :].astype(F32)
        scale = lax.rsqrt(jnp.mean(inputs * inputs, axis=-1, keepdims=True) + eps_norm)
        normed = (inputs * scale * gain_one[...]).astype(BF16)
        values[rows, :] = mm(normed, w_value[...]).astype(BF16)
        swap = swap_halves(lanes)
        for weight_ref, made in ((w_query, query), (w_key, keys)):
            plain = mm(normed, weight_ref[...])
            swapped = mm(normed, mm(weight_ref[...], swap).astype(BF16))
            made[rows, :] = (plain * cosine[rows, :] + swapped * sine[rows, :]).astype(BF16)

    def project(i):
        rows = pl.ds(i * block, block)
        piece(i, 1).wait_recv()
        piece(i, 2).wait_recv()
        total = hidden[rows, :].astype(F32)
        for m in range(4):
            total = total + mm(mixed_all[m, rows, :], out_all[m])
        residual[rows, :] = total
        scale = lax.rsqrt(jnp.mean(total * total, axis=-1, keepdims=True) + eps_norm)
        normed_two[rows, :] = (total * scale * gain_two[...]).astype(BF16)

    for i in range(blocks):
        rows = pl.ds(i * block, block)
        reach = (i + 1) * block
        key_at = lax.broadcasted_iota(jnp.int32, (reach, block), 0)
        query_at = lax.broadcasted_iota(jnp.int32, (reach, block), 1) + i * block
        allowed = (seg_col[0:reach, :] == seg_row[:, rows]) & (key_at <= query_at)
        q_block = query[rows, :] * (HD ** (-0.5))
        mixed = jnp.zeros((block, lanes), F32)
        for h in range(heads):
            scores = mm_nt(keys[0:reach, :], only(q_block, h))
            scores = jnp.where(allowed, scores, -1e30)
            top = jnp.max(scores, axis=0, keepdims=True)
            expo = jnp.exp(scores - top)
            total = jnp.sum(expo, axis=0, keepdims=True)
            prob = (expo * (1.0 / total)).astype(BF16)
            mixed = mixed + mm_tn(prob, only(values[0:reach, :], h))
            summary[h : h + 1, rows] = top + jnp.log(total)
        mixed_all[t, rows, :] = mixed.astype(BF16)
        piece(i, 0).start()
        piece(i, 1).start()
        if i == 0:
            weight(0).wait_recv()
            weight(2).start()
        else:
            piece(i - 1, 0).wait_recv()
            piece(i - 1, 2).start()
        if i == 1:
            own.wait()
            weight(1).wait_recv()
            weight(2).wait_recv()
        if i >= 2:
            project(i - 2)
    piece(blocks - 1, 0).wait_recv()
    piece(blocks - 1, 2).start()
    for i in range(max(blocks - 2, 0), blocks):
        project(i)
    for i in range(blocks):
        for k in range(3):
            piece(i, k).wait_send()
    for k in range(3):
        weight(k).wait_send()


def attend(hidden, gain_one, w_query, w_key, w_value, w_out, gain_two, tables, seg_col, seg_row):
    length, width = hidden.shape
    lanes = w_query.shape[1]
    block = length // 4
    shape = jax.ShapeDtypeStruct
    vmem = pl.BlockSpec(memory_space=pltpu.VMEM)
    dma = pltpu.SemaphoreType.DMA
    return pl.pallas_call(
        functools.partial(attend_kernel, block),
        out_shape=(
            shape((length, lanes), BF16),
            shape((length, lanes), BF16),
            shape((length, lanes), BF16),
            shape((8, length), F32),
            shape((length, width), F32),
            shape((length, width), BF16),
            shape((4, length, lanes), BF16),
        ),
        in_specs=[vmem] * 11,
        out_specs=(vmem,) * 7,
        scratch_shapes=[
            pltpu.VMEM((4, lanes, width), BF16),
            dma((4, 3)),
            dma((4, 3)),
            dma((3,)),
            dma((3,)),
            dma,
        ],
        compiler_params=pltpu.CompilerParams(
            collective_id=1, has_side_effects=True, vmem_limit_bytes=56 * 2**20
        ),
        name="attend",
    )(hidden, gain_one, w_query, w_key, w_value, w_out, gain_two, *tables, seg_col, seg_row)


def rope_tables(length, head_dim):
    half = head_dim // 2
    freqs = 10000.0 ** (-2.0 * jnp.arange(half, dtype=jnp.float32) / head_dim)
    angles = jnp.arange(length, dtype=jnp.float32)[:, None] * freqs[None, :]
    return (jnp.cos(angles), jnp.sin(angles))


def rotate(vec, cosine, sine):
    half = vec.shape[-1] // 2
    first = vec[..., :half]
    second = vec[..., half:]
    return jnp.concatenate(
        [first * cosine - second * sine, second * cosine + first * sine], axis=-1
    )


def rotate_back(grad, cosine, sine):
    half = grad.shape[-1] // 2
    first = grad[..., :half]
    second = grad[..., half:]
    return jnp.concatenate(
        [first * cosine + second * sine, second * cosine - first * sine], axis=-1
    )


def silu_slope(value):
    sigma = jax.nn.sigmoid(value)
    return sigma * (1.0 + value * (1.0 - sigma))


def norm_back(grad, value, scale, gain):
    scaled = grad * gain
    inner = jnp.mean(scaled * value, axis=-1, keepdims=True)
    return (
        scale * scaled - value * scale * scale * scale * inner,
        jnp.sum(grad * value * scale, axis=0),
    )


def split_heads(flat, heads):
    return flat.reshape(flat.shape[0], heads, -1).transpose(1, 0, 2)


def merge_heads(stacked):
    return stacked.transpose(1, 0, 2).reshape(stacked.shape[1], -1)


def block_scores(q_block, keys, segment, start, block):
    length = keys.shape[1]
    scale = keys.shape[2] ** (-0.5)
    seg_block = lax.dynamic_slice_in_dim(segment, start, block, 0)
    places = jnp.arange(length)
    rows_at = start + jnp.arange(block)
    allowed = (seg_block[:, None] == segment[None, :]) & (places[None, :] <= rows_at[:, None])
    scores = jnp.einsum("hqd,hkd->hqk", q_block, keys, preferred_element_type=jnp.float32) * scale
    return (jnp.where(allowed[None], scores, -1e30), allowed)


def attend_forward(query, keys, values, segment, block):
    heads, length, width = query.shape

    def one_block(start):
        q_block = lax.dynamic_slice_in_dim(query, start, block, 1)
        scores, allowed = block_scores(q_block, keys, segment, start, block)
        top = jnp.max(scores, axis=-1, keepdims=True)
        expo = jnp.exp(scores - top)
        total = jnp.sum(expo, axis=-1, keepdims=True)
        prob = (expo / total).astype(jnp.bfloat16)
        mixed = jnp.einsum("hqk,hkd->hqd", prob, values, preferred_element_type=jnp.float32)
        return (mixed, (top + jnp.log(total))[..., 0])

    starts = jnp.arange(length // block) * block
    mixed, summary = lax.map(one_block, starts)
    mixed = mixed.transpose(1, 0, 2, 3).reshape(heads, length, width)
    summary = summary.transpose(1, 0, 2).reshape(heads, length)
    return (mixed, summary)


def attend_backward(query, keys, values, segment, summary, grad_mixed, block):
    heads, length, width = query.shape
    scale = width ** (-0.5)

    def one_block(carry, start):
        grad_keys, grad_values = carry
        q_block = lax.dynamic_slice_in_dim(query, start, block, 1)
        scores, allowed = block_scores(q_block, keys, segment, start, block)
        sum_block = lax.dynamic_slice_in_dim(summary, start, block, 1)
        prob = jnp.where(allowed[None], jnp.exp(scores - sum_block[..., None]), 0.0)
        grad_block = lax.dynamic_slice_in_dim(grad_mixed, start, block, 1)
        grad_prob = jnp.einsum(
            "hqd,hkd->hqk", grad_block, values, preferred_element_type=jnp.float32
        )
        inner = jnp.sum(prob * grad_prob, axis=-1, keepdims=True)
        grad_scores = (prob * (grad_prob - inner)).astype(jnp.bfloat16)
        grad_q = (
            jnp.einsum("hqk,hkd->hqd", grad_scores, keys, preferred_element_type=jnp.float32)
            * scale
        )
        grad_keys = (
            grad_keys
            + jnp.einsum("hqk,hqd->hkd", grad_scores, q_block, preferred_element_type=jnp.float32)
            * scale
        )
        grad_values = grad_values + jnp.einsum(
            "hqk,hqd->hkd",
            prob.astype(jnp.bfloat16),
            grad_block,
            preferred_element_type=jnp.float32,
        )
        return ((grad_keys, grad_values), grad_q)

    starts = jnp.arange(length // block) * block
    zeros = jnp.zeros((heads, length, width), jnp.float32)
    (grad_keys, grad_values), grad_q = lax.scan(one_block, (zeros, zeros), starts)
    grad_q = grad_q.transpose(1, 0, 2, 3).reshape(heads, length, width)
    return (grad_q, grad_keys, grad_values)


def body(
    hidden_in,
    norm_attn,
    w_query,
    w_key,
    w_value,
    w_out,
    norm_ffn,
    w_router,
    shared_gate,
    shared_up,
    shared_down,
    expert_gate,
    expert_up,
    expert_down,
    segment,
    routes,
    slots,
    teacher,
):
    length, width = hidden_in.shape
    groups = lax.axis_size("expert")
    members = lax.axis_size("tensor")
    me = lax.axis_index("tensor")
    quarter = width // members
    experts = w_router.shape[1]
    capacity = 3 * length // groups
    share = capacity // members
    rows = groups * share
    tokens = length * groups
    local_heads = w_query.shape[1] // HD
    block = min(512, length)
    f32, bf16 = jnp.float32, jnp.bfloat16

    gate_all = lax.all_gather(expert_gate[0], "tensor", axis=0)
    up_all = lax.all_gather(expert_up[0], "tensor", axis=0)
    down_all = lax.all_gather(expert_down[0], "tensor", axis=0)

    tables = rope_rows(length, local_heads)
    query_rows, keys_rows, values_rows, summary_rows, residual, normed_two, mixed_all = attend(
        hidden_in,
        norm_attn[None],
        w_query,
        w_key,
        w_value,
        w_out,
        norm_ffn[None],
        tables,
        segment[:, None],
        segment[None],
    )
    mixed_low = lax.dynamic_index_in_dim(mixed_all, me, 0, keepdims=False)
    query, keys, values = (split_heads(a, local_heads) for a in (query_rows, keys_rows, values_rows))
    summary = summary_rows[:local_heads]
    inputs = hidden_in.astype(f32)
    scale_one = lax.rsqrt(jnp.mean(inputs * inputs, axis=-1, keepdims=True) + eps_norm)
    normed_one = (inputs * scale_one * norm_attn).astype(bf16)
    scale_two = lax.rsqrt(jnp.mean(residual * residual, axis=-1, keepdims=True) + eps_norm)
    cosine, sine = rope_tables(length, HD)
    logits = mm(normed_two, w_router)
    onehot = (routes[:, :, None] == jnp.arange(experts, dtype=jnp.int32)[None, None, :]).astype(f32)
    chosen = jnp.sum(logits[:, None, :] * onehot, axis=2)
    gates = jax.nn.softmax(chosen, axis=1)
    mine = (slots < capacity) & (slots // share == me)
    place = jnp.where(mine, routes * share + slots - me * share, -1)
    columns = jnp.arange(rows, dtype=jnp.int32)[None, :]
    pick = [(place[:, k][:, None] == columns).astype(bf16) for k in range(2)]
    outgoing = mm((pick[0] + pick[1]).T, normed_two).astype(bf16).reshape(groups, share, width)
    arrived = lax.all_to_all(outgoing, "expert", split_axis=0, concat_axis=0, tiled=True)
    side_pre = mm(normed_two, shared_gate)
    side_lin = mm(normed_two, shared_up)
    side_hidden = (jax.nn.silu(side_pre) * side_lin).astype(bf16)
    side_part = mm(side_hidden, shared_down)
    rows_in = arrived.reshape(rows, width)
    pre = [mm(rows_in, gate_all[m]) for m in range(members)]
    lin = [mm(rows_in, up_all[m]) for m in range(members)]
    hid = [(jax.nn.silu(p) * u).astype(bf16) for p, u in zip(pre, lin)]
    made = sum(mm(hid[m], down_all[m]) for m in range(members))
    returned = lax.all_to_all(
        made.astype(bf16).reshape(groups, share, width),
        "expert",
        split_axis=0,
        concat_axis=0,
        tiled=True,
    ).reshape(rows, width)
    fetched = [mm(p, returned) for p in pick]
    mixture = gates[:, 0:1] * fetched[0] + gates[:, 1:2] * fetched[1]
    own = lax.dynamic_slice_in_dim
    part_sum = lax.psum_scatter(
        (side_part + mixture).astype(bf16), "tensor", scatter_dimension=1, tiled=True
    ).astype(f32)
    final = own(residual, me * quarter, quarter, 1) + part_sum
    valid = (segment != 0).astype(f32)
    error = (final - teacher.astype(f32)) * valid[:, None]
    grad_full = lax.all_gather(error.astype(bf16), "tensor", axis=1, tiled=True)
    grad_wide = grad_full.astype(f32)
    gate_part = jnp.concatenate(
        [jnp.sum(grad_wide * f, axis=1, keepdims=True) for f in fetched], axis=1
    )
    pair_grad = [(gates[:, k : k + 1] * grad_wide).astype(bf16) for k in range(2)]
    grad_out_rows = (mm(pick[0].T, pair_grad[0]) + mm(pick[1].T, pair_grad[1])).astype(bf16)
    grad_arrived = lax.all_to_all(
        grad_out_rows.reshape(groups, share, width), "expert", split_axis=0, concat_axis=0, tiled=True
    ).reshape(rows, width)
    grad_side_hidden = mm(grad_full, shared_down.T)
    grad_shared_down = mm(side_hidden.T, grad_full)
    side_pre_grad = (grad_side_hidden * side_lin * silu_slope(side_pre)).astype(bf16)
    side_lin_grad = (grad_side_hidden * jax.nn.silu(side_pre)).astype(bf16)
    grad_shared_gate = mm(normed_two.T, side_pre_grad)
    grad_shared_up = mm(normed_two.T, side_lin_grad)
    grad_normed = mm(side_pre_grad, shared_gate.T) + mm(side_lin_grad, shared_up.T)

    grad_hid = [mm(grad_arrived, down_all[m].T) for m in range(members)]
    pre_grad = [
        (g * u * silu_slope(p)).astype(bf16) for g, u, p in zip(grad_hid, lin, pre)
    ]
    lin_grad = [(g * jax.nn.silu(p)).astype(bf16) for g, p in zip(grad_hid, pre)]
    grad_rows = sum(
        mm(pre_grad[m], gate_all[m].T) + mm(lin_grad[m], up_all[m].T) for m in range(members)
    )
    grad_back = lax.all_to_all(
        grad_rows.astype(bf16).reshape(groups, share, width),
        "expert",
        split_axis=0,
        concat_axis=0,
        tiled=True,
    ).reshape(rows, width)

    def reduced(parts):
        return lax.psum_scatter(jnp.stack(parts), "tensor", scatter_dimension=0)

    grad_expert_down = reduced([mm(h.T, grad_arrived).astype(bf16) for h in hid])
    grad_expert_gate = reduced([mm(rows_in.T, g).astype(bf16) for g in pre_grad])
    grad_expert_up = reduced([mm(rows_in.T, g).astype(bf16) for g in lin_grad])

    grad_normed = grad_normed + mm(pick[0] + pick[1], grad_back)
    grad_chosen = gates * (gate_part - jnp.sum(gates * gate_part, axis=1, keepdims=True))
    grad_logits = jnp.sum(grad_chosen[:, :, None] * onehot, axis=1).astype(bf16)
    grad_router = mm(normed_two.T, grad_logits)
    grad_normed = grad_normed + mm(grad_logits, w_router.T)
    grad_normed = lax.psum(grad_normed.astype(bf16), "tensor").astype(f32)
    grad_through, grad_norm_ffn = norm_back(grad_normed, residual, scale_two, norm_ffn)
    grad_residual = grad_wide + grad_through
    grad_attention = grad_residual.astype(bf16)
    grad_w_out = mm(mixed_low.T, grad_attention)
    grad_mixed = split_heads(mm(grad_attention, w_out.T), local_heads).astype(bf16)
    grad_q, grad_k, grad_v = attend_backward(
        query, keys, values, segment, summary, grad_mixed, block
    )
    grad_q = merge_heads(rotate_back(grad_q, cosine, sine)).astype(bf16)
    grad_k = merge_heads(rotate_back(grad_k, cosine, sine)).astype(bf16)
    grad_v = merge_heads(grad_v).astype(bf16)
    grad_w_query = mm(normed_one.T, grad_q)
    grad_w_key = mm(normed_one.T, grad_k)
    grad_w_value = mm(normed_one.T, grad_v)
    grad_normed_one = mm(grad_q, w_query.T) + mm(grad_k, w_key.T) + mm(grad_v, w_value.T)
    grad_normed_one = lax.psum(grad_normed_one.astype(bf16), "tensor").astype(f32)
    grad_inner, grad_norm_attn = norm_back(grad_normed_one, inputs, scale_one, norm_attn)
    grad_input = grad_residual + grad_inner
    early = lax.psum(
        tuple(g.astype(bf16) for g in (grad_shared_gate, grad_shared_up, grad_shared_down)), "expert"
    )
    late = lax.psum(
        tuple(g.astype(bf16) for g in (grad_w_query, grad_w_key, grad_w_value, grad_w_out)), "expert"
    )
    square_sum, count, grad_router, grad_norm_ffn, grad_norm_attn = lax.psum(
        (
            jnp.sum(error * error),
            jnp.sum(valid) / members,
            grad_router,
            grad_norm_ffn / members,
            grad_norm_attn / members,
        ),
        ("expert", "tensor"),
    )
    factor = 2.0 * tokens / count

    def scaled(value):
        return value.astype(f32) * factor

    return (
        square_sum / (count * width),
        final.astype(bf16),
        scaled(own(grad_input, me * quarter, quarter, 1)),
        scaled(grad_norm_attn),
        *(scaled(g) for g in late),
        scaled(grad_norm_ffn),
        scaled(grad_router),
        *(scaled(g) for g in early),
        scaled(grad_expert_gate)[None],
        scaled(grad_expert_up)[None],
        scaled(grad_expert_down)[None],
    )


def solution(mesh):
    placed = (
        P("expert", None),
        P(),
        P(None, "tensor"),
        P(None, "tensor"),
        P(None, "tensor"),
        P("tensor", None),
        P(),
        P(),
        P(None, "tensor"),
        P(None, "tensor"),
        P("tensor", None),
        P("expert", None, "tensor"),
        P("expert", None, "tensor"),
        P("expert", "tensor", None),
        P("expert"),
        P("expert", None),
        P("expert", None),
        P("expert", "tensor"),
    )
    return jax.shard_map(
        body,
        mesh=mesh,
        in_specs=placed,
        out_specs=(
            P(),
            P("expert", "tensor"),
            P("expert", "tensor"),
            P(),
            P(None, "tensor"),
            P(None, "tensor"),
            P(None, "tensor"),
            P("tensor", None),
            P(),
            P(),
            P(None, "tensor"),
            P(None, "tensor"),
            P("tensor", None),
            P("expert", None, "tensor"),
            P("expert", None, "tensor"),
            P("expert", "tensor", None),
        ),
        check_vma=False,
    )
```

```python
import functools

import jax
import jax.numpy as jnp
import numpy as np
from jax import lax
from jax.experimental import pallas as pl
from jax.experimental.pallas import tpu as pltpu
from jax.sharding import PartitionSpec as P

HD = 64
F32, BF16 = jnp.float32, jnp.bfloat16
MESH = pl.DeviceIdType.MESH


eps_norm = 1e-06


def rope_rows(length, heads):
    half = HD // 2
    freqs = (10000.0 ** (-2.0 * np.arange(half) / HD)).astype(np.float32)
    angles = np.arange(length, dtype=np.float32)[:, None] * freqs[None, :]
    cosine, sine = np.cos(angles), np.sin(angles)
    return (
        np.tile(np.concatenate([cosine, cosine], axis=1), (1, heads)).astype(np.float32),
        np.tile(np.concatenate([-sine, sine], axis=1), (1, heads)).astype(np.float32),
    )


def peer_of(t, step):
    if step == 1:
        return t + 1 - 2 * lax.rem(t, 2)
    return lax.rem(t + 2, 4)


def greet(peers):
    barrier = pltpu.get_barrier_semaphore()
    for peer in peers:
        pl.semaphore_signal(barrier, inc=1, device_id=peer, device_id_type=MESH)
    pl.semaphore_wait(barrier, len(peers))


def mm(a, b):
    return lax.dot_general(a, b, (((1,), (0,)), ((), ())), preferred_element_type=F32)


def mm_nt(a, b):
    return lax.dot_general(a, b, (((1,), (1,)), ((), ())), preferred_element_type=F32)


def mm_tn(a, b):
    return lax.dot_general(a, b, (((0,), (0,)), ((), ())), preferred_element_type=F32)


def swap_halves(width):
    row = lax.broadcasted_iota(jnp.int32, (width, width), 0)
    col = lax.broadcasted_iota(jnp.int32, (width, width), 1)
    half = HD // 2
    other = jnp.where(lax.rem(col, HD) < half, col + half, col - half)
    return (row == other).astype(F32).astype(BF16)


def head_mask(rows, width, head):
    col = lax.broadcasted_iota(jnp.int32, (rows, width), 1)
    return (col >= head * HD) & (col < (head + 1) * HD)


def only(value, head):
    keep = head_mask(value.shape[0], value.shape[1], head)
    return jnp.where(keep, value, jnp.zeros_like(value))


def column_of(row):
    wide = jnp.broadcast_to(row.astype(F32), (128, row.shape[1]))
    return wide.T[:, 0:1]


def own_columns(lanes, width, t):
    row = lax.broadcasted_iota(jnp.int32, (lanes, width), 0)
    col = lax.broadcasted_iota(jnp.int32, (lanes, width), 1)
    return (col == row + t * lanes).astype(F32).astype(BF16)


class Stream:
    def __init__(self, buf, out, base, size, order, land, land_at, send, recv, index):
        self.buf, self.out, self.land, self.index = buf, out, land, index
        self.send, self.recv = send, recv
        e, self.t = lax.axis_index("expert"), lax.axis_index("tensor")
        self.stages, start = [], base
        for k, b in enumerate(order):
            half = size >> (k + 1)
            bit = lax.rem(e // 2**b, 2)
            keep = pl.ds(pl.multiple_of(start + bit * half, 16), half)
            give = pl.ds(pl.multiple_of(start + (1 - bit) * half, 16), half)
            self.stages.append((e + 2**b - 2 * 2**b * bit, keep, give, pl.ds(land_at, half)))
            land_at += half
            start = start + bit * half

    def copy(self, step, arriving=False):
        peer, keep, give, land = self.stages[step if step < 3 else 5 - step]
        if step < 3:
            src, dst = self.buf.at[give], self.land.at[land]
        else:
            src, dst = self.out.at[keep], self.out.at[give if arriving else keep]
        return pltpu.make_async_remote_copy(
            src_ref=src,
            dst_ref=dst,
            send_sem=self.send.at[self.index, step],
            recv_sem=self.recv.at[self.index, step],
            device_id=(peer, self.t),
            device_id_type=MESH,
        )

    def begin(self, step):
        if step == 3 and self.buf is not None:
            keep = self.stages[2][1]
            self.out[keep, :] = self.buf[keep, :]
        self.copy(step).start()

    def end(self, step):
        self.copy(step, True).wait_recv()
        if step < 3:
            _, keep, _, land = self.stages[step]
            self.buf[keep, :] = (
                self.buf[keep, :].astype(F32) + self.land[land, :].astype(F32)
            ).astype(BF16)

    def close(self, steps):
        for step in steps:
            self.copy(step).wait_send()


def advance(streams, last, first):
    for s in streams:
        if last is not None:
            s.end(last)
        if first is not None:
            s.begin(first)


def expert_peers(bits):
    e, t = lax.axis_index("expert"), lax.axis_index("tensor")
    return [(e + 2**b - 2 * 2**b * lax.rem(e // 2**b, 2), t) for b in range(bits)]


def attend_kernel(
    block,
    hidden,
    gain_one,
    w_query,
    w_key,
    w_value,
    w_out,
    gain_two,
    cosine,
    sine,
    seg_row,
    query,
    keys,
    values,
    summary,
    residual,
    normed_two,
    mixed_own,
    values_turned,
    mixed_all,
    out_all,
    send_sem,
    recv_sem,
    wsend_sem,
    wrecv_sem,
    copy_sem,
):
    length = hidden.shape[0]
    lanes = w_query.shape[0]
    heads = lanes // HD
    blocks = length // block
    e, t = lax.axis_index("expert"), lax.axis_index("tensor")
    beside, across = peer_of(t, 1), peer_of(t, 2)
    gain_one_row = gain_one[...].reshape(1, -1)
    gain_two_row = gain_two[...].reshape(1, -1)
    greet([(e, beside), (e, across)])

    def share(src, dst, device, sem):
        return pltpu.make_async_remote_copy(
            src_ref=src,
            dst_ref=dst,
            send_sem=sem[0],
            recv_sem=sem[1],
            device_id=(e, device),
            device_id_type=MESH,
        )

    def weight(k):
        src = w_out if k < 2 else out_all.at[across]
        dst = out_all.at[t] if k < 2 else out_all.at[across]
        return share(src, dst, across if k == 0 else beside, (wsend_sem.at[k], wrecv_sem.at[k]))

    own = pltpu.make_async_copy(w_out, out_all.at[t], copy_sem)
    own.start()
    weight(0).start()
    weight(1).start()
    seg_col = column_of(seg_row[...])
    seg_line = seg_row[...].astype(F32)

    def piece(i, k):
        slot = t if k < 2 else across
        ref = mixed_all.at[slot, i]
        return share(
            ref, ref, across if k == 0 else beside, (send_sem.at[i, k], recv_sem.at[i, k])
        )

    swap = swap_halves(lanes)
    turns = [mm(swap, w[...]).astype(BF16) for w in (w_query, w_key)]

    def make(i):
        rows = pl.ds(i * block, block)
        inputs = hidden[rows, :].astype(F32)
        scale = lax.rsqrt(jnp.mean(inputs * inputs, axis=-1, keepdims=True) + eps_norm)
        normed = (inputs * scale * gain_one_row).astype(BF16)
        values[rows, :] = mm_nt(normed, w_value[...]).astype(BF16)
        values_turned[:, rows] = mm_nt(w_value[...], normed).astype(BF16)
        for weight_ref, turn, made in zip((w_query, w_key), turns, (query, keys)):
            plain = mm_nt(normed, weight_ref[...])
            swapped = mm_nt(normed, turn)
            made[rows, :] = (plain * cosine[rows, :] + swapped * sine[rows, :]).astype(BF16)

    def project(i):
        rows = pl.ds(i * block, block)
        piece(i, 1).wait_recv()
        piece(i, 2).wait_recv()
        total = hidden[rows, :].astype(F32)
        for m in range(4):
            total = total + mm_tn(mixed_all[m, i], out_all[m])
        residual[rows, :] = total
        scale = lax.rsqrt(jnp.mean(total * total, axis=-1, keepdims=True) + eps_norm)
        normed_two[rows, :] = (total * scale * gain_two_row).astype(BF16)

    for i in range(blocks):
        make(i)
        rows = pl.ds(i * block, block)
        reach = (i + 1) * block
        key_at = lax.broadcasted_iota(jnp.int32, (reach, block), 0)
        query_at = lax.broadcasted_iota(jnp.int32, (reach, block), 1) + i * block
        allowed = (seg_col[0:reach, :] == seg_line[:, i * block : (i + 1) * block]) & (key_at <= query_at)
        q_block = query[rows, :] * (HD ** (-0.5))
        for h in range(heads):
            head = slice(h * HD, (h + 1) * HD)
            scores = mm_nt(keys[0:reach, :], only(q_block, h))
            scores = jnp.where(allowed, scores, -1e30)
            top = jnp.max(scores, axis=0, keepdims=True)
            expo = jnp.exp(scores - top)
            total = jnp.sum(expo, axis=0, keepdims=True)
            prob = (expo * (1.0 / total)).astype(BF16)
            mixed_all[t, i, head, :] = mm(values_turned[head, 0:reach], prob).astype(BF16)
            summary[h : h + 1, rows] = top + jnp.log(total)
        mixed_own[:, rows] = mixed_all[t, i]
        piece(i, 0).start()
        piece(i, 1).start()
        if i == 0:
            weight(0).wait_recv()
            weight(2).start()
        else:
            piece(i - 1, 0).wait_recv()
            piece(i - 1, 2).start()
        if i == 1:
            own.wait()
            weight(1).wait_recv()
            weight(2).wait_recv()
        if i >= 2:
            project(i - 2)
    piece(blocks - 1, 0).wait_recv()
    piece(blocks - 1, 2).start()
    for i in range(max(blocks - 2, 0), blocks):
        project(i)
    for i in range(blocks):
        for k in range(3):
            piece(i, k).wait_send()
    for k in range(3):
        weight(k).wait_send()


def attend(
    hidden, gain_one, w_query, w_key, w_value, w_out, gain_two, tables, seg_row
):
    length, width = hidden.shape
    lanes = w_query.shape[0]
    block = length // 4
    shape = jax.ShapeDtypeStruct
    vmem = pl.BlockSpec(memory_space=pltpu.VMEM)
    dma = pltpu.SemaphoreType.DMA
    return pl.pallas_call(
        functools.partial(attend_kernel, block),
        out_shape=(
            shape((length, lanes), BF16),
            shape((length, lanes), BF16),
            shape((length, lanes), BF16),
            shape((8, length), F32),
            shape((length, width), F32),
            shape((length, width), BF16),
            shape((lanes, length), BF16),
        ),
        in_specs=[vmem] * 10,
        out_specs=(vmem,) * 7,
        scratch_shapes=[
            pltpu.VMEM((lanes, length), BF16),
            pltpu.VMEM((4, 4, lanes, block), BF16),
            pltpu.VMEM((4, lanes, width), BF16),
            dma((4, 3)),
            dma((4, 3)),
            dma((3,)),
            dma((3,)),
            dma,
        ],
        compiler_params=pltpu.CompilerParams(
            collective_id=1, has_side_effects=True, vmem_limit_bytes=56 * 2**20
        ),
        name="attend",
    )(hidden, gain_one, w_query, w_key, w_value, w_out, gain_two, *tables, seg_row)


def each(count, do):
    if count <= 8:
        for i in range(count):
            do(i)
    else:
        lax.fori_loop(0, count, lambda i, none: (do(i), none)[1], 0)


def steps(count, do):
    lax.fori_loop(0, count, lambda i, none: (do(i), none)[1], 0)


def side_streams(groups, wide, tall, halving, wide_land, tall_land, send, recv):
    if groups != 8:
        return []
    rows, few = wide.shape[0] // 2, tall.shape[0] // 2
    wides = (wide, None) if halving else (None, wide)
    talls = (tall, None) if halving else (None, tall)
    return [
        Stream(*wides, 0, rows, (0, 1, 2), wide_land, 0, send, recv, 0),
        Stream(*wides, rows, rows, (1, 0, 2), wide_land, 7 * rows // 8, send, recv, 1),
        Stream(*talls, 0, few, (0, 1, 2), tall_land, 0, send, recv, 2),
        Stream(*talls, few, few, (1, 0, 2), tall_land, 7 * few // 8, send, recv, 3),
    ]


def moe_kernel(
    groups,
    share,
    pad,
    normed,
    residual,
    teacher,
    seg_row,
    routes,
    slots,
    router,
    gain,
    shared_gate,
    shared_up,
    shared_down,
    gate_in,
    up_in,
    down_in,
    activations,
    grad_residual,
    side_wide,
    side_tall,
    grad_gate,
    grad_up,
    grad_down,
    small,
    grad_router,
    gate_all,
    up_all,
    down_all,
    pick,
    weigh,
    out_buf,
    back_buf,
    rows_in,
    returned,
    grad_rows,
    act,
    slope,
    hidden,
    side_act,
    side_slope,
    side_hidden,
    residual_half,
    off,
    part,
    error,
    pair_dot,
    wide_land,
    tall_land,
    half_out,
    half_in,
    chip_out,
    chip_in,
    a2a_send,
    a2a_recv,
    sum_send,
    sum_recv,
    gather_send,
    gather_recv,
    side_send,
    side_recv,
    pair_send,
    pair_recv,
    free_sem,
    copy_sem,
):
    length, width = normed.shape
    lanes = teacher.shape[0]
    units = shared_gate.shape[1]
    experts = router.shape[0]
    rows = groups * pad
    half_groups, half_rows = groups // 2, rows // 2
    chunk = length // 4
    e, t = lax.axis_index("expert"), lax.axis_index("tensor")
    beside, across = peer_of(t, 1), peer_of(t, 2)
    gain_row = gain[...].reshape(1, -1)
    greet(
        [(lax.rem(e + j, groups), t) for j in range(1, groups)] + [(e, beside), (e, across)]
    )

    def remote(src, dst, device, send, recv):
        return pltpu.make_async_remote_copy(
            src_ref=src,
            dst_ref=dst,
            send_sem=send,
            recv_sem=recv,
            device_id=device,
            device_id_type=MESH,
        )

    gathers = ((gate_in, gate_all), (up_in, up_all), (down_in, down_all))

    def gather(w, k):
        src, slots_ref = gathers[w]
        slot = t if k < 2 else across
        return remote(
            src if k < 2 else slots_ref.at[slot],
            slots_ref.at[slot],
            (e, across if k == 0 else beside),
            gather_send.at[w, k],
            gather_recv.at[w, k],
        )

    def own_weights(w):
        src, slots_ref = gathers[w]
        return pltpu.make_async_copy(src, slots_ref.at[t], copy_sem.at[w])

    for w in range(3):
        gather(w, 0).start()
        gather(w, 1).start()
        own_weights(w).start()
    core = lax.rem(t, 2)
    half_copy = pltpu.make_async_copy(
        residual.at[pl.ds(pl.multiple_of(core * (length // 2), 16), length // 2)],
        residual_half,
        copy_sem.at[11],
    )
    half_copy.start()
    seg_col = column_of(seg_row[...])

    far_half = 1 - e // half_groups
    near_half = e // half_groups

    def block_at(group):
        return pl.ds(pl.multiple_of(group * pad, 16), pad)

    def half_at(half):
        return pl.ds(pl.multiple_of(half * half_rows, 16), half_rows)

    def exchange(phase, sent, landed, group):
        return remote(
            sent.at[block_at(group)],
            landed.at[block_at(e)],
            (group, t),
            a2a_send.at[phase, group],
            a2a_recv.at[phase, e],
        )

    def arrival(phase, sent, landed, group):
        return remote(
            sent.at[block_at(group)],
            landed.at[block_at(group)],
            (group, t),
            a2a_send.at[phase, group],
            a2a_recv.at[phase, group],
        )

    def near_group(j):
        return near_half * half_groups + lax.rem(e + j, half_groups)

    def far_group(j):
        return far_half * half_groups + lax.rem(e + j, half_groups)

    def send_far(phase, sent, landed):
        each(half_groups, lambda j: exchange(phase, sent, landed, far_group(j)).start())

    def send_near(phase, sent, landed):
        each(half_groups - 1, lambda j: exchange(phase, sent, landed, near_group(j + 1)).start())
        landed[block_at(e), :] = sent[block_at(e), :]

    def await_far(phase, sent, landed):
        each(half_groups, lambda j: arrival(phase, sent, landed, far_group(j)).wait_recv())

    def await_near(phase, sent, landed):
        each(half_groups - 1, lambda j: arrival(phase, sent, landed, near_group(j + 1)).wait_recv())

    def await_sent(phase, sent, landed):
        each(half_groups, lambda j: exchange(phase, sent, landed, far_group(j)).wait_send())
        each(half_groups - 1, lambda j: exchange(phase, sent, landed, near_group(j + 1)).wait_send())

    low = t * share
    mine = (slots[...] >= low) & (slots[...] < low + share)
    place = jnp.where(mine, routes[...] * pad + slots[...] - low, -1)
    place_one, place_two = place[0:1, :], place[1:2, :]
    build = rows // 8

    def pick_rows(i):
        at = lax.broadcasted_iota(jnp.int32, (build, length), 0) + i * build
        hit = (at == place_one) | (at == place_two)
        block = pl.ds(pl.multiple_of(i * build, 16), build)
        pick[block, :] = jnp.where(hit, 1.0, 0.0).astype(BF16)

    for half, send in ((far_half, send_far), (near_half, send_near)):
        steps(4, lambda i, half=half: pick_rows(half * 4 + i))
        out_buf[half_at(half), :] = mm(pick[half_at(half), :], normed[...]).astype(BF16)
        send(0, out_buf, rows_in)

    logits = mm_nt(router[...], normed[...])
    named = lax.broadcasted_iota(jnp.int32, (experts, length), 0)
    here = [named == routes[k : k + 1, :] for k in range(2)]
    chosen = [jnp.sum(jnp.where(h, logits, 0.0), axis=0, keepdims=True) for h in here]
    top = jnp.maximum(chosen[0], chosen[1])
    raised = [jnp.exp(c - top) for c in chosen]
    total = raised[0] + raised[1]
    gate_one, gate_two = raised[0] / total, raised[1] / total

    def weigh_rows(i):
        at = lax.broadcasted_iota(jnp.int32, (build, length), 0) + i * build
        value = jnp.where(at == place_one, gate_one, jnp.where(at == place_two, gate_two, 0.0))
        weigh[pl.ds(pl.multiple_of(i * build, 16), build), :] = value.astype(BF16)

    steps(8, weigh_rows)

    def tokens_at(i):
        return pl.ds(pl.multiple_of(i * chunk, chunk), chunk)

    def silu_parts(pre, lin):
        sigma = 1.0 / (1.0 + jnp.exp(-pre))
        active = pre * sigma
        return active, lin * (sigma * (1.0 + pre * (1.0 - sigma))), active * lin

    def shared_forward(i):
        at = tokens_at(i)
        a, s, h = silu_parts(mm(normed[at, :], shared_gate[...]), mm(normed[at, :], shared_up[...]))
        side_act[at, :] = a.astype(BF16)
        side_slope[at, :] = s.astype(BF16)
        side_hidden[at, :] = h.astype(BF16)
        part[at, :] = mm(side_hidden[at, :], shared_down[...]) - mm_tn(teacher[:, at], place_own)

    place_own = own_columns(lanes, width, t)
    steps(4, shared_forward)
    half_copy.wait()
    for w in range(3):
        gather(w, 0).wait_recv()
        gather(w, 2).start()
        own_weights(w).wait()
        gather(w, 1).wait_recv()
    for w in range(3):
        gather(w, 2).wait_recv()

    for half, wait, send in (
        (far_half, await_far, send_far),
        (near_half, await_near, send_near),
    ):
        wait(0, out_buf, rows_in)
        at = half_at(half)
        for m in range(4):
            cols = pl.ds(m * units, units)
            a, s, h = silu_parts(mm(rows_in[at, :], gate_all[m]), mm(rows_in[at, :], up_all[m]))
            act[at, cols] = a.astype(BF16)
            slope[at, cols] = s.astype(BF16)
            hidden[at, cols] = h.astype(BF16)
        made = sum(mm(hidden[at, pl.ds(m * units, units)], down_all[m]) for m in range(4))
        back_buf[at, :] = made.astype(BF16)
        send(1, back_buf, returned)

    span = length // 8

    def tokens_of(which, q):
        return pl.ds(pl.multiple_of(which * (length // 2) + q * span, span), span)

    def piece(q):
        return pl.ds(q * span, span)

    def halves(turn, q):
        return remote(
            half_out.at[piece(q)],
            half_in.at[turn, piece(q)],
            (e, beside),
            sum_send.at[turn, 0, q],
            sum_recv.at[turn, 0, q],
        )

    def chips(turn, q):
        return remote(
            chip_out.at[piece(q)],
            chip_in.at[turn, piece(q)],
            (e, across),
            sum_send.at[turn, 1, q],
            sum_recv.at[turn, 1, q],
        )

    def spread(turn, result, which, q):
        return remote(
            result.at[tokens_of(which, q)],
            result.at[tokens_of(which, q)],
            (e, beside),
            sum_send.at[turn, 2, q],
            sum_recv.at[turn, 2, q],
        )

    def combine(matrix, landed, half, tokens, count):
        at = half_at(half)
        part[tokens, :] += mm_tn(matrix[at, tokens], landed[at, :])

    def sum_over_tensor(turn, matrix, landed, wait_near, wait_far, finish, result, then=None):
        wait_near()
        steps(4, lambda i: combine(matrix, landed, near_half, tokens_at(i), chunk))
        wait_far()
        if then is not None:
            then()
        def to_chip(q):
            halves(turn, q).wait_recv()
            chip_out[piece(q), :] = (
                part[tokens_of(core, q), :] + half_in[turn, piece(q), :].astype(F32)
            ).astype(BF16)
            chips(turn, q).start()

        for q in range(4):
            at = tokens_of(1 - core, q)
            combine(matrix, landed, far_half, at, span)
            half_out[piece(q), :] = part[at, :].astype(BF16)
            halves(turn, q).start()
            combine(matrix, landed, far_half, tokens_of(core, q), span)
            if q > 0:
                to_chip(q - 1)
        to_chip(3)
        for q in range(4):
            chips(turn, q).wait_recv()
            finish(
                q,
                tokens_of(core, q),
                chip_out[piece(q), :].astype(F32) + chip_in[turn, piece(q), :].astype(F32),
            )
            spread(turn, result, core, q).start()
        for q in range(4):
            spread(turn, result, 1 - core, q).wait_recv()
        for q in range(4):
            halves(turn, q).wait_send()
            chips(turn, q).wait_send()
            spread(turn, result, core, q).wait_send()

    seen = seg_col != 0.0
    small[...] = jnp.zeros_like(small)
    half_seen = column_of(
        jnp.where(core == 0, seg_row[:, 0 : length // 2], seg_row[:, length // 2 : length])
    )

    def finish_forward(q, at, value):
        value = residual_half[piece(q), :] + value
        off[at, :] = value.astype(BF16)
        value = jnp.where(half_seen[q * span : (q + 1) * span, :] != 0.0, value, 0.0)
        small[0:1, :] += jnp.sum(value * value, axis=0, keepdims=True)

    sum_over_tensor(
        0,
        weigh,
        returned,
        lambda: await_near(1, back_buf, returned),
        lambda: await_far(1, back_buf, returned),
        finish_forward,
        off,
    )
    for i in range(4):
        at = slice(i * chunk, (i + 1) * chunk)
        error[at, :] = jnp.where(seen[at, :], off[at, :].astype(F32), 0.0).astype(BF16)

    await_sent(0, out_buf, rows_in)
    for half, send in ((far_half, send_far), (near_half, send_near)):
        at = half_at(half)
        pair = mm(weigh[at, :], error[...])
        out_buf[at, :] = pair.astype(BF16)
        dots = jnp.sum(pair * returned[at, :].astype(F32), axis=1, keepdims=True)
        pair_dot[at, :] = jnp.broadcast_to(dots, (half_rows, 128))
        send(2, out_buf, grad_rows)
    pl.semaphore_signal(free_sem.at[0], inc=1, device_id=(e, beside), device_id_type=MESH)
    activations[...] = (mm_nt(place_own, off[...]) + teacher[...].astype(F32)).astype(BF16)

    def shared_backward(i):
        at = tokens_at(i)
        hid_grad = mm_nt(error[at, :], shared_down[...])
        side_slope[at, :] = (hid_grad * side_slope[at, :].astype(F32)).astype(BF16)
        side_act[at, :] = (hid_grad * side_act[at, :].astype(F32)).astype(BF16)
        part[at, :] = mm_nt(side_slope[at, :], shared_gate[...]) + mm_nt(
            side_act[at, :], shared_up[...]
        )

    steps(4, shared_backward)
    side_wide[0:width, :] = mm_tn(normed[...], side_slope[...]).astype(BF16)
    side_wide[width : 2 * width, :] = mm_tn(normed[...], side_act[...]).astype(BF16)
    side_tall[...] = mm_tn(side_hidden[...], error[...]).astype(BF16)
    sides = side_streams(
        groups, side_wide, side_tall, True, wide_land, tall_land, side_send, side_recv
    )
    advance(sides, None, 0)

    def take_dots(i, sums):
        block = pl.ds(pl.multiple_of(i * build, 16), build)
        at = lax.broadcasted_iota(jnp.int32, (build, length), 0) + i * build
        dots = pair_dot[block, 0:1]
        return tuple(
            s + jnp.sum(jnp.where(at == p, dots, 0.0), axis=0, keepdims=True)
            for s, p in zip(sums, (place_one, place_two))
        )

    zero = jnp.zeros((1, length), F32)
    dot_one, dot_two = lax.fori_loop(0, 8, take_dots, (zero, zero))
    both = dot_one + dot_two
    grad_logits = (
        jnp.where(here[0], dot_one - gate_one * both, 0.0)
        + jnp.where(here[1], dot_two - gate_two * both, 0.0)
    ).astype(BF16)
    grad_router[...] = mm(grad_logits, normed[...])
    part[...] += mm_tn(grad_logits, router[...])

    await_sent(1, back_buf, returned)
    for half, wait, send in (
        (far_half, await_far, send_far),
        (near_half, await_near, send_near),
    ):
        wait(2, out_buf, grad_rows)
        at = half_at(half)
        for m in range(4):
            cols = pl.ds(m * units, units)
            hid_grad = mm_nt(grad_rows[at, :], down_all[m])
            slope[at, cols] = (hid_grad * slope[at, cols].astype(F32)).astype(BF16)
            act[at, cols] = (hid_grad * act[at, cols].astype(F32)).astype(BF16)
        made = sum(
            mm_nt(slope[at, pl.ds(m * units, units)], gate_all[m])
            + mm_nt(act[at, pl.ds(m * units, units)], up_all[m])
            for m in range(4)
        )
        back_buf[at, :] = made.astype(BF16)
        send(3, back_buf, returned)

    advance(sides, 0, 1)
    for w in range(3):
        for k in range(3):
            gather(w, k).wait_send()
    await_sent(2, out_buf, grad_rows)
    pl.semaphore_signal(free_sem.at[1], inc=1, device_id=(e, across), device_id_type=MESH)
    for m in range(4):
        cols = pl.ds(m * units, units)
        gate_all[m] = mm_tn(rows_in[...], slope[:, cols]).astype(BF16)

    def gate_core(n):
        return remote(
            gate_all.at[(peer_of(across, 1), beside)[n]],
            weigh.at[pl.ds(0, width), pl.ds(n * units, units)],
            (e, beside),
            pair_send.at[n],
            pair_recv.at[n],
        )

    gate_chip = remote(
        gate_all.at[across],
        out_buf.at[pl.ds(0, width), pl.ds(0, units)],
        (e, across),
        pair_send.at[2],
        pair_recv.at[2],
    )
    pl.semaphore_wait(free_sem.at[0], 1)
    gate_core(0).start()
    gate_core(1).start()
    outs = []

    def store(m, w, src, dst):
        out = pltpu.make_async_copy(src.at[m], dst.at[m], copy_sem.at[3 + 2 * m + w])
        out.start()
        outs.append(out)

    for m in range(4):
        up_all[m] = mm_tn(rows_in[...], act[:, pl.ds(m * units, units)]).astype(BF16)
        store(m, 0, up_all, grad_up)
        if m == 0:
            gate_core(0).wait_recv()
            gate_all[across] = (
                gate_all[across].astype(F32) + weigh[0:width, 0:units].astype(F32)
            ).astype(BF16)
            pl.semaphore_wait(free_sem.at[1], 1)
            gate_chip.start()
    for m in range(4):
        down_all[m] = mm_tn(hidden[:, pl.ds(m * units, units)], grad_rows[...]).astype(BF16)
        store(m, 1, down_all, grad_down)

    def finish_backward(q, at, value):
        inputs = residual_half[piece(q), :]
        scale = lax.rsqrt(jnp.mean(inputs * inputs, axis=-1, keepdims=True) + eps_norm)
        scaled = value * gain_row
        inner = jnp.mean(scaled * inputs, axis=-1, keepdims=True)
        through = scale * scaled - inputs * (scale * scale * scale * inner)
        grad_residual[at, :] = (error[at, :].astype(F32) + through).astype(BF16)
        small[1:2, :] += jnp.sum(value * inputs * scale, axis=0, keepdims=True)

    sum_over_tensor(
        1,
        pick,
        returned,
        lambda: await_near(3, back_buf, returned),
        lambda: await_far(3, back_buf, returned),
        finish_backward,
        grad_residual,
        lambda: advance(sides, 1, 2),
    )
    await_sent(3, back_buf, returned)
    advance(sides, 2, None)
    for s in sides:
        s.close(range(3))
    for out in outs:
        out.wait()
    gate_core(1).wait_recv()
    gate_chip.wait()
    grad_gate[...] = (
        gate_all[t].astype(F32)
        + weigh[0:width, units : 2 * units].astype(F32)
        + out_buf[0:width, 0:units].astype(F32)
    ).astype(BF16)
    for n in range(2):
        gate_core(n).wait_send()


def moe(
    groups,
    capacity,
    normed,
    residual,
    teacher,
    seg_row,
    routes,
    slots,
    router,
    gain,
    shared_gate,
    shared_up,
    shared_down,
    gate_in,
    up_in,
    down_in,
):
    length, width = normed.shape
    units = shared_gate.shape[1]
    experts = router.shape[0]
    share = capacity // 4
    pad = -(-share // 16) * 16
    rows = groups * pad
    shape = jax.ShapeDtypeStruct
    vmem = pl.BlockSpec(memory_space=pltpu.VMEM)
    hbm = pl.BlockSpec(memory_space=pl.ANY)
    dma = pltpu.SemaphoreType.DMA
    wide, tall, deep = (4, width, units), (4, units, width), (rows, 4 * units)
    return pl.pallas_call(
        functools.partial(moe_kernel, groups, share, pad),
        out_shape=(
            shape(teacher.shape, BF16),
            shape((length, width), BF16),
            shape((2 * width, units), BF16),
            shape((units, width), BF16),
            shape((width, units), BF16),
            shape(wide, BF16),
            shape(tall, BF16),
            shape((8, width), F32),
            shape((experts, width), F32),
        ),
        in_specs=[vmem, hbm] + [vmem] * 9 + [hbm] * 3,
        out_specs=(vmem,) * 5 + (hbm,) * 2 + (vmem,) * 2,
        scratch_shapes=[
            pltpu.VMEM(wide, BF16),
            pltpu.VMEM(wide, BF16),
            pltpu.VMEM(tall, BF16),
            pltpu.VMEM((rows, length), BF16),
            pltpu.VMEM((rows, length), BF16),
            pltpu.VMEM((rows, width), BF16),
            pltpu.VMEM((rows, width), BF16),
            pltpu.VMEM((rows, width), BF16),
            pltpu.VMEM((rows, width), BF16),
            pltpu.VMEM((rows, width), BF16),
            pltpu.VMEM(deep, BF16),
            pltpu.VMEM(deep, BF16),
            pltpu.VMEM(deep, BF16),
            pltpu.VMEM((length, units), BF16),
            pltpu.VMEM((length, units), BF16),
            pltpu.VMEM((length, units), BF16),
            pltpu.VMEM((length // 2, width), F32),
            pltpu.VMEM((length, width), BF16),
            pltpu.VMEM((length, width), F32),
            pltpu.VMEM((length, width), BF16),
            pltpu.VMEM((rows, 128), F32),
            pltpu.VMEM((7 * width // 4 if groups == 8 else 16, units), BF16),
            pltpu.VMEM((7 * units // 8 if groups == 8 else 16, width), BF16),
            pltpu.VMEM((length // 2, width), BF16),
            pltpu.VMEM((2, length // 2, width), BF16),
            pltpu.VMEM((length // 2, width), BF16),
            pltpu.VMEM((2, length // 2, width), BF16),
            dma((4, groups)),
            dma((4, groups)),
            dma((2, 3, 4)),
            dma((2, 3, 4)),
            dma((3, 3)),
            dma((3, 3)),
            dma((4, 3)),
            dma((4, 3)),
            dma((3,)),
            dma((3,)),
            pltpu.SemaphoreType.REGULAR((2,)),
            dma((12,)),
        ],
        compiler_params=pltpu.CompilerParams(
            collective_id=2, has_side_effects=True, vmem_limit_bytes=63 * 2**20
        ),
        name="moe",
    )(
        normed,
        residual,
        teacher,
        seg_row,
        routes,
        slots,
        router,
        gain,
        shared_gate,
        shared_up,
        shared_down,
        gate_in,
        up_in,
        down_in,
    )


def finish_kernel(
    groups,
    grad_residual,
    hidden,
    gain_one,
    w_query,
    w_key,
    w_value,
    w_out,
    query,
    keys,
    values,
    summary,
    mixed,
    cosine,
    sine,
    seg_row,
    small_in,
    router_in,
    wide_in,
    tall_in,
    up_in,
    down_in,
    grad_input,
    grad_up,
    grad_down,
    side_wide,
    side_tall,
    sums_out,
    small,
    normed,
    grad_mixed,
    grad_query,
    grad_keys,
    grad_values,
    turned,
    product,
    scales,
    pair_wide,
    pair_tall,
    core_wide,
    core_tall,
    chip_wide,
    chip_tall,
    pay,
    pay_core,
    pay_out,
    pay_in,
    sums,
    landed,
    direct_land,
    small_land,
    pair_send,
    pair_recv,
    side_send,
    side_recv,
    sum_send,
    sum_recv,
    direct_send,
    direct_recv,
    small_send,
    small_recv,
    pay_send,
    pay_recv,
    copy_sem,
):
    length, width = hidden.shape
    lanes = w_query.shape[0]
    heads = lanes // HD
    block = length // 4
    bits = 3 if groups == 8 else 0
    e, t = lax.axis_index("expert"), lax.axis_index("tensor")
    beside, across = peer_of(t, 1), peer_of(t, 2)
    opposite = peer_of(across, 1)
    peers = expert_peers(bits)
    gain_one_row = gain_one[...].reshape(1, -1)
    others = [(lax.rem(e + n, groups), t) for n in range(1, groups)] if bits else []
    greet(others + [(e, beside), (e, across)])

    def remote(src, dst, device, send, recv):
        return pltpu.make_async_remote_copy(
            src_ref=src,
            dst_ref=dst,
            send_sem=send,
            recv_sem=recv,
            device_id=device,
            device_id_type=MESH,
        )

    parts = (
        (up_in, pair_wide, core_wide, chip_wide, 0, grad_up),
        (down_in, pair_tall, core_tall, chip_tall, 0, grad_down),
    )

    def core_copy(w, k):
        src, _, core, _, at, _ = parts[w]
        return remote(
            src.at[(opposite, beside)[k]],
            core.at[2 * at + k],
            (e, beside),
            pair_send.at[w, k],
            pair_recv.at[w, k],
        )

    def own_copy(w, k):
        src, pair, _, _, at, _ = parts[w]
        return pltpu.make_async_copy(
            src.at[(across, t)[k]], pair.at[2 * at + k], copy_sem.at[2 * w + k]
        )

    def chip_copy(w):
        _, pair, _, chip, at, _ = parts[w]
        return remote(
            pair.at[2 * at], chip.at[at], (e, across), pair_send.at[w, 2], pair_recv.at[w, 2]
        )

    sides = side_streams(
        groups, side_wide, side_tall, False, None, None, side_send, side_recv
    )
    side_copies = []
    for n, s in enumerate(sides):
        rows = s.stages[2][1]
        src = wide_in if n < 2 else tall_in
        side_copies.append(
            pltpu.make_async_copy(src.at[rows], s.out.at[rows], copy_sem.at[6 + n])
        )
    if not sides:
        side_copies = [
            pltpu.make_async_copy(wide_in, side_wide, copy_sem.at[6]),
            pltpu.make_async_copy(tall_in, side_tall, copy_sem.at[7]),
        ]
    for copy in side_copies:
        copy.start()
    for k in range(2):
        for w in range(2):
            core_copy(w, k).start()
            own_copy(w, k).start()
    for copy in side_copies:
        copy.wait()
    advance(sides, None, 3)

    streams = []
    if not bits:
        sums = sums_out
    if bits:
        streams = [
            Stream(
                sums,
                sums_out,
                h * 4 * HD,
                4 * HD,
                (0, 1, 2) if h % 2 == 0 else (1, 0, 2),
                landed,
                h * 7 * HD // 2,
                sum_send,
                sum_recv,
                h,
            )
            for h in range(heads - 1)
        ]

    last = (heads - 1) * 4 * HD
    few = 4 * HD // 8

    def part_of(group):
        return pl.ds(pl.multiple_of(last + group * few, 16), few)

    def direct(n, phase, arriving=False):
        group = others[n][0]
        if phase == 0:
            src = sums.at[part_of(group)]
            dst = direct_land.at[group if arriving else e]
        else:
            src = sums_out.at[part_of(e)]
            dst = sums_out.at[part_of(group if arriving else e)]
        return remote(
            src,
            dst,
            others[n],
            direct_send.at[phase, n],
            direct_recv.at[phase, group if arriving else e],
        )

    def direct_begin(phase):
        for n in range(len(others)):
            direct(n, phase).start()

    def direct_end(phase):
        for n in range(len(others)):
            direct(n, phase, True).wait_recv()
        if phase == 0 and bits:
            total = sums[part_of(e), :].astype(F32)
            for group, _ in others:
                total = total + direct_land[group].astype(F32)
            sums_out[part_of(e), :] = total.astype(BF16)

    seg_col = column_of(seg_row[...])
    seg_line = seg_row[...].astype(F32)
    for i in range(4):
        rows = pl.ds(i * block, block)
        inputs = hidden[rows, :].astype(F32)
        scale = lax.rsqrt(jnp.mean(inputs * inputs, axis=-1, keepdims=True) + eps_norm)
        normed[rows, :] = (inputs * scale * gain_one_row).astype(BF16)
        scales[:, rows] = jnp.broadcast_to(scale, (block, 128)).T[0:8, :]
        grad_mixed[rows, :] = mm_nt(grad_residual[rows, :], w_out[...]).astype(BF16)
    grad_out = mm(mixed[...], grad_residual[...]).astype(BF16)
    for h in range(heads):
        sums[pl.ds(h * 4 * HD + 3 * HD, HD), :] = grad_out[h * HD : (h + 1) * HD, :]
    for ref in (grad_query, grad_keys, grad_values):
        ref[...] = jnp.zeros_like(ref)
    swap = swap_halves(lanes)
    small[...] = jnp.concatenate([small_in[...], router_in[...]], axis=0)
    gain_sum = jnp.zeros((1, width), F32)

    for h in range(heads):
        for i in range(4):
            rows = pl.ds(i * block, block)
            reach = (i + 1) * block
            key_at = lax.broadcasted_iota(jnp.int32, (reach, block), 0)
            query_at = lax.broadcasted_iota(jnp.int32, (reach, block), 1) + i * block
            allowed = (seg_col[0:reach, :] == seg_line[:, i * block : (i + 1) * block]) & (
                key_at <= query_at
            )
            q_head = only(query[rows, :] * (HD ** (-0.5)), h)
            g_head = only(grad_mixed[rows, :], h)
            scores = mm_nt(keys[0:reach, :], q_head) - summary[h : h + 1, rows]
            prob = jnp.exp(jnp.where(allowed, scores, -1e30))
            grad_prob = mm_nt(values[0:reach, :], g_head)
            inner = jnp.sum(prob * grad_prob, axis=0, keepdims=True)
            grad_scores = (prob * (grad_prob - inner)).astype(BF16)
            grad_values[0:reach, :] += mm(prob.astype(BF16), g_head)
            grad_keys[0:reach, :] += mm(grad_scores, q_head)
            grad_query[rows, :] += mm_tn(grad_scores, only(keys[0:reach, :], h)) * (HD ** (-0.5))
            if h == 0 and i == 0:
                for w in range(2):
                    _, pair, core, _, at, _ = parts[w]
                    own_copy(w, 0).wait()
                    core_copy(w, 0).wait_recv()
                    pair[2 * at] = (
                        pair[2 * at].astype(F32) + core[2 * at].astype(F32)
                    ).astype(BF16)
                    chip_copy(w).start()
            if h == 2 and i == 2:
                advance(sides, 3, 4)
        for i in range(4):
            rows = pl.ds(i * block, block)
            for n, grad in enumerate((grad_query, grad_keys)):
                value = only(grad[rows, :], h)
                high = value.astype(BF16)
                rest = (value - high.astype(F32)).astype(BF16)
                swapped = mm(high, swap) + mm(rest, swap)
                value = (value * cosine[rows, :] - swapped * sine[rows, :]).astype(BF16)
                turned[n, h, rows, :] = value
            turned[2, h, rows, :] = only(grad_values[rows, :], h).astype(BF16)
        for n, w in enumerate((w_query, w_key, w_value)):
            made = mm_tn(turned[n, h], normed[...])[h * HD : (h + 1) * HD, :]
            gain_sum = gain_sum + jnp.sum(
                made * w[h * HD : (h + 1) * HD, :].astype(F32), axis=0, keepdims=True
            )
            sums[pl.ds(h * 4 * HD + n * HD, HD), :] = made.astype(BF16)
        if h == 1:
            advance(streams[0:1], 0, 1)
        if h < heads - 1:
            advance(streams[h : h + 1], None, 0)
        else:
            direct_begin(0)

    small[2:3, :] = gain_sum / gain_one_row
    valid = jnp.where(seg_row[...] != 0, 1.0, 0.0)
    small[3:4, :] = jnp.broadcast_to(jnp.sum(valid, axis=1, keepdims=True), (1, width))

    def small_copy(k):
        device = peers[k] if k < bits else (e, (beside, across)[k - bits])
        return remote(small, small_land.at[k], device, small_send.at[k], small_recv.at[k])

    def small_next(k):
        if bits:
            if k > 0:
                small_copy(k - 1).wait()
                small[...] += small_land[k - 1]
            if k < 5:
                small_copy(k).start()

    advance(streams[0:1], 1, 2)
    advance(streams[1:2], 0, 1)
    small_next(0)
    for i in range(4):
        rows = pl.ds(i * block, block)
        product[rows, :] = (
            grad_query[rows, :] * query[rows, :].astype(F32)
            + grad_keys[rows, :] * keys[rows, :].astype(F32)
            + grad_values[rows, :] * values[rows, :].astype(F32)
        ).astype(BF16)
    ones = jnp.ones((16, lanes), BF16)
    dots = mm_nt(ones, product[...]).astype(BF16)
    flipped = [w[...].astype(F32).T.astype(BF16) for w in (w_query, w_key, w_value)]
    for n in range(3):
        total = turned[n, 0]
        for h in range(1, heads):
            total = total + turned[n, h]
        turned[n, 0] = total
    for m in range(4):
        rows = slice(m * lanes, (m + 1) * lanes)
        made = sum(mm_nt(flipped[n][rows, :], turned[n, 0]) for n in range(3))
        pay[m, 0:lanes, :] = made.astype(BF16)
        pay[m, lanes : lanes + 16, :] = dots

    def pay_copy(k):
        if k < 2:
            return remote(
                pay.at[(opposite, beside)[k]],
                pay_core.at[k],
                (e, beside),
                pay_send.at[k],
                pay_recv.at[k],
            )
        return remote(pay_out, pay_in, (e, across), pay_send.at[k], pay_recv.at[k])

    pay_copy(0).start()
    pay_copy(1).start()
    place_own = own_columns(lanes, width, t)
    gain_col = jnp.sum(jnp.where(place_own != 0, gain_one_row, 0.0), axis=1, keepdims=True)
    pay_copy(0).wait_recv()
    pay_out[...] = (pay[across].astype(F32) + pay_core[0].astype(F32)).astype(BF16)
    pay_copy(2).start()
    advance(streams[0:1], 2, 3)
    advance(streams[1:2], 1, 2)
    advance(sides, 4, 5)
    small_next(1)
    advance(streams[0:1], 3, 4)
    small_next(2)
    advance(streams[1:2], 2, 3)
    direct_end(0)
    direct_begin(1)
    advance(streams[0:1], 4, 5)
    small_next(3)
    advance(streams[1:2], 3, 4)
    small_next(4)
    for w in range(2):
        _, pair, core, chip, at, result = parts[w]
        own_copy(w, 1).wait()
        core_copy(w, 1).wait_recv()
        chip_copy(w).wait_recv()
        result[...] = (
            pair[2 * at + 1].astype(F32)
            + core[2 * at + 1].astype(F32)
            + chip[at].astype(F32)
        ).astype(BF16)
    small_next(5)
    advance(streams[1:2], 4, 5)
    pay_copy(1).wait_recv()
    pay_copy(2).wait_recv()
    columns = pay[t].astype(F32) + pay_core[1].astype(F32) + pay_in[...].astype(F32)
    scale = scales[0:1, :]
    grad_input[...] = (
        mm_nt(place_own, grad_residual[...])
        + scale * (columns[0:lanes, :] * gain_col)
        - mm_nt(place_own, hidden[...])
        * (scale * scale * (columns[lanes : lanes + 1, :] / width))
    )
    advance(streams[0:1], 5, None)
    advance(sides, 5, None)
    direct_end(1)
    advance(streams[1:2], 5, None)
    for s in sides:
        s.close(range(3, 6))
    for s in streams:
        s.close(range(6))
    for n in range(len(others)):
        direct(n, 0).wait_send()
        direct(n, 1).wait_send()
    for w in range(2):
        for k in range(2):
            core_copy(w, k).wait_send()
        chip_copy(w).wait_send()
    for k in range(3):
        pay_copy(k).wait_send()


def finish(groups, *args):
    hidden, w_query, small_in, router_in, wide_in, tall_in = args[1], args[3], *args[15:19]
    length, width = hidden.shape
    lanes = w_query.shape[0]
    units = tall_in.shape[0]
    smalls = 8 + router_in.shape[0]
    shape = jax.ShapeDtypeStruct
    vmem = pl.BlockSpec(memory_space=pltpu.VMEM)
    hbm = pl.BlockSpec(memory_space=pl.ANY)
    dma = pltpu.SemaphoreType.DMA
    return pl.pallas_call(
        functools.partial(finish_kernel, groups),
        out_shape=(
            shape((lanes, length), F32),
            shape((width, units), BF16),
            shape((units, width), BF16),
            shape(wide_in.shape, BF16),
            shape(tall_in.shape, BF16),
            shape((4 * lanes, width), BF16),
            shape((smalls, width), F32),
        ),
        in_specs=[vmem] * 17 + [hbm] * 4,
        out_specs=(vmem,) * 7,
        scratch_shapes=[
            pltpu.VMEM((length, width), BF16),
            pltpu.VMEM((length, lanes), BF16),
            pltpu.VMEM((length, lanes), F32),
            pltpu.VMEM((length, lanes), F32),
            pltpu.VMEM((length, lanes), F32),
            pltpu.VMEM((3, lanes // HD, length, lanes), BF16),
            pltpu.VMEM((length, lanes), BF16),
            pltpu.VMEM((8, length), F32),
            pltpu.VMEM((2, width, units), BF16),
            pltpu.VMEM((2, units, width), BF16),
            pltpu.VMEM((2, width, units), BF16),
            pltpu.VMEM((2, units, width), BF16),
            pltpu.VMEM((1, width, units), BF16),
            pltpu.VMEM((1, units, width), BF16),
            pltpu.VMEM((4, lanes + 16, length), BF16),
            pltpu.VMEM((2, lanes + 16, length), BF16),
            pltpu.VMEM((lanes + 16, length), BF16),
            pltpu.VMEM((lanes + 16, length), BF16),
            pltpu.VMEM((4 * lanes, width), BF16),
            pltpu.VMEM((7 * lanes // 2, width), BF16),
            pltpu.VMEM((8, HD // 2, width), BF16),
            pltpu.VMEM((5, smalls, width), F32),
            dma((3, 3)),
            dma((3, 3)),
            dma((4, 6)),
            dma((4, 6)),
            dma((3, 6)),
            dma((3, 6)),
            dma((2, 8)),
            dma((2, 8)),
            dma((5,)),
            dma((5,)),
            dma((3,)),
            dma((3,)),
            dma((10,)),
        ],
        compiler_params=pltpu.CompilerParams(
            collective_id=3, has_side_effects=True, vmem_limit_bytes=60 * 2**20
        ),
        name="finish",
    )(*args)


def scale_kernel(numbers, small, *refs):
    tokens, width, members = numbers
    ins, outs = refs[:11], refs[11:]
    count = small[3:4, 0:1] * (1.0 / members)
    factor = 2.0 * tokens / count
    for src, dst in zip(ins, outs):
        dst[...] = src[...].astype(F32) * factor
    attn, ffn, router, loss = outs[11:]
    attn[...] = (small[2:3, :] * factor).reshape(width)
    ffn[...] = (small[1:2, :] * (0.5 * factor)).reshape(width)
    router[...] = small[8:, :] * factor
    loss[...] = jnp.sum(small[0:1, :], axis=1, keepdims=True) * 0.5 / (count * width)


def scale_all(tokens, members, small, grad_input, gate, up, down, wide, tall, sums):
    width = sums.shape[1]
    lanes, length = grad_input.shape
    units = gate.shape[1]
    experts = small.shape[0] - 8
    parts = 6
    row = width // parts
    head = lanes // parts
    shape = jax.ShapeDtypeStruct

    def rows_of(n, offset=0):
        return lambda i: (offset + i, 0)

    def own(n):
        return pl.BlockSpec((head, width), lambda i, n=n: ((i // 2) * 8 + 2 * n + i % 2, 0))

    by_rows = pl.BlockSpec((row, units), lambda i: (i, 0))
    by_cols = pl.BlockSpec((units, row), lambda i: (0, i))
    in_specs = [
        pl.BlockSpec(small.shape, lambda i: (0, 0)),
        pl.BlockSpec((head, length), lambda i: (i, 0)),
        by_rows,
        by_rows,
        by_cols,
        pl.BlockSpec((row, units), lambda i: (i, 0)),
        pl.BlockSpec((row, units), lambda i: (parts + i, 0)),
        by_cols,
        own(0),
        own(1),
        own(2),
        own(3),
    ]
    own_out = pl.BlockSpec((head, width), lambda i: (i, 0))

    def whole(rows, cols):
        return pl.BlockSpec((rows, cols), lambda i: (0, 0))

    out_specs = [
        pl.BlockSpec((head, length), lambda i: (i, 0)),
        by_rows,
        by_rows,
        by_cols,
        by_rows,
        by_rows,
        by_cols,
        *([own_out] * 4),
        pl.BlockSpec((width,), lambda i: (0,)),
        pl.BlockSpec((width,), lambda i: (0,)),
        whole(experts, width),
        whole(1, 1),
    ]
    wide_shape, tall_shape = shape((width, units), F32), shape((units, width), F32)
    return pl.pallas_call(
        functools.partial(scale_kernel, (tokens, width, members)),
        grid=(parts,),
        out_shape=[
            shape((lanes, length), F32),
            wide_shape,
            wide_shape,
            tall_shape,
            wide_shape,
            wide_shape,
            tall_shape,
            *([shape((lanes, width), F32)] * 4),
            shape((width,), F32),
            shape((width,), F32),
            shape((experts, width), F32),
            shape((1, 1), F32),
        ],
        in_specs=in_specs,
        out_specs=out_specs,
        name="scale",
    )(small, grad_input, gate, up, down, wide, wide, tall, sums, sums, sums, sums)


def body(
    hidden_in,
    norm_attn,
    w_query,
    w_key,
    w_value,
    w_out,
    norm_ffn,
    w_router,
    shared_gate,
    shared_up,
    shared_down,
    expert_gate,
    expert_up,
    expert_down,
    segment,
    routes,
    slots,
    teacher,
):
    length, width = hidden_in.shape
    groups = lax.axis_size("expert")
    members = lax.axis_size("tensor")
    capacity = 3 * length // groups
    lanes = w_query.shape[1]
    tables = rope_rows(length, lanes // HD)
    seg_row = segment[None]
    gain_one, gain_two = norm_attn, norm_ffn
    query, keys, values, summary, residual, normed_two, mixed = attend(
        hidden_in,
        gain_one,
        w_query.T,
        w_key.T,
        w_value.T,
        w_out,
        gain_two,
        tables,
        seg_row,
    )
    activations, grad_residual, wide, tall, gate, up_parts, down_parts, small, router = moe(
        groups,
        capacity,
        normed_two,
        residual,
        teacher.T,
        seg_row,
        routes.T,
        slots.T,
        w_router.T,
        gain_two,
        shared_gate,
        shared_up,
        shared_down,
        expert_gate[0],
        expert_up[0],
        expert_down[0],
    )
    grad_input, up, down, wide, tall, sums, small = finish(
        groups,
        grad_residual,
        hidden_in,
        gain_one,
        w_query.T,
        w_key.T,
        w_value.T,
        w_out,
        query,
        keys,
        values,
        summary,
        mixed,
        *tables,
        seg_row,
        small,
        router,
        wide,
        tall,
        up_parts,
        down_parts,
    )
    if groups != 8:
        wide, tall, sums = lax.psum((wide, tall, sums), "expert")
        small = lax.psum(small, ("expert", "tensor"))
    (
        grad_input,
        gate,
        up,
        down,
        side_gate,
        side_up,
        side_down,
        grad_query,
        grad_key,
        grad_value,
        grad_out,
        grad_norm_attn,
        grad_norm_ffn,
        grad_router,
        loss,
    ) = scale_all(
        length * groups, members, small, grad_input, gate, up, down, wide, tall, sums
    )
    return (
        loss[0, 0],
        activations.T,
        grad_input.T,
        grad_norm_attn,
        grad_query.T,
        grad_key.T,
        grad_value.T,
        grad_out,
        grad_norm_ffn,
        grad_router.T,
        side_gate,
        side_up,
        side_down,
        gate[None],
        up[None],
        down[None],
    )


def solution(mesh):
    placed = (
        P("expert", None),
        P(),
        P(None, "tensor"),
        P(None, "tensor"),
        P(None, "tensor"),
        P("tensor", None),
        P(),
        P(),
        P(None, "tensor"),
        P(None, "tensor"),
        P("tensor", None),
        P("expert", None, "tensor"),
        P("expert", None, "tensor"),
        P("expert", "tensor", None),
        P("expert"),
        P("expert", None),
        P("expert", None),
        P("expert", "tensor"),
    )
    return jax.shard_map(
        body,
        mesh=mesh,
        in_specs=placed,
        out_specs=(
            P(),
            P("expert", "tensor"),
            P("expert", "tensor"),
            P(),
            P(None, "tensor"),
            P(None, "tensor"),
            P(None, "tensor"),
            P("tensor", None),
            P(),
            P(),
            P(None, "tensor"),
            P(None, "tensor"),
            P("tensor", None),
            P("expert", None, "tensor"),
            P("expert", None, "tensor"),
            P("expert", "tensor", None),
        ),
        check_vma=False,
    )
```

```python
import functools

import jax
import jax.numpy as jnp
import numpy as np
from jax import lax
from jax.experimental import pallas as pl
from jax.experimental.pallas import tpu as pltpu
from jax.sharding import PartitionSpec as P

HD = 64
WIDE = 256
F32, BF16 = jnp.float32, jnp.bfloat16
MESH = pl.DeviceIdType.MESH


eps_norm = 1e-06


def rope_rows(length, heads):
    half = HD // 2
    freqs = (10000.0 ** (-2.0 * np.arange(half) / HD)).astype(np.float32)
    angles = np.arange(length, dtype=np.float32)[:, None] * freqs[None, :]
    cosine, sine = np.cos(angles), np.sin(angles)
    table = np.zeros((length, 2 * WIDE), np.float32)
    table[:, : heads * HD] = np.tile(np.concatenate([cosine, cosine], axis=1), (1, heads))
    table[:, WIDE : WIDE + heads * HD] = np.tile(np.concatenate([-sine, sine], axis=1), (1, heads))
    return table


def peer_of(t, step):
    if step == 1:
        return t + 1 - 2 * lax.rem(t, 2)
    return lax.rem(t + 2, 4)


def greet(peers):
    barrier = pltpu.get_barrier_semaphore()
    for peer in peers:
        pl.semaphore_signal(barrier, inc=1, device_id=peer, device_id_type=MESH)
    pl.semaphore_wait(barrier, len(peers))


def mm(a, b):
    return lax.dot_general(a, b, (((1,), (0,)), ((), ())), preferred_element_type=F32)


def mm_nt(a, b):
    return lax.dot_general(a, b, (((1,), (1,)), ((), ())), preferred_element_type=F32)


def mm_tn(a, b):
    return lax.dot_general(a, b, (((0,), (0,)), ((), ())), preferred_element_type=F32)


def swap_halves(width):
    row = lax.broadcasted_iota(jnp.int32, (width, width), 0)
    col = lax.broadcasted_iota(jnp.int32, (width, width), 1)
    half = HD // 2
    other = jnp.where(lax.rem(col, HD) < half, col + half, col - half)
    return (row == other).astype(F32).astype(BF16)


def head_mask(rows, width, head):
    col = lax.broadcasted_iota(jnp.int32, (rows, width), 1)
    return (col >= head * HD) & (col < (head + 1) * HD)


def only(value, head):
    keep = head_mask(value.shape[0], value.shape[1], head)
    return jnp.where(keep, value, jnp.zeros_like(value))


def column_of(row):
    wide = jnp.broadcast_to(row.astype(F32), (128, row.shape[1]))
    return wide.T[:, 0:1]


def own_columns(lanes, width, t):
    row = lax.broadcasted_iota(jnp.int32, (lanes, width), 0)
    col = lax.broadcasted_iota(jnp.int32, (lanes, width), 1)
    return (col == row + t * lanes).astype(F32).astype(BF16)


class Stream:
    def __init__(self, buf, out, base, size, order, land, land_at, send, recv, index):
        self.buf, self.out, self.land, self.index = buf, out, land, index
        self.send, self.recv = send, recv
        e, self.t = lax.axis_index("expert"), lax.axis_index("tensor")
        self.stages, start = [], base
        for k, b in enumerate(order):
            half = size >> min(k + 1, 2)
            bit = lax.rem(e // 2**b, 2)
            peer = e + 2**b - 2 * 2**b * bit
            if k == 2:
                bit = give = keep = None
                keep = give = self.stages[1][1]
            else:
                keep = pl.ds(pl.multiple_of(start + bit * half, 16), half)
                give = pl.ds(pl.multiple_of(start + (1 - bit) * half, 16), half)
                start = start + bit * half
            self.stages.append((peer, keep, give, pl.ds(land_at, half)))
            land_at += half

    def copy(self, step, arriving=False):
        peer, keep, give, land = self.stages[step if step < 3 else 4 - step]
        if step < 3:
            src, dst = self.buf.at[give], self.land.at[land]
        else:
            src, dst = self.out.at[keep], self.out.at[give if arriving else keep]
        return pltpu.make_async_remote_copy(
            src_ref=src,
            dst_ref=dst,
            send_sem=self.send.at[self.index, step],
            recv_sem=self.recv.at[self.index, step],
            device_id=(peer, self.t),
            device_id_type=MESH,
        )

    def begin(self, step):
        self.copy(step).start()

    def end(self, step):
        self.copy(step, True).wait_recv()
        if step < 3:
            _, keep, _, land = self.stages[step]
            total = self.buf[keep, :].astype(F32) + self.land[land, :].astype(F32)
            if step == 2:
                self.copy(2).wait_send()
            if step == 2 and self.out is not None:
                self.out[keep, :] = total.astype(BF16)
            else:
                self.buf[keep, :] = total.astype(BF16)

    def close(self, steps):
        for step in steps:
            if step != 2:
                self.copy(step).wait_send()


def advance(streams, last, first):
    for s in streams:
        if last is not None:
            s.end(last)
        if first is not None:
            s.begin(first)


def expert_peers(bits):
    e, t = lax.axis_index("expert"), lax.axis_index("tensor")
    return [(e + 2**b - 2 * 2**b * lax.rem(e // 2**b, 2), t) for b in range(bits)]


def each(count, do):
    if count <= 8:
        for i in range(count):
            do(i)
    else:
        lax.fori_loop(0, count, lambda i, none: (do(i), none)[1], 0)


def steps(count, do):
    lax.fori_loop(0, count, lambda i, none: (do(i), none)[1], 0)


def side_streams(groups, wide, tall, halving, wide_land, tall_land, send, recv):
    if groups != 8:
        return []
    rows, few = wide.shape[0] // 2, tall.shape[0] // 2
    wides = (wide, None) if halving else (None, wide)
    talls = (tall, None) if halving else (None, tall)
    return [
        Stream(*wides, 0, rows, (0, 1, 2), wide_land, 0, send, recv, 0),
        Stream(*wides, rows, rows, (1, 0, 2), wide_land, rows, send, recv, 1),
        Stream(*talls, 0, few, (0, 1, 2), tall_land, 0, send, recv, 2),
        Stream(*talls, few, few, (1, 0, 2), tall_land, few, send, recv, 3),
    ]


def moe_kernel(
    groups,
    share,
    pad,
    hidden_in,
    table,
    gain_one,
    query_in,
    key_in,
    value_in,
    w_out,
    teacher_in,
    seg_row,
    routes,
    slots,
    router,
    gain,
    shared_gate_in,
    shared_up_in,
    shared_down_in,
    gate_in,
    up_in,
    down_in,
    query_out,
    mixed_out,
    summary,
    activations,
    grad_residual,
    side_wide,
    side_tall,
    grad_gate,
    grad_up,
    grad_down,
    small,
    grad_router,
    w_query,
    w_key,
    w_value,
    teacher,
    shared_gate,
    shared_up,
    shared_down,
    normed,
    gate_all,
    up_all,
    down_all,
    pick,
    weigh,
    out_buf,
    back_buf,
    rows_in,
    returned,
    grad_rows,
    act,
    slope,
    hidden,
    side_act,
    side_slope,
    side_hidden,
    residual_half,
    off,
    part,
    error,
    wide_land,
    tall_land,
    half_out,
    half_in,
    chip_out,
    chip_in,
    a2a_send,
    a2a_recv,
    sum_send,
    sum_recv,
    gather_send,
    gather_recv,
    mixed_send,
    mixed_recv,
    out_send,
    out_recv,
    side_send,
    side_recv,
    input_sem,
    pair_send,
    pair_recv,
    free_sem,
    copy_sem,
):
    length, width = normed.shape
    lanes = teacher.shape[0]
    heads = lanes // HD
    units = shared_gate.shape[1]
    experts = router.shape[0]
    rows = groups * pad
    half_groups, half_rows = groups // 2, rows // 2
    chunk = length // 4
    e, t = lax.axis_index("expert"), lax.axis_index("tensor")
    beside, across = peer_of(t, 1), peer_of(t, 2)
    opposite = peer_of(across, 1)
    gain_row = gain[...].reshape(1, -1)
    gain_one_row = gain_one[...].reshape(1, -1)
    greet(
        [(lax.rem(e + j, groups), t) for j in range(1, groups)] + [(e, beside), (e, across)]
    )

    def remote(src, dst, device, send, recv):
        return pltpu.make_async_remote_copy(
            src_ref=src,
            dst_ref=dst,
            send_sem=send,
            recv_sem=recv,
            device_id=device,
            device_id_type=MESH,
        )

    above, below = pl.ds(0, width // 2), pl.ds(width // 2, width // 2)
    gathers = (
        (gate_in.at[above], lambda m: gate_all.at[m, above]),
        (gate_in.at[below], lambda m: gate_all.at[m, below]),
        (up_in, lambda m: up_all.at[m]),
        (down_in, lambda m: down_all.at[m]),
    )

    def gather(w, k):
        src, slot_of = gathers[w]
        slot = t if k < 2 else across
        return remote(
            src if k < 2 else slot_of(slot),
            slot_of(slot),
            (e, across if k == 0 else beside),
            gather_send.at[w, k],
            gather_recv.at[w, k],
        )

    def own_weights(w):
        src, dst = ((gate_in, gate_all), (up_in, up_all), (down_in, down_all))[w]
        return pltpu.make_async_copy(src, dst.at[t], copy_sem.at[w])

    block = length // 4

    def out_rows(m):
        return hidden.at[pl.ds(pl.multiple_of(m * lanes, HD), lanes), pl.ds(0, width)]

    def mixed_block(m, i):
        return act.at[pl.ds(pl.multiple_of(m * lanes, HD), lanes), pl.ds(i * block, block)]

    def out_copy(k):
        rows = out_rows(t if k < 2 else across)
        return remote(
            w_out if k < 2 else rows,
            rows,
            (e, across if k == 0 else beside),
            out_send.at[k],
            out_recv.at[k],
        )

    def piece_of(i, k):
        ref = mixed_block(t if k < 2 else across, i)
        return remote(
            ref,
            ref,
            (e, across if k == 0 else beside),
            mixed_send.at[i, k],
            mixed_recv.at[i, k],
        )

    for k in range(2):
        out_copy(k).start()
    gather(0, 0).start()
    loads = [
        pltpu.make_async_copy(src, dst, input_sem.at[n])
        for n, (src, dst) in enumerate(
            (
                (query_in, w_query),
                (key_in, w_key),
                (value_in, w_value),
                (w_out, out_rows(t)),
                (teacher_in, teacher),
                (shared_gate_in, shared_gate),
                (shared_up_in, shared_up),
                (shared_down_in, shared_down),
            )
        )
    ]
    inputs_copy = pltpu.make_async_copy(hidden_in, off, copy_sem.at[11])
    inputs_copy.start()
    for load in loads[:4]:
        load.start()
    table_copy = pltpu.make_async_copy(table, part.at[:, pl.ds(0, 2 * WIDE)], copy_sem.at[12])
    table_copy.start()
    for w in range(4):
        gather(w, 1).start()
    for w in range(3):
        own_weights(w).start()
    for load in loads[4:]:
        load.start()
    for load in loads[:4]:
        load.wait()
    core = lax.rem(t, 2)
    seg_col = column_of(seg_row[...])
    seg_line = seg_row[...].astype(F32)
    swap = swap_halves(lanes)
    turns = [mm(swap, w[...]).astype(BF16) for w in (w_query, w_key)]
    columns = [pl.ds(n * WIDE, lanes) for n in range(3)]
    turned = pl.ds(0, lanes)
    inputs_copy.wait()
    table_copy.wait()

    def make(i):
        rows = pl.ds(i * block, block)
        inputs = off[rows, :].astype(F32)
        scale = lax.rsqrt(jnp.mean(inputs * inputs, axis=-1, keepdims=True) + eps_norm)
        value = (inputs * scale * gain_one_row).astype(BF16)
        error[rows, columns[2]] = mm_nt(value, w_value[...]).astype(BF16)
        slope[turned, rows] = mm_nt(w_value[...], value).astype(BF16)
        for n, (w, turn) in enumerate(zip((w_query, w_key), turns)):
            error[rows, columns[n]] = (
                mm_nt(value, w[...]) * part[rows, columns[0]]
                + mm_nt(value, turn) * part[rows, columns[1]]
            ).astype(BF16)

    def project(i):
        rows = pl.ds(i * block, block)
        piece_of(i, 1).wait_recv()
        piece_of(i, 2).wait_recv()
        total = off[rows, :].astype(F32)
        for m in range(4):
            total = total + mm_tn(mixed_block(m, i)[...], out_rows(m)[...])
        scale = lax.rsqrt(jnp.mean(total * total, axis=-1, keepdims=True) + eps_norm)
        normed[rows, :] = (total * scale * gain_row).astype(BF16)

        @pl.when(core == i // 2)
        def keep():
            residual_half[pl.ds((i % 2) * block, block), :] = total

    for i in range(4):
        make(i)
        tokens = pl.ds(i * block, block)
        reach = (i + 1) * block
        key_at = lax.broadcasted_iota(jnp.int32, (reach, block), 0)
        query_at = lax.broadcasted_iota(jnp.int32, (reach, block), 1) + i * block
        allowed = (seg_col[0:reach, :] == seg_line[:, i * block : (i + 1) * block]) & (
            key_at <= query_at
        )
        q_block = error[tokens, columns[0]] * (HD ** (-0.5))
        made = []
        for h in range(heads):
            scores = mm_nt(error[0:reach, columns[1]], only(q_block, h))
            scores = jnp.where(allowed, scores, -1e30)
            top = jnp.max(scores, axis=0, keepdims=True)
            expo = jnp.exp(scores - top)
            whole = jnp.sum(expo, axis=0, keepdims=True)
            prob = (expo * (1.0 / whole)).astype(BF16)
            made.append(mm(slope[h * HD : (h + 1) * HD, 0:reach], prob).astype(BF16))
            summary[h : h + 1, tokens] = top + jnp.log(whole)
        mixed_block(t, i)[...] = jnp.concatenate(made, axis=0)
        piece_of(i, 0).start()
        piece_of(i, 1).start()
        if i == 0:
            out_copy(0).wait_recv()
            out_copy(2).start()
        else:
            piece_of(i - 1, 0).wait_recv()
            piece_of(i - 1, 2).start()
        if i == 1:
            out_copy(1).wait_recv()
            out_copy(2).wait_recv()
        if i >= 2:
            project(i - 2)
    for w in range(1, 4):
        gather(w, 0).start()
    query_copy = pltpu.make_async_copy(error, query_out, copy_sem.at[13])
    query_copy.start()
    piece_of(3, 0).wait_recv()
    piece_of(3, 2).start()
    mixed_copy = pltpu.make_async_copy(
        act.at[pl.ds(pl.multiple_of(t * lanes, HD), lanes), pl.ds(0, length)],
        mixed_out,
        copy_sem.at[14],
    )
    mixed_copy.start()
    project(2)
    project(3)

    far_half = 1 - e // half_groups
    near_half = e // half_groups

    def block_at(group):
        return pl.ds(pl.multiple_of(group * pad, 16), pad)

    def half_at(half):
        return pl.ds(pl.multiple_of(half * half_rows, 16), half_rows)

    def exchange(phase, sent, landed, group):
        return remote(
            sent.at[block_at(group)],
            landed.at[block_at(e)],
            (group, t),
            a2a_send.at[phase, group],
            a2a_recv.at[phase, e],
        )

    def arrival(phase, sent, landed, group):
        return remote(
            sent.at[block_at(group)],
            landed.at[block_at(group)],
            (group, t),
            a2a_send.at[phase, group],
            a2a_recv.at[phase, group],
        )

    def near_group(j):
        return near_half * half_groups + lax.rem(e + j, half_groups)

    def far_group(j):
        return far_half * half_groups + lax.rem(e + j, half_groups)

    def send_far(phase, sent, landed):
        each(half_groups, lambda j: exchange(phase, sent, landed, far_group(j)).start())

    def send_near(phase, sent, landed):
        each(half_groups - 1, lambda j: exchange(phase, sent, landed, near_group(j + 1)).start())
        landed[block_at(e), :] = sent[block_at(e), :]

    def await_far(phase, sent, landed):
        each(half_groups, lambda j: arrival(phase, sent, landed, far_group(j)).wait_recv())

    def await_near(phase, sent, landed):
        each(half_groups - 1, lambda j: arrival(phase, sent, landed, near_group(j + 1)).wait_recv())

    def await_sent(phase, sent, landed):
        each(half_groups, lambda j: exchange(phase, sent, landed, far_group(j)).wait_send())
        each(half_groups - 1, lambda j: exchange(phase, sent, landed, near_group(j + 1)).wait_send())

    low = t * share
    mine = (slots[...] >= low) & (slots[...] < low + share)
    place = jnp.where(mine, routes[...] * pad + slots[...] - low, -1)
    place_one, place_two = place[0:1, :], place[1:2, :]
    build = rows // 8

    def pick_rows(i):
        at = lax.broadcasted_iota(jnp.int32, (build, length), 0) + i * build
        hit = (at == place_one) | (at == place_two)
        block = pl.ds(pl.multiple_of(i * build, 16), build)
        pick[block, :] = jnp.where(hit, 1.0, 0.0).astype(BF16)

    for half, send in ((far_half, send_far), (near_half, send_near)):
        steps(4, lambda i, half=half: pick_rows(half * 4 + i))
        out_buf[half_at(half), :] = mm(pick[half_at(half), :], normed[...]).astype(BF16)
        send(0, out_buf, rows_in)

    logits = mm_nt(router[...], normed[...])
    named = lax.broadcasted_iota(jnp.int32, (experts, length), 0)
    here = [named == routes[k : k + 1, :] for k in range(2)]
    chosen = [jnp.sum(jnp.where(h, logits, 0.0), axis=0, keepdims=True) for h in here]
    top = jnp.maximum(chosen[0], chosen[1])
    raised = [jnp.exp(c - top) for c in chosen]
    total = raised[0] + raised[1]
    gate_one, gate_two = raised[0] / total, raised[1] / total

    def weigh_rows(i):
        at = lax.broadcasted_iota(jnp.int32, (build, length), 0) + i * build
        value = jnp.where(at == place_one, gate_one, jnp.where(at == place_two, gate_two, 0.0))
        weigh[pl.ds(pl.multiple_of(i * build, 16), build), :] = value.astype(BF16)

    steps(8, weigh_rows)

    def tokens_at(i):
        return pl.ds(pl.multiple_of(i * chunk, chunk), chunk)

    def silu_parts(pre, lin):
        sigma = 1.0 / (1.0 + jnp.exp(-pre))
        active = pre * sigma
        return active, lin * (sigma * (1.0 + pre * (1.0 - sigma))), active * lin

    def shared_forward(i):
        at = tokens_at(i)
        a, s, h = silu_parts(mm(normed[at, :], shared_gate[...]), mm(normed[at, :], shared_up[...]))
        side_act[at, :] = a.astype(BF16)
        side_slope[at, :] = s.astype(BF16)
        side_hidden[at, :] = h.astype(BF16)
        part[at, :] = mm(side_hidden[at, :], shared_down[...]) - mm_tn(teacher[:, at], place_own)

    place_own = own_columns(lanes, width, t)
    for load in loads[4:]:
        load.wait()
    steps(4, shared_forward)
    for w in range(3):
        own_weights(w).wait()
    for w in range(4):
        gather(w, 1).wait_recv()
    mixed_copy.wait()
    for k in range(3):
        out_copy(k).wait_send()
        for i in range(4):
            piece_of(i, k).wait_send()

    def units_of(m):
        return pl.ds(pl.multiple_of(m * units, units), units)

    def expert_units(half, m):
        at, cols = half_at(half), units_of(m)
        a, s, h = silu_parts(mm(rows_in[at, :], gate_all[m]), mm(rows_in[at, :], up_all[m]))
        act[at, cols] = a.astype(BF16)
        slope[at, cols] = s.astype(BF16)
        hidden[at, cols] = h.astype(BF16)

    await_far(0, out_buf, rows_in)
    for m in (t, beside):
        expert_units(far_half, m)
    await_near(0, out_buf, rows_in)
    for m in (t, beside):
        expert_units(near_half, m)
    for w in range(3):
        gather(w, 0).wait_recv()
        gather(w, 2).start()
    for half in (far_half, near_half):
        expert_units(half, across)
    for w in range(3):
        gather(w, 2).wait_recv()
    for half in (far_half, near_half):
        expert_units(half, opposite)
    gather(3, 0).wait_recv()
    gather(3, 2).start()
    gather(3, 2).wait_recv()
    for half, send in ((far_half, send_far), (near_half, send_near)):
        at = half_at(half)
        made = sum(mm(hidden[at, pl.ds(m * units, units)], down_all[m]) for m in range(4))
        back_buf[at, :] = made.astype(BF16)
        send(1, back_buf, returned)

    span = length // 8

    def tokens_of(which, q):
        return pl.ds(pl.multiple_of(which * (length // 2) + q * span, span), span)

    def piece(q):
        return pl.ds(q * span, span)

    def halves(turn, q):
        return remote(
            half_out.at[piece(q)],
            half_in.at[turn, piece(q)],
            (e, beside),
            sum_send.at[turn, 0, q],
            sum_recv.at[turn, 0, q],
        )

    def chips(turn, q):
        return remote(
            chip_out.at[piece(q)],
            chip_in.at[turn, piece(q)],
            (e, across),
            sum_send.at[turn, 1, q],
            sum_recv.at[turn, 1, q],
        )

    def spread(turn, which, q):
        return remote(
            off.at[tokens_of(which, q)],
            off.at[tokens_of(which, q)],
            (e, beside),
            sum_send.at[turn, 2, q],
            sum_recv.at[turn, 2, q],
        )

    def combine(matrix, landed, at, tokens):
        part[tokens, :] += mm_tn(matrix[at, tokens], landed[at, :])

    def sum_over_tensor(turn, matrix, phase, finish, then, idle):
        await_near(phase, back_buf, returned)
        steps(4, lambda i: combine(matrix, returned, half_at(near_half), tokens_at(i)))
        await_far(phase, back_buf, returned)
        last = half_at(far_half)
        then()

        def to_chip(q):
            halves(turn, q).wait_recv()
            chip_out[piece(q), :] = (
                part[tokens_of(core, q), :] + half_in[turn, piece(q), :].astype(F32)
            ).astype(BF16)
            chips(turn, q).start()

        for q in range(4):
            at = tokens_of(1 - core, q)
            combine(matrix, returned, last, at)
            half_out[piece(q), :] = part[at, :].astype(BF16)
            halves(turn, q).start()
            combine(matrix, returned, last, tokens_of(core, q))
            to_chip(q)
        idle()
        for q in range(4):
            chips(turn, q).wait_recv()
            finish(
                q,
                tokens_of(core, q),
                chip_out[piece(q), :].astype(F32) + chip_in[turn, piece(q), :].astype(F32),
            )
            spread(turn, core, q).start()
        for q in range(4):
            spread(turn, 1 - core, q).wait_recv()
        for q in range(4):
            halves(turn, q).wait_send()
            chips(turn, q).wait_send()
            spread(turn, core, q).wait_send()

    query_copy.wait()
    seen = seg_col != 0.0
    small[...] = jnp.zeros_like(small)
    half_seen = column_of(
        jnp.where(core == 0, seg_row[:, 0 : length // 2], seg_row[:, length // 2 : length])
    )

    def finish_forward(q, at, value):
        value = residual_half[piece(q), :] + value
        off[at, :] = value.astype(BF16)
        value = jnp.where(half_seen[q * span : (q + 1) * span, :] != 0.0, value, 0.0)
        small[0:1, :] += jnp.sum(value * value, axis=0, keepdims=True)

    sum_over_tensor(0, weigh, 1, finish_forward, lambda: None, lambda: None)
    for i in range(4):
        at = slice(i * chunk, (i + 1) * chunk)
        error[at, :] = jnp.where(seen[at, :], off[at, :].astype(F32), 0.0).astype(BF16)

    await_sent(0, out_buf, rows_in)
    for half, send in ((far_half, send_far), (near_half, send_near)):
        at = half_at(half)
        pair = mm(weigh[at, :], error[...])
        out_buf[at, :] = pair.astype(BF16)
        dots = jnp.sum(pair * returned[at, :].astype(F32), axis=1, keepdims=True)
        part[at, 0:128] = jnp.broadcast_to(dots, (half_rows, 128))
        send(2, out_buf, grad_rows)
    pl.semaphore_signal(free_sem.at[0], inc=1, device_id=(e, beside), device_id_type=MESH)
    activations[...] = (mm_nt(place_own, off[...]) + teacher[...].astype(F32)).astype(BF16)

    def take_dots(i, sums):
        block = pl.ds(pl.multiple_of(i * build, 16), build)
        at = lax.broadcasted_iota(jnp.int32, (build, length), 0) + i * build
        dots = part[block, 0:1]
        return tuple(
            s + jnp.sum(jnp.where(at == p, dots, 0.0), axis=0, keepdims=True)
            for s, p in zip(sums, (place_one, place_two))
        )

    zero = jnp.zeros((1, length), F32)
    dot_one, dot_two = lax.fori_loop(0, 8, take_dots, (zero, zero))

    def shared_backward(i):
        at = tokens_at(i)
        hid_grad = mm_nt(error[at, :], shared_down[...])
        side_slope[at, :] = (hid_grad * side_slope[at, :].astype(F32)).astype(BF16)
        side_act[at, :] = (hid_grad * side_act[at, :].astype(F32)).astype(BF16)
        part[at, :] = mm_nt(side_slope[at, :], shared_gate[...]) + mm_nt(
            side_act[at, :], shared_up[...]
        )

    def expert_backward(at):
        for m in range(4):
            cols = pl.ds(m * units, units)
            hid_grad = mm_nt(grad_rows[at, :], down_all[m])
            slope[at, cols] = (hid_grad * slope[at, cols].astype(F32)).astype(BF16)
            act[at, cols] = (hid_grad * act[at, cols].astype(F32)).astype(BF16)
        made = sum(
            mm_nt(slope[at, pl.ds(m * units, units)], gate_all[m])
            + mm_nt(act[at, pl.ds(m * units, units)], up_all[m])
            for m in range(4)
        )
        back_buf[at, :] = made.astype(BF16)

    def half_backward(half, wait, send):
        wait(2, out_buf, grad_rows)
        expert_backward(half_at(half))
        send(3, back_buf, returned)

    steps(4, shared_backward)
    await_sent(1, back_buf, returned)
    side_wide[0:width, :] = mm_tn(normed[...], side_slope[...]).astype(BF16)
    side_wide[width : 2 * width, :] = mm_tn(normed[...], side_act[...]).astype(BF16)
    side_tall[...] = mm_tn(side_hidden[...], error[...]).astype(BF16)
    sides = side_streams(
        groups, side_wide, side_tall, True, wide_land, tall_land, side_send, side_recv
    )
    advance(sides, None, 0)
    both = dot_one + dot_two
    grad_logits = (
        jnp.where(here[0], dot_one - gate_one * both, 0.0)
        + jnp.where(here[1], dot_two - gate_two * both, 0.0)
    ).astype(BF16)
    grad_router[...] = mm(grad_logits, normed[...])
    part[...] += mm_tn(grad_logits, router[...])
    half_backward(far_half, await_far, send_far)
    half_backward(near_half, await_near, send_near)

    advance(sides, 0, 1)
    for w in range(4):
        for k in range(3):
            gather(w, k).wait_send()
    await_sent(2, out_buf, grad_rows)
    pl.semaphore_signal(free_sem.at[1], inc=1, device_id=(e, across), device_id_type=MESH)
    for m in range(4):
        cols = pl.ds(m * units, units)
        gate_all[m] = mm_tn(rows_in[...], slope[:, cols]).astype(BF16)

    def gate_core(n):
        return remote(
            gate_all.at[(opposite, beside)[n]],
            weigh.at[pl.ds(0, width), pl.ds(n * units, units)],
            (e, beside),
            pair_send.at[n],
            pair_recv.at[n],
        )

    gate_chip = remote(
        gate_all.at[across],
        out_buf.at[pl.ds(0, width), pl.ds(0, units)],
        (e, across),
        pair_send.at[2],
        pair_recv.at[2],
    )
    pl.semaphore_wait(free_sem.at[0], 1)
    gate_core(0).start()
    gate_core(1).start()
    for m in range(4):
        up_all[m] = mm_tn(rows_in[...], act[:, pl.ds(m * units, units)]).astype(BF16)
        if m == 0:
            gate_core(0).wait_recv()
            gate_all[across] = (
                gate_all[across].astype(F32) + weigh[0:width, 0:units].astype(F32)
            ).astype(BF16)
            pl.semaphore_wait(free_sem.at[1], 1)
            gate_chip.start()
    for m in range(4):
        down_all[m] = mm_tn(hidden[:, pl.ds(m * units, units)], grad_rows[...]).astype(BF16)
    pl.semaphore_signal(free_sem.at[2], inc=1, device_id=(e, beside), device_id_type=MESH)

    def up_land(n):
        return act.at[pl.ds(0, width), pl.ds(n * units, units)]

    def down_land(n):
        return hidden.at[pl.ds(0, units), pl.ds(n * width, width)]

    def pair_core(w, n):
        slot = (opposite, beside)[n]
        return remote(
            (up_all, down_all)[w].at[slot],
            (up_land, down_land)[w](n),
            (e, beside),
            pair_send.at[3 + 2 * w + n],
            pair_recv.at[3 + 2 * w + n],
        )

    pl.semaphore_wait(free_sem.at[2], 1)
    for w in range(2):
        for n in range(2):
            pair_core(w, n).start()
    outs = []

    def add_pairs():
        for n, m in enumerate((across, t)):
            for w, (own, dst) in enumerate(((up_all, grad_up), (down_all, grad_down))):
                pair_core(w, n).wait_recv()
                own[m] = (own[m].astype(F32) + (up_land, down_land)[w](n)[...].astype(F32)).astype(
                    BF16
                )
                out = pltpu.make_async_copy(own.at[m], dst.at[n], copy_sem.at[3 + 2 * n + w])
                out.start()
                outs.append(out)

    def finish_backward(q, at, value):
        inputs = residual_half[piece(q), :]
        scale = lax.rsqrt(jnp.mean(inputs * inputs, axis=-1, keepdims=True) + eps_norm)
        scaled = value * gain_row
        inner = jnp.mean(scaled * inputs, axis=-1, keepdims=True)
        through = scale * scaled - inputs * (scale * scale * scale * inner)
        off[at, :] = (error[at, :].astype(F32) + through).astype(BF16)
        small[1:2, :] += jnp.sum(value * inputs * scale, axis=0, keepdims=True)

    sum_over_tensor(1, pick, 3, finish_backward, lambda: advance(sides, 1, 2), add_pairs)
    residual_copy = pltpu.make_async_copy(off, grad_residual, copy_sem.at[11])
    residual_copy.start()
    await_sent(3, back_buf, returned)
    advance(sides, 2, None)
    for s in sides:
        s.close(range(3))
    residual_copy.wait()
    for out in outs:
        out.wait()
    gate_core(1).wait_recv()
    gate_chip.wait()
    grad_gate[...] = (
        gate_all[t].astype(F32)
        + weigh[0:width, units : 2 * units].astype(F32)
        + out_buf[0:width, 0:units].astype(F32)
    ).astype(BF16)
    for n in range(2):
        gate_core(n).wait_send()
        for w in range(2):
            pair_core(w, n).wait_send()


def moe(
    groups,
    capacity,
    hidden_in,
    table,
    gain_one,
    w_query,
    w_key,
    w_value,
    w_out,
    teacher,
    seg_row,
    routes,
    slots,
    router,
    gain,
    shared_gate,
    shared_up,
    shared_down,
    gate_in,
    up_in,
    down_in,
):
    length, width = hidden_in.shape
    lanes = teacher.shape[0]
    units = shared_gate.shape[1]
    experts = router.shape[0]
    share = capacity // 4
    pad = -(-share // 16) * 16
    rows = groups * pad
    shape = jax.ShapeDtypeStruct
    vmem = pl.BlockSpec(memory_space=pltpu.VMEM)
    hbm = pl.BlockSpec(memory_space=pl.ANY)
    dma = pltpu.SemaphoreType.DMA
    wide, tall, deep = (4, width, units), (4, units, width), (rows, 4 * units)
    return pl.pallas_call(
        functools.partial(moe_kernel, groups, share, pad),
        out_shape=(
            shape((length, width), BF16),
            shape((lanes, length), BF16),
            shape((8, length), F32),
            shape(teacher.shape, BF16),
            shape((length, width), BF16),
            shape((2 * width, units), BF16),
            shape((units, width), BF16),
            shape((width, units), BF16),
            shape((2, width, units), BF16),
            shape((2, units, width), BF16),
            shape((8, width), F32),
            shape((experts, width), F32),
        ),
        in_specs=[hbm] * 2 + [vmem] + [hbm] * 5 + [vmem] * 5 + [hbm] * 6,
        out_specs=(hbm,) * 2 + (vmem,) * 2 + (hbm,) + (vmem,) * 3 + (hbm,) * 2 + (vmem,) * 2,
        scratch_shapes=[
            *([pltpu.VMEM((lanes, width), BF16)] * 3),
            pltpu.VMEM((lanes, length), BF16),
            pltpu.VMEM((width, units), BF16),
            pltpu.VMEM((width, units), BF16),
            pltpu.VMEM((units, width), BF16),
            pltpu.VMEM((length, width), BF16),
            pltpu.VMEM(wide, BF16),
            pltpu.VMEM(wide, BF16),
            pltpu.VMEM(tall, BF16),
            pltpu.VMEM((rows, length), BF16),
            pltpu.VMEM((rows, length), BF16),
            pltpu.VMEM((rows, width), BF16),
            pltpu.VMEM((rows, width), BF16),
            pltpu.VMEM((rows, width), BF16),
            pltpu.VMEM((rows, width), BF16),
            pltpu.VMEM((rows, width), BF16),
            pltpu.VMEM(deep, BF16),
            pltpu.VMEM(deep, BF16),
            pltpu.VMEM(deep, BF16),
            pltpu.VMEM((length, units), BF16),
            pltpu.VMEM((length, units), BF16),
            pltpu.VMEM((length, units), BF16),
            pltpu.VMEM((length // 2, width), F32),
            pltpu.VMEM((length, width), BF16),
            pltpu.VMEM((length, width), F32),
            pltpu.VMEM((length, width), BF16),
            pltpu.VMEM((2 * width if groups == 8 else 16, units), BF16),
            pltpu.VMEM((units if groups == 8 else 16, width), BF16),
            pltpu.VMEM((length // 2, width), BF16),
            pltpu.VMEM((2, length // 2, width), BF16),
            pltpu.VMEM((length // 2, width), BF16),
            pltpu.VMEM((2, length // 2, width), BF16),
            dma((4, groups)),
            dma((4, groups)),
            dma((2, 3, 4)),
            dma((2, 3, 4)),
            dma((4, 3)),
            dma((4, 3)),
            dma((4, 3)),
            dma((4, 3)),
            dma((3,)),
            dma((3,)),
            dma((4, 3)),
            dma((4, 3)),
            dma((8,)),
            dma((7,)),
            dma((7,)),
            pltpu.SemaphoreType.REGULAR((3,)),
            dma((15,)),
        ],
        compiler_params=pltpu.CompilerParams(
            collective_id=2, has_side_effects=True, vmem_limit_bytes=63 * 2**20
        ),
        name="layer",
    )(
        hidden_in,
        table,
        gain_one,
        w_query,
        w_key,
        w_value,
        w_out,
        teacher,
        seg_row,
        routes,
        slots,
        router,
        gain,
        shared_gate,
        shared_up,
        shared_down,
        gate_in,
        up_in,
        down_in,
    )


def finish_kernel(
    groups,
    residual_in,
    hidden_in,
    gain_one,
    w_query,
    w_key,
    w_value,
    w_out,
    qkv_in,
    summary,
    mixed,
    table_in,
    seg_row,
    small_in,
    router_in,
    wide_in,
    tall_in,
    up_in,
    down_in,
    grad_input,
    grad_up,
    grad_down,
    side_wide,
    side_tall,
    sums_out,
    small,
    grad_residual,
    hidden,
    qkv,
    table,
    normed,
    grad_mixed,
    grad_query,
    grad_keys,
    grad_values,
    turned,
    product,
    scales,
    pair_wide,
    pair_tall,
    chip_wide,
    chip_tall,
    pay,
    pay_core,
    pay_out,
    pay_in,
    sums,
    landed,
    direct_land,
    small_land,
    pair_send,
    pair_recv,
    side_send,
    side_recv,
    sum_send,
    sum_recv,
    direct_send,
    direct_recv,
    small_send,
    small_recv,
    pay_send,
    pay_recv,
    copy_sem,
):
    length, width = hidden.shape
    lanes = w_query.shape[0]
    heads = lanes // HD
    block = length // 4
    bits = 3 if groups == 8 else 0
    e, t = lax.axis_index("expert"), lax.axis_index("tensor")
    beside, across = peer_of(t, 1), peer_of(t, 2)
    opposite = peer_of(across, 1)
    peers = expert_peers(bits)
    gain_one_row = gain_one[...].reshape(1, -1)
    others = [(lax.rem(e + n, groups), t) for n in range(1, groups)] if bits else []
    greet(others + [(e, beside), (e, across)])

    loads = [
        pltpu.make_async_copy(src, dst, copy_sem.at[10 + n])
        for n, (src, dst) in enumerate(
            ((hidden_in, hidden), (residual_in, grad_residual), (qkv_in, qkv), (table_in, table))
        )
    ]
    for load in loads:
        load.start()

    def remote(src, dst, device, send, recv):
        return pltpu.make_async_remote_copy(
            src_ref=src,
            dst_ref=dst,
            send_sem=send,
            recv_sem=recv,
            device_id=device,
            device_id_type=MESH,
        )

    parts = ((up_in, pair_wide, chip_wide, grad_up), (down_in, pair_tall, chip_tall, grad_down))

    def own_copy(w):
        return pltpu.make_async_copy(parts[w][0].at[1], parts[w][1], copy_sem.at[w])

    def chip_copy(w):
        return remote(
            parts[w][0].at[0], parts[w][2], (e, across), pair_send.at[w], pair_recv.at[w]
        )

    for w in range(2):
        chip_copy(w).start()
        own_copy(w).start()

    sides = side_streams(
        groups, side_wide, side_tall, False, None, None, side_send, side_recv
    )
    side_copies = []
    for n, s in enumerate(sides):
        rows = s.stages[1][1]
        src = wide_in if n < 2 else tall_in
        side_copies.append(
            pltpu.make_async_copy(src.at[rows], s.out.at[rows], copy_sem.at[6 + n])
        )
    if not sides:
        side_copies = [
            pltpu.make_async_copy(wide_in, side_wide, copy_sem.at[6]),
            pltpu.make_async_copy(tall_in, side_tall, copy_sem.at[7]),
        ]
    for copy in side_copies:
        copy.start()
    for copy in side_copies:
        copy.wait()
    advance(sides, None, 3)

    streams = []
    if not bits:
        sums = sums_out
    if bits:
        streams = [
            Stream(
                sums,
                sums_out,
                h * 4 * HD,
                4 * HD,
                (0, 1, 2) if h % 2 == 0 else (1, 0, 2),
                landed,
                h * 4 * HD,
                sum_send,
                sum_recv,
                h,
            )
            for h in range(heads - 1)
        ]

    last = (heads - 1) * 4 * HD
    few = 4 * HD // 8

    def part_of(group):
        return pl.ds(pl.multiple_of(last + group * few, 16), few)

    def direct(n, phase, arriving=False):
        group = others[n][0]
        if phase == 0:
            src = sums.at[part_of(group)]
            dst = direct_land.at[group if arriving else e]
        else:
            src = sums_out.at[part_of(e)]
            dst = sums_out.at[part_of(group if arriving else e)]
        return remote(
            src,
            dst,
            others[n],
            direct_send.at[phase, n],
            direct_recv.at[phase, group if arriving else e],
        )

    def direct_begin(phase):
        for n in range(len(others)):
            direct(n, phase).start()

    def direct_end(phase):
        for n in range(len(others)):
            direct(n, phase, True).wait_recv()
        if phase == 0 and bits:
            total = sums[part_of(e), :].astype(F32)
            for group, _ in others:
                total = total + direct_land[group].astype(F32)
            sums_out[part_of(e), :] = total.astype(BF16)

    columns = [pl.ds(n * WIDE, lanes) for n in range(3)]
    seg_col = column_of(seg_row[...])
    seg_line = seg_row[...].astype(F32)
    for load in loads:
        load.wait()
    for i in range(4):
        rows = pl.ds(i * block, block)
        inputs = hidden[rows, :].astype(F32)
        scale = lax.rsqrt(jnp.mean(inputs * inputs, axis=-1, keepdims=True) + eps_norm)
        normed[rows, :] = (inputs * scale * gain_one_row).astype(BF16)
        scales[:, rows] = jnp.broadcast_to(scale, (block, 128)).T[0:8, :]
        grad_mixed[rows, :] = mm_nt(grad_residual[rows, :], w_out[...]).astype(BF16)
    grad_out = mm(mixed[...], grad_residual[...]).astype(BF16)
    for h in range(heads):
        sums[pl.ds(h * 4 * HD + 3 * HD, HD), :] = grad_out[h * HD : (h + 1) * HD, :]
    for ref in (grad_query, grad_keys, grad_values):
        ref[...] = jnp.zeros_like(ref)
    swap = swap_halves(lanes)
    small[...] = jnp.concatenate([small_in[...], router_in[...]], axis=0)
    gain_sum = jnp.zeros((1, width), F32)

    for h in range(heads):
        for i in range(4):
            rows = pl.ds(i * block, block)
            reach = (i + 1) * block
            key_at = lax.broadcasted_iota(jnp.int32, (reach, block), 0)
            query_at = lax.broadcasted_iota(jnp.int32, (reach, block), 1) + i * block
            allowed = (seg_col[0:reach, :] == seg_line[:, i * block : (i + 1) * block]) & (
                key_at <= query_at
            )
            q_head = only(qkv[rows, columns[0]] * (HD ** (-0.5)), h)
            g_head = only(grad_mixed[rows, :], h)
            scores = mm_nt(qkv[0:reach, columns[1]], q_head) - summary[h : h + 1, rows]
            prob = jnp.exp(jnp.where(allowed, scores, -1e30))
            grad_prob = mm_nt(qkv[0:reach, columns[2]], g_head)
            inner = jnp.sum(prob * grad_prob, axis=0, keepdims=True)
            grad_scores = (prob * (grad_prob - inner)).astype(BF16)
            grad_values[0:reach, :] += mm(prob.astype(BF16), g_head)
            grad_keys[0:reach, :] += mm(grad_scores, q_head)
            grad_query[rows, :] += mm_tn(grad_scores, only(qkv[0:reach, columns[1]], h)) * (HD ** (-0.5))
            if h == 1 and i == 3:
                advance(sides, 3, 4)
        for i in range(4):
            rows = pl.ds(i * block, block)
            for n, grad in enumerate((grad_query, grad_keys)):
                value = only(grad[rows, :], h)
                high = value.astype(BF16)
                rest = (value - high.astype(F32)).astype(BF16)
                swapped = mm(high, swap) + mm(rest, swap)
                value = (value * table[rows, columns[0]] - swapped * table[rows, columns[1]]).astype(BF16)
                turned[n, h, rows, :] = value
            turned[2, h, rows, :] = only(grad_values[rows, :], h).astype(BF16)
        for n, w in enumerate((w_query, w_key, w_value)):
            made = mm_tn(turned[n, h], normed[...])[h * HD : (h + 1) * HD, :]
            gain_sum = gain_sum + jnp.sum(
                made * w[h * HD : (h + 1) * HD, :].astype(F32), axis=0, keepdims=True
            )
            sums[pl.ds(h * 4 * HD + n * HD, HD), :] = made.astype(BF16)
        if h == 1:
            advance(streams[0:1], 0, 1)
        if h < heads - 1:
            advance(streams[h : h + 1], None, 0)
        else:
            direct_begin(0)

    small[2:3, :] = gain_sum / gain_one_row
    valid = jnp.where(seg_row[...] != 0, 1.0, 0.0)
    small[3:4, :] = jnp.broadcast_to(jnp.sum(valid, axis=1, keepdims=True), (1, width))

    def small_copy(k):
        device = peers[k] if k < bits else (e, (beside, across)[k - bits])
        return remote(small, small_land.at[k], device, small_send.at[k], small_recv.at[k])

    def small_next(k):
        if bits:
            if k > 0:
                small_copy(k - 1).wait()
                small[...] += small_land[k - 1]
            if k < 5:
                small_copy(k).start()

    advance(streams[0:1], 1, 2)
    advance(streams[1:2], 0, 1)
    small_next(0)
    for i in range(4):
        rows = pl.ds(i * block, block)
        product[rows, :] = (
            grad_query[rows, :] * qkv[rows, columns[0]].astype(F32)
            + grad_keys[rows, :] * qkv[rows, columns[1]].astype(F32)
            + grad_values[rows, :] * qkv[rows, columns[2]].astype(F32)
        ).astype(BF16)
    ones = jnp.ones((16, lanes), BF16)
    dots = mm_nt(ones, product[...]).astype(BF16)
    flipped = [w[...].astype(F32).T.astype(BF16) for w in (w_query, w_key, w_value)]
    for n in range(3):
        total = turned[n, 0]
        for h in range(1, heads):
            total = total + turned[n, h]
        turned[n, 0] = total
    for m in range(4):
        rows = slice(m * lanes, (m + 1) * lanes)
        made = sum(mm_nt(flipped[n][rows, :], turned[n, 0]) for n in range(3))
        pay[m, 0:lanes, :] = made.astype(BF16)
        pay[m, lanes : lanes + 16, :] = dots

    def pay_copy(k):
        if k < 2:
            return remote(
                pay.at[(opposite, beside)[k]],
                pay_core.at[k],
                (e, beside),
                pay_send.at[k],
                pay_recv.at[k],
            )
        return remote(pay_out, pay_in, (e, across), pay_send.at[k], pay_recv.at[k])

    pay_copy(0).start()
    pay_copy(1).start()
    place_own = own_columns(lanes, width, t)
    gain_col = jnp.sum(jnp.where(place_own != 0, gain_one_row, 0.0), axis=1, keepdims=True)
    pay_copy(0).wait_recv()
    pay_out[...] = (pay[across].astype(F32) + pay_core[0].astype(F32)).astype(BF16)
    pay_copy(2).start()
    advance(streams[0:1], 2, 3)
    advance(streams[1:2], 1, 2)
    advance(sides, 4, None)
    small_next(1)
    direct_end(0)
    direct_begin(1)
    advance(streams[0:1], 3, 4)
    small_next(2)
    advance(streams[1:2], 2, 3)
    small_next(3)
    for w in range(2):
        _, pair, chip, result = parts[w]
        own_copy(w).wait()
        chip_copy(w).wait_recv()
        result[...] = (pair[...].astype(F32) + chip[...].astype(F32)).astype(BF16)
    advance(streams[0:1], 4, None)
    advance(streams[1:2], 3, 4)
    small_next(4)
    pay_copy(1).wait_recv()
    pay_copy(2).wait_recv()
    received = pay[t].astype(F32) + pay_core[1].astype(F32) + pay_in[...].astype(F32)
    scale = scales[0:1, :]
    grad_input[...] = (
        mm_nt(place_own, grad_residual[...])
        + scale * (received[0:lanes, :] * gain_col)
        - mm_nt(place_own, hidden[...])
        * (scale * scale * (received[lanes : lanes + 1, :] / width))
    )
    small_next(5)
    advance(streams[1:2], 4, None)
    direct_end(1)
    for s in sides:
        s.close(range(3, 5))
    for s in streams:
        s.close(range(5))
    for n in range(len(others)):
        direct(n, 0).wait_send()
        direct(n, 1).wait_send()
    for w in range(2):
        chip_copy(w).wait_send()
    for k in range(3):
        pay_copy(k).wait_send()


def finish(groups, *args):
    hidden, w_query, small_in, router_in, wide_in, tall_in = args[1], args[3], *args[12:16]
    length, width = hidden.shape
    lanes = w_query.shape[0]
    units = tall_in.shape[0]
    smalls = 8 + router_in.shape[0]
    shape = jax.ShapeDtypeStruct
    vmem = pl.BlockSpec(memory_space=pltpu.VMEM)
    hbm = pl.BlockSpec(memory_space=pl.ANY)
    dma = pltpu.SemaphoreType.DMA
    return pl.pallas_call(
        functools.partial(finish_kernel, groups),
        out_shape=(
            shape((lanes, length), F32),
            shape((width, units), BF16),
            shape((units, width), BF16),
            shape(wide_in.shape, BF16),
            shape(tall_in.shape, BF16),
            shape((4 * lanes, width), BF16),
            shape((smalls, width), F32),
        ),
        in_specs=[hbm] * 2 + [vmem] * 5 + [hbm] + [vmem] * 2 + [hbm] + [vmem] * 3 + [hbm] * 4,
        out_specs=(vmem,) * 7,
        scratch_shapes=[
            pltpu.VMEM((length, width), BF16),
            pltpu.VMEM((length, width), BF16),
            pltpu.VMEM((length, 3 * WIDE), BF16),
            pltpu.VMEM((length, 2 * WIDE), F32),
            pltpu.VMEM((length, width), BF16),
            pltpu.VMEM((length, lanes), BF16),
            pltpu.VMEM((length, lanes), F32),
            pltpu.VMEM((length, lanes), F32),
            pltpu.VMEM((length, lanes), F32),
            pltpu.VMEM((3, lanes // HD, length, lanes), BF16),
            pltpu.VMEM((length, lanes), BF16),
            pltpu.VMEM((8, length), F32),
            pltpu.VMEM((width, units), BF16),
            pltpu.VMEM((units, width), BF16),
            pltpu.VMEM((width, units), BF16),
            pltpu.VMEM((units, width), BF16),
            pltpu.VMEM((4, lanes + 16, length), BF16),
            pltpu.VMEM((2, lanes + 16, length), BF16),
            pltpu.VMEM((lanes + 16, length), BF16),
            pltpu.VMEM((lanes + 16, length), BF16),
            pltpu.VMEM((4 * lanes, width), BF16),
            pltpu.VMEM((8 * HD, width), BF16),
            pltpu.VMEM((8, HD // 2, width), BF16),
            pltpu.VMEM((5, smalls, width), F32),
            dma((2,)),
            dma((2,)),
            dma((4, 6)),
            dma((4, 6)),
            dma((3, 6)),
            dma((3, 6)),
            dma((2, 8)),
            dma((2, 8)),
            dma((5,)),
            dma((5,)),
            dma((3,)),
            dma((3,)),
            dma((14,)),
        ],
        compiler_params=pltpu.CompilerParams(
            collective_id=3, has_side_effects=True, vmem_limit_bytes=60 * 2**20
        ),
        name="finish",
    )(*args)


def scale_kernel(numbers, small, *refs):
    tokens, width, members = numbers
    ins, outs = refs[:11], refs[11:]
    count = small[3:4, 0:1] * (1.0 / members)
    factor = 2.0 * tokens / count
    for src, dst in zip(ins, outs):
        dst[...] = src[...].astype(F32) * factor
    attn, ffn, router, loss = outs[11:]
    attn[...] = (small[2:3, :] * factor).reshape(width)
    ffn[...] = (small[1:2, :] * (0.5 * factor)).reshape(width)
    router[...] = small[8:, :] * factor
    loss[...] = jnp.sum(small[0:1, :], axis=1, keepdims=True) * 0.5 / (count * width)


def scale_all(tokens, members, small, grad_input, gate, up, down, wide, tall, sums):
    width = sums.shape[1]
    lanes, length = grad_input.shape
    units = gate.shape[1]
    experts = small.shape[0] - 8
    parts = 6
    row = width // parts
    head = lanes // parts
    shape = jax.ShapeDtypeStruct

    def rows_of(n, offset=0):
        return lambda i: (offset + i, 0)

    def own(n):
        return pl.BlockSpec((head, width), lambda i, n=n: ((i // 2) * 8 + 2 * n + i % 2, 0))

    by_rows = pl.BlockSpec((row, units), lambda i: (i, 0))
    by_cols = pl.BlockSpec((units, row), lambda i: (0, i))
    in_specs = [
        pl.BlockSpec(small.shape, lambda i: (0, 0)),
        pl.BlockSpec((head, length), lambda i: (i, 0)),
        by_rows,
        by_rows,
        by_cols,
        pl.BlockSpec((row, units), lambda i: (i, 0)),
        pl.BlockSpec((row, units), lambda i: (parts + i, 0)),
        by_cols,
        own(0),
        own(1),
        own(2),
        own(3),
    ]
    own_out = pl.BlockSpec((head, width), lambda i: (i, 0))

    def whole(rows, cols):
        return pl.BlockSpec((rows, cols), lambda i: (0, 0))

    out_specs = [
        pl.BlockSpec((head, length), lambda i: (i, 0)),
        by_rows,
        by_rows,
        by_cols,
        by_rows,
        by_rows,
        by_cols,
        *([own_out] * 4),
        pl.BlockSpec((width,), lambda i: (0,)),
        pl.BlockSpec((width,), lambda i: (0,)),
        whole(experts, width),
        whole(1, 1),
    ]
    wide_shape, tall_shape = shape((width, units), F32), shape((units, width), F32)
    return pl.pallas_call(
        functools.partial(scale_kernel, (tokens, width, members)),
        grid=(parts,),
        out_shape=[
            shape((lanes, length), F32),
            wide_shape,
            wide_shape,
            tall_shape,
            wide_shape,
            wide_shape,
            tall_shape,
            *([shape((lanes, width), F32)] * 4),
            shape((width,), F32),
            shape((width,), F32),
            shape((experts, width), F32),
            shape((1, 1), F32),
        ],
        in_specs=in_specs,
        out_specs=out_specs,
        name="scale",
    )(small, grad_input, gate, up, down, wide, wide, tall, sums, sums, sums, sums)


def body(
    hidden_in,
    norm_attn,
    w_query,
    w_key,
    w_value,
    w_out,
    norm_ffn,
    w_router,
    shared_gate,
    shared_up,
    shared_down,
    expert_gate,
    expert_up,
    expert_down,
    segment,
    routes,
    slots,
    teacher,
):
    length, width = hidden_in.shape
    groups = lax.axis_size("expert")
    members = lax.axis_size("tensor")
    capacity = 3 * length // groups
    lanes = w_query.shape[1]
    table = jnp.asarray(rope_rows(length, lanes // HD))
    seg_row = segment[None]
    gain_one, gain_two = norm_attn, norm_ffn
    (
        qkv,
        mixed,
        summary,
        activations,
        grad_residual,
        wide,
        tall,
        gate,
        up_parts,
        down_parts,
        small,
        router,
    ) = moe(
        groups,
        capacity,
        hidden_in,
        table,
        gain_one,
        w_query.T,
        w_key.T,
        w_value.T,
        w_out,
        teacher.T,
        seg_row,
        routes.T,
        slots.T,
        w_router.T,
        gain_two,
        shared_gate,
        shared_up,
        shared_down,
        expert_gate[0],
        expert_up[0],
        expert_down[0],
    )
    grad_input, up, down, wide, tall, sums, small = finish(
        groups,
        grad_residual,
        hidden_in,
        gain_one,
        w_query.T,
        w_key.T,
        w_value.T,
        w_out,
        qkv,
        summary,
        mixed,
        table,
        seg_row,
        small,
        router,
        wide,
        tall,
        up_parts,
        down_parts,
    )
    if groups != 8:
        wide, tall, sums = lax.psum((wide, tall, sums), "expert")
        small = lax.psum(small, ("expert", "tensor"))
    (
        grad_input,
        gate,
        up,
        down,
        side_gate,
        side_up,
        side_down,
        grad_query,
        grad_key,
        grad_value,
        grad_out,
        grad_norm_attn,
        grad_norm_ffn,
        grad_router,
        loss,
    ) = scale_all(
        length * groups, members, small, grad_input, gate, up, down, wide, tall, sums
    )
    return (
        loss[0, 0],
        activations.T,
        grad_input.T,
        grad_norm_attn,
        grad_query.T,
        grad_key.T,
        grad_value.T,
        grad_out,
        grad_norm_ffn,
        grad_router.T,
        side_gate,
        side_up,
        side_down,
        gate[None],
        up[None],
        down[None],
    )


def solution(mesh):
    placed = (
        P("expert", None),
        P(),
        P(None, "tensor"),
        P(None, "tensor"),
        P(None, "tensor"),
        P("tensor", None),
        P(),
        P(),
        P(None, "tensor"),
        P(None, "tensor"),
        P("tensor", None),
        P("expert", None, "tensor"),
        P("expert", None, "tensor"),
        P("expert", "tensor", None),
        P("expert"),
        P("expert", None),
        P("expert", None),
        P("expert", "tensor"),
    )
    return jax.shard_map(
        body,
        mesh=mesh,
        in_specs=placed,
        out_specs=(
            P(),
            P("expert", "tensor"),
            P("expert", "tensor"),
            P(),
            P(None, "tensor"),
            P(None, "tensor"),
            P(None, "tensor"),
            P("tensor", None),
            P(),
            P(),
            P(None, "tensor"),
            P(None, "tensor"),
            P("tensor", None),
            P("expert", None, "tensor"),
            P("expert", None, "tensor"),
            P("expert", "tensor", None),
        ),
        check_vma=False,
    )
```

```python
import functools

import jax
import jax.numpy as jnp
import numpy as np
from jax import lax
from jax.experimental import pallas as pl
from jax.experimental.pallas import tpu as pltpu
from jax.sharding import PartitionSpec as P

HD = 64
WIDE = 256
F32, BF16 = jnp.float32, jnp.bfloat16
MESH = pl.DeviceIdType.MESH


eps_norm = 1e-06


def rope_rows(length, heads):
    half = HD // 2
    freqs = (10000.0 ** (-2.0 * np.arange(half) / HD)).astype(np.float32)
    angles = np.arange(length, dtype=np.float32)[:, None] * freqs[None, :]
    cosine, sine = np.cos(angles), np.sin(angles)
    table = np.zeros((length, 2 * WIDE), np.float32)
    table[:, : heads * HD] = np.tile(np.concatenate([cosine, cosine], axis=1), (1, heads))
    table[:, WIDE : WIDE + heads * HD] = np.tile(np.concatenate([-sine, sine], axis=1), (1, heads))
    return table


def peer_of(t, step):
    if step == 1:
        return t + 1 - 2 * lax.rem(t, 2)
    return lax.rem(t + 2, 4)


def greet(peers):
    barrier = pltpu.get_barrier_semaphore()
    for peer in peers:
        pl.semaphore_signal(barrier, inc=1, device_id=peer, device_id_type=MESH)
    pl.semaphore_wait(barrier, len(peers))


def mm(a, b):
    return lax.dot_general(a, b, (((1,), (0,)), ((), ())), preferred_element_type=F32)


def mm_nt(a, b):
    return lax.dot_general(a, b, (((1,), (1,)), ((), ())), preferred_element_type=F32)


def mm_tn(a, b):
    return lax.dot_general(a, b, (((0,), (0,)), ((), ())), preferred_element_type=F32)


def swap_halves(width):
    row = lax.broadcasted_iota(jnp.int32, (width, width), 0)
    col = lax.broadcasted_iota(jnp.int32, (width, width), 1)
    half = HD // 2
    other = jnp.where(lax.rem(col, HD) < half, col + half, col - half)
    return (row == other).astype(F32).astype(BF16)


def head_mask(rows, width, head):
    col = lax.broadcasted_iota(jnp.int32, (rows, width), 1)
    return (col >= head * HD) & (col < (head + 1) * HD)


def only(value, head):
    keep = head_mask(value.shape[0], value.shape[1], head)
    return jnp.where(keep, value, jnp.zeros_like(value))


def column_of(row):
    wide = jnp.broadcast_to(row.astype(F32), (128, row.shape[1]))
    return wide.T[:, 0:1]


def own_columns(lanes, width, t):
    row = lax.broadcasted_iota(jnp.int32, (lanes, width), 0)
    col = lax.broadcasted_iota(jnp.int32, (lanes, width), 1)
    return (col == row + t * lanes).astype(F32).astype(BF16)


class Stream:
    def __init__(self, buf, out, base, size, order, land, land_at, send, recv, index):
        self.buf, self.out, self.land, self.index = buf, out, land, index
        self.send, self.recv = send, recv
        e, self.t = lax.axis_index("expert"), lax.axis_index("tensor")
        self.stages, start = [], base
        for k, b in enumerate(order):
            half = size >> min(k + 1, 2)
            bit = lax.rem(e // 2**b, 2)
            peer = e + 2**b - 2 * 2**b * bit
            if k == 2:
                bit = give = keep = None
                keep = give = self.stages[1][1]
            else:
                keep = pl.ds(pl.multiple_of(start + bit * half, 16), half)
                give = pl.ds(pl.multiple_of(start + (1 - bit) * half, 16), half)
                start = start + bit * half
            self.stages.append((peer, keep, give, pl.ds(land_at, half)))
            land_at += half

    def copy(self, step, arriving=False):
        peer, keep, give, land = self.stages[step if step < 3 else 4 - step]
        if step < 3:
            src, dst = self.buf.at[give], self.land.at[land]
        else:
            src, dst = self.out.at[keep], self.out.at[give if arriving else keep]
        return pltpu.make_async_remote_copy(
            src_ref=src,
            dst_ref=dst,
            send_sem=self.send.at[self.index, step],
            recv_sem=self.recv.at[self.index, step],
            device_id=(peer, self.t),
            device_id_type=MESH,
        )

    def begin(self, step):
        self.copy(step).start()

    def end(self, step):
        self.copy(step, True).wait_recv()
        if step < 3:
            _, keep, _, land = self.stages[step]
            total = self.buf[keep, :].astype(F32) + self.land[land, :].astype(F32)
            if step == 2:
                self.copy(2).wait_send()
            if step == 2 and self.out is not None:
                self.out[keep, :] = total.astype(BF16)
            else:
                self.buf[keep, :] = total.astype(BF16)

    def close(self, steps):
        for step in steps:
            if step != 2:
                self.copy(step).wait_send()


def advance(streams, last, first):
    for s in streams:
        if last is not None:
            s.end(last)
        if first is not None:
            s.begin(first)


def expert_peers(bits):
    e, t = lax.axis_index("expert"), lax.axis_index("tensor")
    return [(e + 2**b - 2 * 2**b * lax.rem(e // 2**b, 2), t) for b in range(bits)]


def each(count, do):
    if count <= 8:
        for i in range(count):
            do(i)
    else:
        lax.fori_loop(0, count, lambda i, none: (do(i), none)[1], 0)


def steps(count, do):
    lax.fori_loop(0, count, lambda i, none: (do(i), none)[1], 0)


def side_streams(groups, wide, tall, halving, wide_land, tall_land, send, recv):
    if groups != 8:
        return []
    rows, few = wide.shape[0] // 2, tall.shape[0] // 2
    wides = (wide, None) if halving else (None, wide)
    talls = (tall, None) if halving else (None, tall)
    return [
        Stream(*wides, 0, rows, (0, 1, 2), wide_land, 0, send, recv, 0),
        Stream(*wides, rows, rows, (1, 0, 2), wide_land, rows, send, recv, 1),
        Stream(*talls, 0, few, (0, 1, 2), tall_land, 0, send, recv, 2),
        Stream(*talls, few, few, (1, 0, 2), tall_land, few, send, recv, 3),
    ]


def moe_kernel(
    groups,
    share,
    pad,
    hidden_in,
    table,
    gain_one,
    query_in,
    key_in,
    value_in,
    w_out,
    teacher_in,
    seg_row,
    routes,
    slots,
    router,
    gain,
    shared_gate_in,
    shared_up_in,
    shared_down_in,
    gate_in,
    up_in,
    down_in,
    query_out,
    mixed_out,
    summary,
    activations,
    grad_residual,
    side_wide,
    side_tall,
    grad_gate,
    grad_up,
    grad_down,
    small,
    grad_router,
    w_query,
    w_key,
    w_value,
    teacher,
    shared_gate,
    shared_up,
    shared_down,
    normed,
    gate_all,
    up_all,
    down_all,
    pick,
    weigh,
    out_buf,
    back_buf,
    rows_in,
    returned,
    grad_rows,
    act,
    slope,
    hidden,
    side_act,
    side_slope,
    side_hidden,
    residual_half,
    off,
    part,
    error,
    wide_land,
    tall_land,
    half_out,
    half_in,
    chip_out,
    chip_in,
    a2a_send,
    a2a_recv,
    sum_send,
    sum_recv,
    gather_send,
    gather_recv,
    mixed_send,
    mixed_recv,
    out_send,
    out_recv,
    side_send,
    side_recv,
    input_sem,
    pair_send,
    pair_recv,
    free_sem,
    copy_sem,
):
    length, width = normed.shape
    lanes = teacher.shape[0]
    heads = lanes // HD
    units = shared_gate.shape[1]
    experts = router.shape[0]
    rows = groups * pad
    half_groups, half_rows = groups // 2, rows // 2
    chunk = length // 4
    e, t = lax.axis_index("expert"), lax.axis_index("tensor")
    beside, across = peer_of(t, 1), peer_of(t, 2)
    opposite = peer_of(across, 1)
    gain_row = gain[...].reshape(1, -1)
    gain_one_row = gain_one[...].reshape(1, -1)
    greet(
        [(lax.rem(e + j, groups), t) for j in range(1, groups)] + [(e, beside), (e, across)]
    )

    def remote(src, dst, device, send, recv):
        return pltpu.make_async_remote_copy(
            src_ref=src,
            dst_ref=dst,
            send_sem=send,
            recv_sem=recv,
            device_id=device,
            device_id_type=MESH,
        )

    above, below = pl.ds(0, width // 2), pl.ds(width // 2, width // 2)
    gathers = (
        (gate_in.at[above], lambda m: gate_all.at[m, above]),
        (gate_in.at[below], lambda m: gate_all.at[m, below]),
        (up_in, lambda m: up_all.at[m]),
        (down_in, lambda m: down_all.at[m]),
    )

    def gather(w, k):
        src, slot_of = gathers[w]
        slot = t if k < 2 else across
        return remote(
            src if k < 2 else slot_of(slot),
            slot_of(slot),
            (e, across if k == 0 else beside),
            gather_send.at[w, k],
            gather_recv.at[w, k],
        )

    def own_weights(w):
        src, dst = ((gate_in, gate_all), (up_in, up_all), (down_in, down_all))[w]
        return pltpu.make_async_copy(src, dst.at[t], copy_sem.at[w])

    block = length // 4

    def out_rows(m):
        return hidden.at[pl.ds(pl.multiple_of(m * lanes, HD), lanes), pl.ds(0, width)]

    def mixed_block(m, i):
        return act.at[pl.ds(pl.multiple_of(m * lanes, HD), lanes), pl.ds(i * block, block)]

    def out_copy(k):
        rows = out_rows(t if k < 2 else across)
        return remote(
            w_out if k < 2 else rows,
            rows,
            (e, across if k == 0 else beside),
            out_send.at[k],
            out_recv.at[k],
        )

    def piece_of(i, k):
        ref = mixed_block(t if k < 2 else across, i)
        return remote(
            ref,
            ref,
            (e, across if k == 0 else beside),
            mixed_send.at[i, k],
            mixed_recv.at[i, k],
        )

    for k in range(2):
        out_copy(k).start()
    loads = [
        pltpu.make_async_copy(src, dst, input_sem.at[n])
        for n, (src, dst) in enumerate(
            (
                (query_in, w_query),
                (key_in, w_key),
                (value_in, w_value),
                (w_out, out_rows(t)),
                (teacher_in, teacher),
                (shared_gate_in, shared_gate),
                (shared_up_in, shared_up),
                (shared_down_in, shared_down),
            )
        )
    ]
    inputs_copy = pltpu.make_async_copy(hidden_in, off, copy_sem.at[11])
    inputs_copy.start()
    for load in loads[:4]:
        load.start()
    table_copy = pltpu.make_async_copy(table, part.at[:, pl.ds(0, 2 * WIDE)], copy_sem.at[12])
    table_copy.start()
    for w in range(4):
        gather(w, 1).start()
    for w in range(3):
        own_weights(w).start()
    for load in loads[4:]:
        load.start()
    for load in loads[:4]:
        load.wait()
    core = lax.rem(t, 2)
    seg_col = column_of(seg_row[...])
    seg_line = seg_row[...].astype(F32)
    swap = swap_halves(lanes)
    turns = [mm(swap, w[...]).astype(BF16) for w in (w_query, w_key)]
    columns = [pl.ds(n * WIDE, lanes) for n in range(3)]
    turned = pl.ds(0, lanes)
    inputs_copy.wait()
    table_copy.wait()

    def make(i):
        rows = pl.ds(i * block, block)
        inputs = off[rows, :].astype(F32)
        scale = lax.rsqrt(jnp.mean(inputs * inputs, axis=-1, keepdims=True) + eps_norm)
        value = (inputs * scale * gain_one_row).astype(BF16)
        error[rows, columns[2]] = mm_nt(value, w_value[...]).astype(BF16)
        slope[turned, rows] = mm_nt(w_value[...], value).astype(BF16)
        for n, (w, turn) in enumerate(zip((w_query, w_key), turns)):
            error[rows, columns[n]] = (
                mm_nt(value, w[...]) * part[rows, columns[0]]
                + mm_nt(value, turn) * part[rows, columns[1]]
            ).astype(BF16)

    def project(i):
        rows = pl.ds(i * block, block)
        piece_of(i, 1).wait_recv()
        piece_of(i, 2).wait_recv()
        total = off[rows, :].astype(F32)
        for m in range(4):
            total = total + mm_tn(mixed_block(m, i)[...], out_rows(m)[...])
        scale = lax.rsqrt(jnp.mean(total * total, axis=-1, keepdims=True) + eps_norm)
        normed[rows, :] = (total * scale * gain_row).astype(BF16)

        @pl.when(core == i // 2)
        def keep():
            residual_half[pl.ds((i % 2) * block, block), :] = total

    for i in range(4):
        make(i)
        tokens = pl.ds(i * block, block)
        reach = (i + 1) * block
        key_at = lax.broadcasted_iota(jnp.int32, (reach, block), 0)
        query_at = lax.broadcasted_iota(jnp.int32, (reach, block), 1) + i * block
        allowed = (seg_col[0:reach, :] == seg_line[:, i * block : (i + 1) * block]) & (
            key_at <= query_at
        )
        q_block = error[tokens, columns[0]] * (HD ** (-0.5))
        made = []
        for h in range(heads):
            scores = mm_nt(error[0:reach, columns[1]], only(q_block, h))
            scores = jnp.where(allowed, scores, -1e30)
            top = jnp.max(scores, axis=0, keepdims=True)
            expo = jnp.exp(scores - top)
            whole = jnp.sum(expo, axis=0, keepdims=True)
            prob = (expo * (1.0 / whole)).astype(BF16)
            made.append(mm(slope[h * HD : (h + 1) * HD, 0:reach], prob).astype(BF16))
            summary[h : h + 1, tokens] = top + jnp.log(whole)
        mixed_block(t, i)[...] = jnp.concatenate(made, axis=0)
        piece_of(i, 0).start()
        piece_of(i, 1).start()
        if i == 0:
            out_copy(0).wait_recv()
            out_copy(2).start()
        else:
            piece_of(i - 1, 0).wait_recv()
            piece_of(i - 1, 2).start()
        if i == 1:
            out_copy(1).wait_recv()
            out_copy(2).wait_recv()
        if i >= 2:
            project(i - 2)
    for w in range(4):
        gather(w, 0).start()
    query_copy = pltpu.make_async_copy(error, query_out, copy_sem.at[13])
    query_copy.start()
    piece_of(3, 0).wait_recv()
    piece_of(3, 2).start()
    mixed_copy = pltpu.make_async_copy(
        act.at[pl.ds(pl.multiple_of(t * lanes, HD), lanes), pl.ds(0, length)],
        mixed_out,
        copy_sem.at[14],
    )
    mixed_copy.start()
    project(2)
    project(3)

    far_half = 1 - e // half_groups
    near_half = e // half_groups

    def block_at(group):
        return pl.ds(pl.multiple_of(group * pad, 16), pad)

    def half_at(half):
        return pl.ds(pl.multiple_of(half * half_rows, 16), half_rows)

    def exchange(phase, sent, landed, group):
        return remote(
            sent.at[block_at(group)],
            landed.at[block_at(e)],
            (group, t),
            a2a_send.at[phase, group],
            a2a_recv.at[phase, e],
        )

    def arrival(phase, sent, landed, group):
        return remote(
            sent.at[block_at(group)],
            landed.at[block_at(group)],
            (group, t),
            a2a_send.at[phase, group],
            a2a_recv.at[phase, group],
        )

    def near_group(j):
        return near_half * half_groups + lax.rem(e + j, half_groups)

    def far_group(j):
        return far_half * half_groups + lax.rem(e + j, half_groups)

    def send_far(phase, sent, landed):
        each(half_groups, lambda j: exchange(phase, sent, landed, far_group(j)).start())

    def send_near(phase, sent, landed):
        each(half_groups - 1, lambda j: exchange(phase, sent, landed, near_group(j + 1)).start())
        landed[block_at(e), :] = sent[block_at(e), :]

    def await_far(phase, sent, landed):
        each(half_groups, lambda j: arrival(phase, sent, landed, far_group(j)).wait_recv())

    def await_near(phase, sent, landed):
        each(half_groups - 1, lambda j: arrival(phase, sent, landed, near_group(j + 1)).wait_recv())

    def await_sent(phase, sent, landed):
        each(half_groups, lambda j: exchange(phase, sent, landed, far_group(j)).wait_send())
        each(half_groups - 1, lambda j: exchange(phase, sent, landed, near_group(j + 1)).wait_send())

    low = t * share
    mine = (slots[...] >= low) & (slots[...] < low + share)
    place = jnp.where(mine, routes[...] * pad + slots[...] - low, -1)
    place_one, place_two = place[0:1, :], place[1:2, :]
    build = rows // 8

    def pick_rows(i):
        at = lax.broadcasted_iota(jnp.int32, (build, length), 0) + i * build
        hit = (at == place_one) | (at == place_two)
        block = pl.ds(pl.multiple_of(i * build, 16), build)
        pick[block, :] = jnp.where(hit, 1.0, 0.0).astype(BF16)

    for half, send in ((far_half, send_far), (near_half, send_near)):
        steps(4, lambda i, half=half: pick_rows(half * 4 + i))
        out_buf[half_at(half), :] = mm(pick[half_at(half), :], normed[...]).astype(BF16)
        send(0, out_buf, rows_in)

    logits = mm_nt(router[...], normed[...])
    named = lax.broadcasted_iota(jnp.int32, (experts, length), 0)
    here = [named == routes[k : k + 1, :] for k in range(2)]
    chosen = [jnp.sum(jnp.where(h, logits, 0.0), axis=0, keepdims=True) for h in here]
    top = jnp.maximum(chosen[0], chosen[1])
    raised = [jnp.exp(c - top) for c in chosen]
    total = raised[0] + raised[1]
    gate_one, gate_two = raised[0] / total, raised[1] / total

    def weigh_rows(i):
        at = lax.broadcasted_iota(jnp.int32, (build, length), 0) + i * build
        value = jnp.where(at == place_one, gate_one, jnp.where(at == place_two, gate_two, 0.0))
        weigh[pl.ds(pl.multiple_of(i * build, 16), build), :] = value.astype(BF16)

    steps(8, weigh_rows)

    def tokens_at(i):
        return pl.ds(pl.multiple_of(i * chunk, chunk), chunk)

    def silu_parts(pre, lin):
        sigma = 1.0 / (1.0 + jnp.exp(-pre))
        active = pre * sigma
        return active, lin * (sigma * (1.0 + pre * (1.0 - sigma))), active * lin

    def shared_forward(i):
        at = tokens_at(i)
        a, s, h = silu_parts(mm(normed[at, :], shared_gate[...]), mm(normed[at, :], shared_up[...]))
        side_act[at, :] = a.astype(BF16)
        side_slope[at, :] = s.astype(BF16)
        side_hidden[at, :] = h.astype(BF16)
        part[at, :] = mm(side_hidden[at, :], shared_down[...]) - mm_tn(teacher[:, at], place_own)

    place_own = own_columns(lanes, width, t)
    for load in loads[4:]:
        load.wait()
    steps(4, shared_forward)
    for w in range(3):
        own_weights(w).wait()
    for w in range(4):
        gather(w, 1).wait_recv()
    mixed_copy.wait()
    for k in range(3):
        out_copy(k).wait_send()
        for i in range(4):
            piece_of(i, k).wait_send()

    def units_of(m):
        return pl.ds(pl.multiple_of(m * units, units), units)

    def expert_units(half, m):
        at, cols = half_at(half), units_of(m)
        a, s, h = silu_parts(mm(rows_in[at, :], gate_all[m]), mm(rows_in[at, :], up_all[m]))
        act[at, cols] = a.astype(BF16)
        slope[at, cols] = s.astype(BF16)
        hidden[at, cols] = h.astype(BF16)

    await_far(0, out_buf, rows_in)
    for m in (t, beside):
        expert_units(far_half, m)
    await_near(0, out_buf, rows_in)
    for m in (t, beside):
        expert_units(near_half, m)
    for w in range(3):
        gather(w, 0).wait_recv()
        gather(w, 2).start()
    for half in (far_half, near_half):
        expert_units(half, across)
    for w in range(3):
        gather(w, 2).wait_recv()
    for half in (far_half, near_half):
        expert_units(half, opposite)
    gather(3, 0).wait_recv()
    gather(3, 2).start()
    gather(3, 2).wait_recv()
    for half, send in ((far_half, send_far), (near_half, send_near)):
        at = half_at(half)
        made = sum(mm(hidden[at, pl.ds(m * units, units)], down_all[m]) for m in range(4))
        back_buf[at, :] = made.astype(BF16)
        send(1, back_buf, returned)

    span = length // 8

    def tokens_of(which, q):
        return pl.ds(pl.multiple_of(which * (length // 2) + q * span, span), span)

    def piece(q):
        return pl.ds(q * span, span)

    def halves(turn, q):
        return remote(
            half_out.at[piece(q)],
            half_in.at[turn, piece(q)],
            (e, beside),
            sum_send.at[turn, 0, q],
            sum_recv.at[turn, 0, q],
        )

    def chips(turn, q):
        return remote(
            chip_out.at[piece(q)],
            chip_in.at[turn, piece(q)],
            (e, across),
            sum_send.at[turn, 1, q],
            sum_recv.at[turn, 1, q],
        )

    def spread(turn, which, q):
        return remote(
            off.at[tokens_of(which, q)],
            off.at[tokens_of(which, q)],
            (e, beside),
            sum_send.at[turn, 2, q],
            sum_recv.at[turn, 2, q],
        )

    def combine(matrix, landed, at, tokens):
        part[tokens, :] += mm_tn(matrix[at, tokens], landed[at, :])

    def sum_over_tensor(turn, matrix, phase, finish, then, idle):
        await_near(phase, back_buf, returned)
        steps(4, lambda i: combine(matrix, returned, half_at(near_half), tokens_at(i)))
        await_far(phase, back_buf, returned)
        last = half_at(far_half)
        then()

        def to_chip(q):
            halves(turn, q).wait_recv()
            chip_out[piece(q), :] = (
                part[tokens_of(core, q), :] + half_in[turn, piece(q), :].astype(F32)
            ).astype(BF16)
            chips(turn, q).start()

        for q in range(4):
            at = tokens_of(1 - core, q)
            combine(matrix, returned, last, at)
            half_out[piece(q), :] = part[at, :].astype(BF16)
            halves(turn, q).start()
            combine(matrix, returned, last, tokens_of(core, q))
            to_chip(q)
        idle()
        for q in range(4):
            chips(turn, q).wait_recv()
            finish(
                q,
                tokens_of(core, q),
                chip_out[piece(q), :].astype(F32) + chip_in[turn, piece(q), :].astype(F32),
            )
            spread(turn, core, q).start()
        for q in range(4):
            spread(turn, 1 - core, q).wait_recv()
        for q in range(4):
            halves(turn, q).wait_send()
            chips(turn, q).wait_send()
            spread(turn, core, q).wait_send()

    query_copy.wait()
    seen = seg_col != 0.0
    small[...] = jnp.zeros_like(small)
    half_seen = column_of(
        jnp.where(core == 0, seg_row[:, 0 : length // 2], seg_row[:, length // 2 : length])
    )

    def finish_forward(q, at, value):
        value = residual_half[piece(q), :] + value
        off[at, :] = value.astype(BF16)
        value = jnp.where(half_seen[q * span : (q + 1) * span, :] != 0.0, value, 0.0)
        small[0:1, :] += jnp.sum(value * value, axis=0, keepdims=True)

    sum_over_tensor(0, weigh, 1, finish_forward, lambda: None, lambda: None)
    for i in range(4):
        at = slice(i * chunk, (i + 1) * chunk)
        error[at, :] = jnp.where(seen[at, :], off[at, :].astype(F32), 0.0).astype(BF16)

    await_sent(0, out_buf, rows_in)
    for half, send in ((far_half, send_far), (near_half, send_near)):
        at = half_at(half)
        pair = mm(weigh[at, :], error[...])
        out_buf[at, :] = pair.astype(BF16)
        dots = jnp.sum(pair * returned[at, :].astype(F32), axis=1, keepdims=True)
        part[at, 0:128] = jnp.broadcast_to(dots, (half_rows, 128))
        send(2, out_buf, grad_rows)
    pl.semaphore_signal(free_sem.at[0], inc=1, device_id=(e, beside), device_id_type=MESH)
    activations[...] = (mm_nt(place_own, off[...]) + teacher[...].astype(F32)).astype(BF16)

    def take_dots(i, sums):
        block = pl.ds(pl.multiple_of(i * build, 16), build)
        at = lax.broadcasted_iota(jnp.int32, (build, length), 0) + i * build
        dots = part[block, 0:1]
        return tuple(
            s + jnp.sum(jnp.where(at == p, dots, 0.0), axis=0, keepdims=True)
            for s, p in zip(sums, (place_one, place_two))
        )

    zero = jnp.zeros((1, length), F32)
    dot_one, dot_two = lax.fori_loop(0, 8, take_dots, (zero, zero))

    def shared_backward(i):
        at = tokens_at(i)
        hid_grad = mm_nt(error[at, :], shared_down[...])
        side_slope[at, :] = (hid_grad * side_slope[at, :].astype(F32)).astype(BF16)
        side_act[at, :] = (hid_grad * side_act[at, :].astype(F32)).astype(BF16)
        part[at, :] = mm_nt(side_slope[at, :], shared_gate[...]) + mm_nt(
            side_act[at, :], shared_up[...]
        )

    def expert_backward(at):
        for m in range(4):
            cols = pl.ds(m * units, units)
            hid_grad = mm_nt(grad_rows[at, :], down_all[m])
            slope[at, cols] = (hid_grad * slope[at, cols].astype(F32)).astype(BF16)
            act[at, cols] = (hid_grad * act[at, cols].astype(F32)).astype(BF16)
        made = sum(
            mm_nt(slope[at, pl.ds(m * units, units)], gate_all[m])
            + mm_nt(act[at, pl.ds(m * units, units)], up_all[m])
            for m in range(4)
        )
        back_buf[at, :] = made.astype(BF16)

    def half_backward(half, wait, send):
        wait(2, out_buf, grad_rows)
        expert_backward(half_at(half))
        send(3, back_buf, returned)

    steps(4, shared_backward)
    await_sent(1, back_buf, returned)
    side_wide[0:width, :] = mm_tn(normed[...], side_slope[...]).astype(BF16)
    side_wide[width : 2 * width, :] = mm_tn(normed[...], side_act[...]).astype(BF16)
    side_tall[...] = mm_tn(side_hidden[...], error[...]).astype(BF16)
    sides = side_streams(
        groups, side_wide, side_tall, True, wide_land, tall_land, side_send, side_recv
    )
    advance(sides, None, 0)
    both = dot_one + dot_two
    grad_logits = (
        jnp.where(here[0], dot_one - gate_one * both, 0.0)
        + jnp.where(here[1], dot_two - gate_two * both, 0.0)
    ).astype(BF16)
    grad_router[...] = mm(grad_logits, normed[...])
    part[...] += mm_tn(grad_logits, router[...])
    half_backward(far_half, await_far, send_far)
    half_backward(near_half, await_near, send_near)

    advance(sides, 0, 1)
    for w in range(4):
        for k in range(3):
            gather(w, k).wait_send()
    await_sent(2, out_buf, grad_rows)
    pl.semaphore_signal(free_sem.at[1], inc=1, device_id=(e, across), device_id_type=MESH)
    for m in range(4):
        cols = pl.ds(m * units, units)
        gate_all[m] = mm_tn(rows_in[...], slope[:, cols]).astype(BF16)

    def gate_core(n):
        return remote(
            gate_all.at[(opposite, beside)[n]],
            weigh.at[pl.ds(0, width), pl.ds(n * units, units)],
            (e, beside),
            pair_send.at[n],
            pair_recv.at[n],
        )

    gate_chip = remote(
        gate_all.at[across],
        out_buf.at[pl.ds(0, width), pl.ds(0, units)],
        (e, across),
        pair_send.at[2],
        pair_recv.at[2],
    )
    pl.semaphore_wait(free_sem.at[0], 1)
    gate_core(0).start()
    gate_core(1).start()
    for m in range(4):
        up_all[m] = mm_tn(rows_in[...], act[:, pl.ds(m * units, units)]).astype(BF16)
        if m == 0:
            gate_core(0).wait_recv()
            gate_all[across] = (
                gate_all[across].astype(F32) + weigh[0:width, 0:units].astype(F32)
            ).astype(BF16)
            pl.semaphore_wait(free_sem.at[1], 1)
            gate_chip.start()
    for m in range(4):
        down_all[m] = mm_tn(hidden[:, pl.ds(m * units, units)], grad_rows[...]).astype(BF16)
    pl.semaphore_signal(free_sem.at[2], inc=1, device_id=(e, beside), device_id_type=MESH)

    def up_land(n):
        return act.at[pl.ds(0, width), pl.ds(n * units, units)]

    def down_land(n):
        return hidden.at[pl.ds(0, units), pl.ds(n * width, width)]

    def pair_core(w, n):
        slot = (opposite, beside)[n]
        return remote(
            (up_all, down_all)[w].at[slot],
            (up_land, down_land)[w](n),
            (e, beside),
            pair_send.at[3 + 2 * w + n],
            pair_recv.at[3 + 2 * w + n],
        )

    pl.semaphore_wait(free_sem.at[2], 1)
    for w in range(2):
        for n in range(2):
            pair_core(w, n).start()
    outs = []

    def add_pairs():
        for n, m in enumerate((across, t)):
            for w, (own, dst) in enumerate(((up_all, grad_up), (down_all, grad_down))):
                pair_core(w, n).wait_recv()
                own[m] = (own[m].astype(F32) + (up_land, down_land)[w](n)[...].astype(F32)).astype(
                    BF16
                )
                out = pltpu.make_async_copy(own.at[m], dst.at[n], copy_sem.at[3 + 2 * n + w])
                out.start()
                outs.append(out)

    def finish_backward(q, at, value):
        inputs = residual_half[piece(q), :]
        scale = lax.rsqrt(jnp.mean(inputs * inputs, axis=-1, keepdims=True) + eps_norm)
        scaled = value * gain_row
        inner = jnp.mean(scaled * inputs, axis=-1, keepdims=True)
        through = scale * scaled - inputs * (scale * scale * scale * inner)
        off[at, :] = (error[at, :].astype(F32) + through).astype(BF16)
        small[1:2, :] += jnp.sum(value * inputs * scale, axis=0, keepdims=True)

    sum_over_tensor(1, pick, 3, finish_backward, lambda: advance(sides, 1, 2), add_pairs)
    residual_copy = pltpu.make_async_copy(off, grad_residual, copy_sem.at[11])
    residual_copy.start()
    await_sent(3, back_buf, returned)
    advance(sides, 2, None)
    for s in sides:
        s.close(range(3))
    residual_copy.wait()
    for out in outs:
        out.wait()
    gate_core(1).wait_recv()
    gate_chip.wait()
    grad_gate[...] = (
        gate_all[t].astype(F32)
        + weigh[0:width, units : 2 * units].astype(F32)
        + out_buf[0:width, 0:units].astype(F32)
    ).astype(BF16)
    for n in range(2):
        gate_core(n).wait_send()
        for w in range(2):
            pair_core(w, n).wait_send()


def moe(
    groups,
    capacity,
    hidden_in,
    table,
    gain_one,
    w_query,
    w_key,
    w_value,
    w_out,
    teacher,
    seg_row,
    routes,
    slots,
    router,
    gain,
    shared_gate,
    shared_up,
    shared_down,
    gate_in,
    up_in,
    down_in,
):
    length, width = hidden_in.shape
    lanes = teacher.shape[0]
    units = shared_gate.shape[1]
    experts = router.shape[0]
    share = capacity // 4
    pad = -(-share // 16) * 16
    rows = groups * pad
    shape = jax.ShapeDtypeStruct
    vmem = pl.BlockSpec(memory_space=pltpu.VMEM)
    hbm = pl.BlockSpec(memory_space=pl.ANY)
    dma = pltpu.SemaphoreType.DMA
    wide, tall, deep = (4, width, units), (4, units, width), (rows, 4 * units)
    return pl.pallas_call(
        functools.partial(moe_kernel, groups, share, pad),
        out_shape=(
            shape((length, width), BF16),
            shape((lanes, length), BF16),
            shape((8, length), F32),
            shape(teacher.shape, BF16),
            shape((length, width), BF16),
            shape((2 * width, units), BF16),
            shape((units, width), BF16),
            shape((width, units), BF16),
            shape((2, width, units), BF16),
            shape((2, units, width), BF16),
            shape((8, width), F32),
            shape((experts, width), F32),
        ),
        in_specs=[hbm] * 2 + [vmem] + [hbm] * 5 + [vmem] * 5 + [hbm] * 6,
        out_specs=(hbm,) * 2 + (vmem,) * 2 + (hbm,) + (vmem,) * 3 + (hbm,) * 2 + (vmem,) * 2,
        scratch_shapes=[
            *([pltpu.VMEM((lanes, width), BF16)] * 3),
            pltpu.VMEM((lanes, length), BF16),
            pltpu.VMEM((width, units), BF16),
            pltpu.VMEM((width, units), BF16),
            pltpu.VMEM((units, width), BF16),
            pltpu.VMEM((length, width), BF16),
            pltpu.VMEM(wide, BF16),
            pltpu.VMEM(wide, BF16),
            pltpu.VMEM(tall, BF16),
            pltpu.VMEM((rows, length), BF16),
            pltpu.VMEM((rows, length), BF16),
            pltpu.VMEM((rows, width), BF16),
            pltpu.VMEM((rows, width), BF16),
            pltpu.VMEM((rows, width), BF16),
            pltpu.VMEM((rows, width), BF16),
            pltpu.VMEM((rows, width), BF16),
            pltpu.VMEM(deep, BF16),
            pltpu.VMEM(deep, BF16),
            pltpu.VMEM(deep, BF16),
            pltpu.VMEM((length, units), BF16),
            pltpu.VMEM((length, units), BF16),
            pltpu.VMEM((length, units), BF16),
            pltpu.VMEM((length // 2, width), F32),
            pltpu.VMEM((length, width), BF16),
            pltpu.VMEM((length, width), F32),
            pltpu.VMEM((length, width), BF16),
            pltpu.VMEM((2 * width if groups == 8 else 16, units), BF16),
            pltpu.VMEM((units if groups == 8 else 16, width), BF16),
            pltpu.VMEM((length // 2, width), BF16),
            pltpu.VMEM((2, length // 2, width), BF16),
            pltpu.VMEM((length // 2, width), BF16),
            pltpu.VMEM((2, length // 2, width), BF16),
            dma((4, groups)),
            dma((4, groups)),
            dma((2, 3, 4)),
            dma((2, 3, 4)),
            dma((4, 3)),
            dma((4, 3)),
            dma((4, 3)),
            dma((4, 3)),
            dma((3,)),
            dma((3,)),
            dma((4, 3)),
            dma((4, 3)),
            dma((8,)),
            dma((7,)),
            dma((7,)),
            pltpu.SemaphoreType.REGULAR((3,)),
            dma((15,)),
        ],
        compiler_params=pltpu.CompilerParams(
            collective_id=2, has_side_effects=True, vmem_limit_bytes=63 * 2**20
        ),
        name="layer",
    )(
        hidden_in,
        table,
        gain_one,
        w_query,
        w_key,
        w_value,
        w_out,
        teacher,
        seg_row,
        routes,
        slots,
        router,
        gain,
        shared_gate,
        shared_up,
        shared_down,
        gate_in,
        up_in,
        down_in,
    )


def finish_kernel(
    groups,
    residual_in,
    hidden_in,
    gain_one,
    w_query,
    w_key,
    w_value,
    w_out,
    qkv_in,
    summary,
    mixed,
    table_in,
    seg_row,
    small_in,
    router_in,
    wide_in,
    tall_in,
    up_in,
    down_in,
    grad_input,
    grad_up,
    grad_down,
    side_wide,
    side_tall,
    sums_out,
    small,
    grad_residual,
    hidden,
    qkv,
    table,
    normed,
    grad_mixed,
    grad_query,
    grad_keys,
    grad_values,
    turned,
    product,
    scales,
    pair_wide,
    pair_tall,
    chip_wide,
    chip_tall,
    pay,
    pay_core,
    pay_out,
    pay_in,
    sums,
    landed,
    direct_land,
    small_land,
    pair_send,
    pair_recv,
    side_send,
    side_recv,
    sum_send,
    sum_recv,
    direct_send,
    direct_recv,
    small_send,
    small_recv,
    pay_send,
    pay_recv,
    copy_sem,
):
    length, width = hidden.shape
    lanes = w_query.shape[0]
    heads = lanes // HD
    block = length // 4
    bits = 3 if groups == 8 else 0
    e, t = lax.axis_index("expert"), lax.axis_index("tensor")
    beside, across = peer_of(t, 1), peer_of(t, 2)
    opposite = peer_of(across, 1)
    peers = expert_peers(bits)
    gain_one_row = gain_one[...].reshape(1, -1)
    others = [(lax.rem(e + n, groups), t) for n in range(1, groups)] if bits else []
    greet(others + [(e, beside), (e, across)])

    loads = [
        pltpu.make_async_copy(src, dst, copy_sem.at[10 + n])
        for n, (src, dst) in enumerate(
            ((hidden_in, hidden), (residual_in, grad_residual), (qkv_in, qkv), (table_in, table))
        )
    ]
    for load in loads:
        load.start()

    def remote(src, dst, device, send, recv):
        return pltpu.make_async_remote_copy(
            src_ref=src,
            dst_ref=dst,
            send_sem=send,
            recv_sem=recv,
            device_id=device,
            device_id_type=MESH,
        )

    parts = ((up_in, pair_wide, chip_wide, grad_up), (down_in, pair_tall, chip_tall, grad_down))

    def own_copy(w):
        return pltpu.make_async_copy(parts[w][0].at[1], parts[w][1], copy_sem.at[w])

    def chip_copy(w):
        return remote(
            parts[w][0].at[0], parts[w][2], (e, across), pair_send.at[w], pair_recv.at[w]
        )

    for w in range(2):
        chip_copy(w).start()
        own_copy(w).start()

    sides = side_streams(
        groups, side_wide, side_tall, False, None, None, side_send, side_recv
    )
    side_copies = []
    for n, s in enumerate(sides):
        rows = s.stages[1][1]
        src = wide_in if n < 2 else tall_in
        side_copies.append(
            pltpu.make_async_copy(src.at[rows], s.out.at[rows], copy_sem.at[6 + n])
        )
    if not sides:
        side_copies = [
            pltpu.make_async_copy(wide_in, side_wide, copy_sem.at[6]),
            pltpu.make_async_copy(tall_in, side_tall, copy_sem.at[7]),
        ]
    for copy in side_copies:
        copy.start()
    for copy in side_copies:
        copy.wait()
    advance(sides, None, 3)

    streams = []
    if not bits:
        sums = sums_out
    if bits:
        streams = [
            Stream(
                sums,
                sums_out,
                h * 4 * HD,
                4 * HD,
                (0, 1, 2) if h % 2 == 0 else (1, 0, 2),
                landed,
                h * 4 * HD,
                sum_send,
                sum_recv,
                h,
            )
            for h in range(heads - 1)
        ]

    last = (heads - 1) * 4 * HD
    few = 4 * HD // 8

    def part_of(group):
        return pl.ds(pl.multiple_of(last + group * few, 16), few)

    def direct(n, phase, arriving=False):
        group = others[n][0]
        if phase == 0:
            src = sums.at[part_of(group)]
            dst = direct_land.at[group if arriving else e]
        else:
            src = sums_out.at[part_of(e)]
            dst = sums_out.at[part_of(group if arriving else e)]
        return remote(
            src,
            dst,
            others[n],
            direct_send.at[phase, n],
            direct_recv.at[phase, group if arriving else e],
        )

    def direct_begin(phase):
        for n in range(len(others)):
            direct(n, phase).start()

    def direct_end(phase):
        for n in range(len(others)):
            direct(n, phase, True).wait_recv()
        if phase == 0 and bits:
            total = sums[part_of(e), :].astype(F32)
            for group, _ in others:
                total = total + direct_land[group].astype(F32)
            sums_out[part_of(e), :] = total.astype(BF16)

    columns = [pl.ds(n * WIDE, lanes) for n in range(3)]
    seg_col = column_of(seg_row[...])
    seg_line = seg_row[...].astype(F32)
    for load in loads:
        load.wait()
    for i in range(4):
        rows = pl.ds(i * block, block)
        inputs = hidden[rows, :].astype(F32)
        scale = lax.rsqrt(jnp.mean(inputs * inputs, axis=-1, keepdims=True) + eps_norm)
        normed[rows, :] = (inputs * scale * gain_one_row).astype(BF16)
        scales[:, rows] = jnp.broadcast_to(scale, (block, 128)).T[0:8, :]
        grad_mixed[rows, :] = mm_nt(grad_residual[rows, :], w_out[...]).astype(BF16)
    grad_out = mm(mixed[...], grad_residual[...]).astype(BF16)
    for h in range(heads):
        sums[pl.ds(h * 4 * HD + 3 * HD, HD), :] = grad_out[h * HD : (h + 1) * HD, :]
    for ref in (grad_query, grad_keys, grad_values):
        ref[...] = jnp.zeros_like(ref)
    swap = swap_halves(lanes)
    small[...] = jnp.concatenate([small_in[...], router_in[...]], axis=0)
    gain_sum = jnp.zeros((1, width), F32)

    for h in range(heads):
        for i in range(4):
            rows = pl.ds(i * block, block)
            reach = (i + 1) * block
            key_at = lax.broadcasted_iota(jnp.int32, (reach, block), 0)
            query_at = lax.broadcasted_iota(jnp.int32, (reach, block), 1) + i * block
            allowed = (seg_col[0:reach, :] == seg_line[:, i * block : (i + 1) * block]) & (
                key_at <= query_at
            )
            q_head = only(qkv[rows, columns[0]] * (HD ** (-0.5)), h)
            g_head = only(grad_mixed[rows, :], h)
            scores = mm_nt(qkv[0:reach, columns[1]], q_head) - summary[h : h + 1, rows]
            prob = jnp.exp(jnp.where(allowed, scores, -1e30))
            grad_prob = mm_nt(qkv[0:reach, columns[2]], g_head)
            inner = jnp.sum(prob * grad_prob, axis=0, keepdims=True)
            grad_scores = (prob * (grad_prob - inner)).astype(BF16)
            grad_values[0:reach, :] += mm(prob.astype(BF16), g_head)
            grad_keys[0:reach, :] += mm(grad_scores, q_head)
            grad_query[rows, :] += mm_tn(grad_scores, only(qkv[0:reach, columns[1]], h)) * (HD ** (-0.5))
            if h == 1 and i == 1:
                advance(sides, 3, 4)
        for i in range(4):
            rows = pl.ds(i * block, block)
            for n, grad in enumerate((grad_query, grad_keys)):
                value = only(grad[rows, :], h)
                high = value.astype(BF16)
                rest = (value - high.astype(F32)).astype(BF16)
                swapped = mm(high, swap) + mm(rest, swap)
                value = (value * table[rows, columns[0]] - swapped * table[rows, columns[1]]).astype(BF16)
                turned[n, h, rows, :] = value
            turned[2, h, rows, :] = only(grad_values[rows, :], h).astype(BF16)
        for n, w in enumerate((w_query, w_key, w_value)):
            made = mm_tn(turned[n, h], normed[...])[h * HD : (h + 1) * HD, :]
            gain_sum = gain_sum + jnp.sum(
                made * w[h * HD : (h + 1) * HD, :].astype(F32), axis=0, keepdims=True
            )
            sums[pl.ds(h * 4 * HD + n * HD, HD), :] = made.astype(BF16)
        if h == 1:
            advance(streams[0:1], 0, 1)
        if h < heads - 1:
            advance(streams[h : h + 1], None, 0)
        else:
            direct_begin(0)

    small[2:3, :] = gain_sum / gain_one_row
    valid = jnp.where(seg_row[...] != 0, 1.0, 0.0)
    small[3:4, :] = jnp.broadcast_to(jnp.sum(valid, axis=1, keepdims=True), (1, width))

    def small_copy(k):
        device = peers[k] if k < bits else (e, (beside, across)[k - bits])
        return remote(small, small_land.at[k], device, small_send.at[k], small_recv.at[k])

    def small_next(k):
        if bits:
            if k > 0:
                small_copy(k - 1).wait()
                small[...] += small_land[k - 1]
            if k < 5:
                small_copy(k).start()

    advance(streams[0:1], 1, 2)
    advance(streams[1:2], 0, 1)
    small_next(0)
    for i in range(4):
        rows = pl.ds(i * block, block)
        product[rows, :] = (
            grad_query[rows, :] * qkv[rows, columns[0]].astype(F32)
            + grad_keys[rows, :] * qkv[rows, columns[1]].astype(F32)
            + grad_values[rows, :] * qkv[rows, columns[2]].astype(F32)
        ).astype(BF16)
    ones = jnp.ones((16, lanes), BF16)
    dots = mm_nt(ones, product[...]).astype(BF16)
    flipped = [w[...].astype(F32).T.astype(BF16) for w in (w_query, w_key, w_value)]
    for n in range(3):
        total = turned[n, 0]
        for h in range(1, heads):
            total = total + turned[n, h]
        turned[n, 0] = total
    for m in range(4):
        rows = slice(m * lanes, (m + 1) * lanes)
        made = sum(mm_nt(flipped[n][rows, :], turned[n, 0]) for n in range(3))
        pay[m, 0:lanes, :] = made.astype(BF16)
        pay[m, lanes : lanes + 16, :] = dots

    def pay_copy(k):
        if k < 2:
            return remote(
                pay.at[(opposite, beside)[k]],
                pay_core.at[k],
                (e, beside),
                pay_send.at[k],
                pay_recv.at[k],
            )
        return remote(pay_out, pay_in, (e, across), pay_send.at[k], pay_recv.at[k])

    pay_copy(0).start()
    pay_copy(1).start()
    place_own = own_columns(lanes, width, t)
    gain_col = jnp.sum(jnp.where(place_own != 0, gain_one_row, 0.0), axis=1, keepdims=True)
    pay_copy(0).wait_recv()
    pay_out[...] = (pay[across].astype(F32) + pay_core[0].astype(F32)).astype(BF16)
    pay_copy(2).start()
    advance(streams[0:1], 2, 3)
    advance(streams[1:2], 1, 2)
    small_next(1)
    direct_end(0)
    direct_begin(1)
    advance(streams[0:1], 3, 4)
    small_next(2)
    advance(streams[1:2], 2, 3)
    small_next(3)
    for w in range(2):
        _, pair, chip, result = parts[w]
        own_copy(w).wait()
        chip_copy(w).wait_recv()
        result[...] = (pair[...].astype(F32) + chip[...].astype(F32)).astype(BF16)
    advance(streams[0:1], 4, None)
    advance(streams[1:2], 3, 4)
    small_next(4)
    pay_copy(1).wait_recv()
    pay_copy(2).wait_recv()
    received = pay[t].astype(F32) + pay_core[1].astype(F32) + pay_in[...].astype(F32)
    scale = scales[0:1, :]
    grad_input[...] = (
        mm_nt(place_own, grad_residual[...])
        + scale * (received[0:lanes, :] * gain_col)
        - mm_nt(place_own, hidden[...])
        * (scale * scale * (received[lanes : lanes + 1, :] / width))
    )
    small_next(5)
    advance(sides, 4, None)
    advance(streams[1:2], 4, None)
    direct_end(1)
    for s in sides:
        s.close(range(3, 5))
    for s in streams:
        s.close(range(5))
    for n in range(len(others)):
        direct(n, 0).wait_send()
        direct(n, 1).wait_send()
    for w in range(2):
        chip_copy(w).wait_send()
    for k in range(3):
        pay_copy(k).wait_send()


def finish(groups, *args):
    hidden, w_query, small_in, router_in, wide_in, tall_in = args[1], args[3], *args[12:16]
    length, width = hidden.shape
    lanes = w_query.shape[0]
    units = tall_in.shape[0]
    smalls = 8 + router_in.shape[0]
    shape = jax.ShapeDtypeStruct
    vmem = pl.BlockSpec(memory_space=pltpu.VMEM)
    hbm = pl.BlockSpec(memory_space=pl.ANY)
    dma = pltpu.SemaphoreType.DMA
    return pl.pallas_call(
        functools.partial(finish_kernel, groups),
        out_shape=(
            shape((lanes, length), F32),
            shape((width, units), BF16),
            shape((units, width), BF16),
            shape(wide_in.shape, BF16),
            shape(tall_in.shape, BF16),
            shape((4 * lanes, width), BF16),
            shape((smalls, width), F32),
        ),
        in_specs=[hbm] * 2 + [vmem] * 5 + [hbm] + [vmem] * 2 + [hbm] + [vmem] * 3 + [hbm] * 4,
        out_specs=(vmem,) * 7,
        scratch_shapes=[
            pltpu.VMEM((length, width), BF16),
            pltpu.VMEM((length, width), BF16),
            pltpu.VMEM((length, 3 * WIDE), BF16),
            pltpu.VMEM((length, 2 * WIDE), F32),
            pltpu.VMEM((length, width), BF16),
            pltpu.VMEM((length, lanes), BF16),
            pltpu.VMEM((length, lanes), F32),
            pltpu.VMEM((length, lanes), F32),
            pltpu.VMEM((length, lanes), F32),
            pltpu.VMEM((3, lanes // HD, length, lanes), BF16),
            pltpu.VMEM((length, lanes), BF16),
            pltpu.VMEM((8, length), F32),
            pltpu.VMEM((width, units), BF16),
            pltpu.VMEM((units, width), BF16),
            pltpu.VMEM((width, units), BF16),
            pltpu.VMEM((units, width), BF16),
            pltpu.VMEM((4, lanes + 16, length), BF16),
            pltpu.VMEM((2, lanes + 16, length), BF16),
            pltpu.VMEM((lanes + 16, length), BF16),
            pltpu.VMEM((lanes + 16, length), BF16),
            pltpu.VMEM((4 * lanes, width), BF16),
            pltpu.VMEM((8 * HD, width), BF16),
            pltpu.VMEM((8, HD // 2, width), BF16),
            pltpu.VMEM((5, smalls, width), F32),
            dma((2,)),
            dma((2,)),
            dma((4, 6)),
            dma((4, 6)),
            dma((3, 6)),
            dma((3, 6)),
            dma((2, 8)),
            dma((2, 8)),
            dma((5,)),
            dma((5,)),
            dma((3,)),
            dma((3,)),
            dma((14,)),
        ],
        compiler_params=pltpu.CompilerParams(
            collective_id=3, has_side_effects=True, vmem_limit_bytes=60 * 2**20
        ),
        name="finish",
    )(*args)


def scale_kernel(numbers, small, *refs):
    tokens, width, members = numbers
    ins, outs = refs[:11], refs[11:]
    count = small[3:4, 0:1] * (1.0 / members)
    factor = 2.0 * tokens / count
    for src, dst in zip(ins, outs):
        dst[...] = src[...].astype(F32) * factor
    attn, ffn, router, loss = outs[11:]
    attn[...] = (small[2:3, :] * factor).reshape(width)
    ffn[...] = (small[1:2, :] * (0.5 * factor)).reshape(width)
    router[...] = small[8:, :] * factor
    loss[...] = jnp.sum(small[0:1, :], axis=1, keepdims=True) * 0.5 / (count * width)


def scale_all(tokens, members, small, grad_input, gate, up, down, wide, tall, sums):
    width = sums.shape[1]
    lanes, length = grad_input.shape
    units = gate.shape[1]
    experts = small.shape[0] - 8
    parts = 6
    row = width // parts
    head = lanes // parts
    shape = jax.ShapeDtypeStruct

    def rows_of(n, offset=0):
        return lambda i: (offset + i, 0)

    def own(n):
        return pl.BlockSpec((head, width), lambda i, n=n: ((i // 2) * 8 + 2 * n + i % 2, 0))

    by_rows = pl.BlockSpec((row, units), lambda i: (i, 0))
    by_cols = pl.BlockSpec((units, row), lambda i: (0, i))
    in_specs = [
        pl.BlockSpec(small.shape, lambda i: (0, 0)),
        pl.BlockSpec((head, length), lambda i: (i, 0)),
        by_rows,
        by_rows,
        by_cols,
        pl.BlockSpec((row, units), lambda i: (i, 0)),
        pl.BlockSpec((row, units), lambda i: (parts + i, 0)),
        by_cols,
        own(0),
        own(1),
        own(2),
        own(3),
    ]
    own_out = pl.BlockSpec((head, width), lambda i: (i, 0))

    def whole(rows, cols):
        return pl.BlockSpec((rows, cols), lambda i: (0, 0))

    out_specs = [
        pl.BlockSpec((head, length), lambda i: (i, 0)),
        by_rows,
        by_rows,
        by_cols,
        by_rows,
        by_rows,
        by_cols,
        *([own_out] * 4),
        pl.BlockSpec((width,), lambda i: (0,)),
        pl.BlockSpec((width,), lambda i: (0,)),
        whole(experts, width),
        whole(1, 1),
    ]
    wide_shape, tall_shape = shape((width, units), F32), shape((units, width), F32)
    return pl.pallas_call(
        functools.partial(scale_kernel, (tokens, width, members)),
        grid=(parts,),
        out_shape=[
            shape((lanes, length), F32),
            wide_shape,
            wide_shape,
            tall_shape,
            wide_shape,
            wide_shape,
            tall_shape,
            *([shape((lanes, width), F32)] * 4),
            shape((width,), F32),
            shape((width,), F32),
            shape((experts, width), F32),
            shape((1, 1), F32),
        ],
        in_specs=in_specs,
        out_specs=out_specs,
        name="scale",
    )(small, grad_input, gate, up, down, wide, wide, tall, sums, sums, sums, sums)


def body(
    hidden_in,
    norm_attn,
    w_query,
    w_key,
    w_value,
    w_out,
    norm_ffn,
    w_router,
    shared_gate,
    shared_up,
    shared_down,
    expert_gate,
    expert_up,
    expert_down,
    segment,
    routes,
    slots,
    teacher,
):
    length, width = hidden_in.shape
    groups = lax.axis_size("expert")
    members = lax.axis_size("tensor")
    capacity = 3 * length // groups
    lanes = w_query.shape[1]
    table = jnp.asarray(rope_rows(length, lanes // HD))
    seg_row = segment[None]
    gain_one, gain_two = norm_attn, norm_ffn
    (
        qkv,
        mixed,
        summary,
        activations,
        grad_residual,
        wide,
        tall,
        gate,
        up_parts,
        down_parts,
        small,
        router,
    ) = moe(
        groups,
        capacity,
        hidden_in,
        table,
        gain_one,
        w_query.T,
        w_key.T,
        w_value.T,
        w_out,
        teacher.T,
        seg_row,
        routes.T,
        slots.T,
        w_router.T,
        gain_two,
        shared_gate,
        shared_up,
        shared_down,
        expert_gate[0],
        expert_up[0],
        expert_down[0],
    )
    grad_input, up, down, wide, tall, sums, small = finish(
        groups,
        grad_residual,
        hidden_in,
        gain_one,
        w_query.T,
        w_key.T,
        w_value.T,
        w_out,
        qkv,
        summary,
        mixed,
        table,
        seg_row,
        small,
        router,
        wide,
        tall,
        up_parts,
        down_parts,
    )
    if groups != 8:
        wide, tall, sums = lax.psum((wide, tall, sums), "expert")
        small = lax.psum(small, ("expert", "tensor"))
    (
        grad_input,
        gate,
        up,
        down,
        side_gate,
        side_up,
        side_down,
        grad_query,
        grad_key,
        grad_value,
        grad_out,
        grad_norm_attn,
        grad_norm_ffn,
        grad_router,
        loss,
    ) = scale_all(
        length * groups, members, small, grad_input, gate, up, down, wide, tall, sums
    )
    return (
        loss[0, 0],
        activations.T,
        grad_input.T,
        grad_norm_attn,
        grad_query.T,
        grad_key.T,
        grad_value.T,
        grad_out,
        grad_norm_ffn,
        grad_router.T,
        side_gate,
        side_up,
        side_down,
        gate[None],
        up[None],
        down[None],
    )


def solution(mesh):
    placed = (
        P("expert", None),
        P(),
        P(None, "tensor"),
        P(None, "tensor"),
        P(None, "tensor"),
        P("tensor", None),
        P(),
        P(),
        P(None, "tensor"),
        P(None, "tensor"),
        P("tensor", None),
        P("expert", None, "tensor"),
        P("expert", None, "tensor"),
        P("expert", "tensor", None),
        P("expert"),
        P("expert", None),
        P("expert", None),
        P("expert", "tensor"),
    )
    return jax.shard_map(
        body,
        mesh=mesh,
        in_specs=placed,
        out_specs=(
            P(),
            P("expert", "tensor"),
            P("expert", "tensor"),
            P(),
            P(None, "tensor"),
            P(None, "tensor"),
            P(None, "tensor"),
            P("tensor", None),
            P(),
            P(),
            P(None, "tensor"),
            P(None, "tensor"),
            P("tensor", None),
            P("expert", None, "tensor"),
            P("expert", None, "tensor"),
            P("expert", "tensor", None),
        ),
        check_vma=False,
    )
```
